512 devices in a mesh: seq: 128 (over z, y, core), head: 4 (over x).
Axes of the slice: x: 4, y: 8, z: 8, core: 2. Of those that a mesh axis runs over, the one named last changes fastest.
Arguments:
- queries: bfloat16 [32768, 1024], P('seq', 'head'), may hold values from -6 to 6
- keys: bfloat16 [32768, 1024], P('seq', 'head'), may hold values from -6 to 6
- values: bfloat16 [32768, 1024], P('seq', 'head'), may hold values from -8 to 8
- grad_out: bfloat16 [32768, 1024], P('seq', 'head'), may hold values from -8 to 8
- proj_weight: bfloat16 [1024, 1024], P('head'), may hold values from -0.1875 to 0.1875
Outputs:
- projected: bfloat16 [32768, 1024], P('seq', 'head')
- query_grad: bfloat16 [32768, 1024], P('seq', 'head')
- key_grad: bfloat16 [32768, 1024], P('seq', 'head')
- value_grad: bfloat16 [32768, 1024], P('seq', 'head')
- proj_grad: float32 [1024, 1024], P('head')
The draws below stay inside these ranges and needn't reach their ends.
All inputs are finite; a program needn't handle non-finite values.
Results may differ from the reference program's by a relative error of at most 0.018.
Values may be sent and summed in bfloat16 or wider, within the bound.
A program may use at most 64 MiB of HBM per device.

```python
import math
import jax
import jax.numpy as jnp
from jax import lax

HEADS = 8
HEAD_DIM = 128
BLOCK = 128
LEVELS = 4
MODEL_DIM = 1024
TOKENS = 32768


def waves(key, amplitude, top_rate):
    freq_key, phase_key = jax.random.split(key)
    columns = HEADS * HEAD_DIM
    log_low = jnp.log(1.0 / TOKENS)
    log_high = jnp.log(top_rate)
    frequencies = jnp.exp(jax.random.uniform(freq_key, (columns,), jnp.float32, log_low, log_high))
    phases = jax.random.uniform(phase_key, (columns,), jnp.float32, -jnp.pi, jnp.pi)
    positions = jnp.arange(TOKENS, dtype=jnp.float32)[:, None]
    return amplitude * jnp.sin(2.0 * jnp.pi * jnp.mod(positions * frequencies, 1.0) + phases)


def draw_queries(key, part):
    key = jax.random.fold_in(key, 1)
    rough_key, wave_key = jax.random.split(key, 2)
    grid_shape = (TOKENS, HEADS * HEAD_DIM)
    sampled = 2.0 * jax.random.truncated_normal(rough_key, -4.0, 4.0, grid_shape, jnp.float32) + waves(wave_key, 0.5, 0.5 / BLOCK)
    return jnp.clip(sampled, -6.0, 6.0).astype(jnp.bfloat16)


def draw_keys(key, part):
    key = jax.random.fold_in(key, 2)
    rough_key = jax.random.fold_in(key, 0)
    wave_key = jax.random.fold_in(key, 1)
    run_key = jax.random.fold_in(key, 3)
    grid_shape = (TOKENS, HEADS * HEAD_DIM)
    run_length = 2 ** LEVELS
    run_shape = (TOKENS // run_length, HEADS * HEAD_DIM)
    own_part = 1.4 * jax.random.truncated_normal(rough_key, -4.0, 4.0, grid_shape, jnp.float32)
    run_part = 1.4 * jax.random.truncated_normal(run_key, -4.0, 4.0, run_shape, jnp.float32)
    sampled = own_part + jnp.repeat(run_part, run_length, axis=0) + waves(wave_key, 0.5, 0.5 / BLOCK)
    return jnp.clip(sampled, -6.0, 6.0).astype(jnp.bfloat16)


def draw_values(key, part):
    key = jax.random.fold_in(key, 3)
    rough_key, wave_key = jax.random.split(key, 2)
    grid_shape = (TOKENS, HEADS * HEAD_DIM)
    sampled = jax.random.truncated_normal(rough_key, -4.0, 4.0, grid_shape, jnp.float32) + waves(wave_key, 1.5, 0.5)
    return jnp.clip(sampled, -8.0, 8.0).astype(jnp.bfloat16)


def draw_grad_out(key, part):
    key = jax.random.fold_in(key, 4)
    rough_key, wave_key = jax.random.split(key, 2)
    grid_shape = (TOKENS, HEADS * HEAD_DIM)
    sampled = jax.random.truncated_normal(rough_key, -4.0, 4.0, grid_shape, jnp.float32) + waves(wave_key, 1.5, 0.5 / BLOCK)
    return jnp.clip(sampled, -8.0, 8.0).astype(jnp.bfloat16)


def block_levels(rng, shape, pieces, smallest, largest):
    gain, own = 1.0, jax.random.fold_in(rng, 6)
    for axis_at, parts in pieces:
        heights = jnp.exp(jax.random.uniform(jax.random.fold_in(own, axis_at), (parts,), jnp.float32, smallest / len(pieces), largest / len(pieces)))
        gain = gain * jnp.repeat(heights, shape[axis_at] // parts).reshape([-1 if axis == axis_at else 1 for axis in range(len(shape))])
    return gain


def bell_draw(own_key, extent, deviation, limit, shards=(), kind=jnp.bfloat16):
    loudness = block_levels(own_key, extent, shards, -0.22, 0.18) if shards else 1.0
    values = jax.random.normal(own_key, extent, jnp.float32) * deviation * loudness
    return jnp.minimum(jnp.maximum(values, -limit), limit).astype(kind)


def setup_inputs(seed: int = 0) -> dict:
    seeds = jax.random.split(jax.random.key(seed), 6)
    queries = draw_queries(jax.random.fold_in(seeds[5], 71), 0)
    keys = draw_keys(jax.random.fold_in(seeds[5], 71), 0)
    values = draw_values(jax.random.fold_in(seeds[5], 71), 0)
    grad_out = draw_grad_out(jax.random.fold_in(seeds[5], 71), 0)
    proj_weight = bell_draw(seeds[4], (HEADS * HEAD_DIM, MODEL_DIM), (HEADS * HEAD_DIM) ** -0.5, 0.1875, ((0, 4),))
    return {"queries": queries, "keys": keys, "values": values, "grad_out": grad_out, "proj_weight": proj_weight}


NEG = -1e+30
OFFSETS = (-3, -2, 2, 3)

def halve_rows(rows):
    paired = rows.astype(jnp.float32).reshape(rows.shape[0] // 2, 2, rows.shape[1])
    return (0.5 * (paired[:, 0] + paired[:, 1])).astype(jnp.bfloat16)

def spread(gradient):
    return jnp.repeat(0.5 * gradient, 2, axis=0)

def tile_mask(first_tile, tile_count, tile_total):
    tile_ids = first_tile + jnp.arange(tile_count, dtype=jnp.int32)
    columns = []
    for offset in OFFSETS:
        target = tile_ids + offset
        in_range = (target >= 0) & (target < tile_total)
        if offset == 3:
            in_range = in_range & (tile_ids % 2 == 0)
        if offset == -3:
            in_range = in_range & (tile_ids % 2 == 1)
        columns.append(in_range)
    return jnp.repeat(jnp.stack(columns, axis=1), BLOCK // 2, axis=1)

def attend_groups(query_head, grad_head, groups):
    length = query_head.shape[0]
    score_scale = 1.0 / math.sqrt(HEAD_DIM)
    score_list = []
    for group_count, keyset, key_mask in groups:
        query_view = query_head.reshape(group_count, -1, HEAD_DIM).astype(jnp.float32)
        key_view = keyset[:, :, :HEAD_DIM].astype(jnp.float32)
        raw_scores = jnp.einsum('grd,gkd->grk', query_view, key_view) * score_scale
        raw_scores = jnp.where(key_mask[:, None, :], raw_scores, NEG)
        score_list.append(raw_scores.reshape(length, -1))
    row_peak = score_list[0].max(axis=1)
    for raw_scores in score_list[1:]:
        row_peak = jnp.maximum(row_peak, raw_scores.max(axis=1))
    row_total = jnp.zeros_like(row_peak)
    for raw_scores in score_list:
        row_total = row_total + jnp.exp(raw_scores - row_peak[:, None]).sum(axis=1)
    prob_list = [jnp.exp(raw_scores - row_peak[:, None]) / row_total[:, None] for raw_scores in score_list]
    attended32 = jnp.zeros((length, HEAD_DIM), jnp.float32)
    weight_list = []
    for (group_count, keyset, key_mask), group_prob in zip(groups, prob_list):
        rounded = lax.optimization_barrier(group_prob.astype(jnp.bfloat16))
        weights = rounded.astype(jnp.float32).reshape(group_count, -1, group_prob.shape[1])
        weight_list.append(weights)
        value_view = keyset[:, :, HEAD_DIM:].astype(jnp.float32)
        attended32 = attended32 + jnp.einsum('grk,gkd->grd', weights, value_view).reshape(length, HEAD_DIM)
    grad32 = grad_head.astype(jnp.float32)
    row_delta = lax.optimization_barrier(jnp.sum(grad32 * attended32, axis=1))
    query_acc = jnp.zeros((length, HEAD_DIM), jnp.float32)
    group_grads = []
    for (group_count, keyset, key_mask), group_prob, weights in zip(groups, prob_list, weight_list):
        query_view = query_head.reshape(group_count, -1, HEAD_DIM).astype(jnp.float32)
        key_view = keyset[:, :, :HEAD_DIM].astype(jnp.float32)
        value_view = keyset[:, :, HEAD_DIM:].astype(jnp.float32)
        grad_view = grad32.reshape(group_count, -1, HEAD_DIM)
        prob_grad = jnp.einsum('grd,gkd->grk', grad_view, value_view).reshape(length, -1)
        dscore = (group_prob * (prob_grad - row_delta[:, None]) * score_scale).astype(jnp.bfloat16)
        dscore = lax.optimization_barrier(dscore).astype(jnp.float32).reshape(group_count, -1, group_prob.shape[1])
        query_acc = query_acc + jnp.einsum('grk,gkd->grd', dscore, key_view).reshape(length, HEAD_DIM)
        key_part = jnp.einsum('grk,grd->gkd', dscore, query_view)
        value_part = jnp.einsum('grk,grd->gkd', weights, grad_view)
        group_grads.append(jnp.concatenate([key_part, value_part], axis=2))
    return (attended32, query_acc, group_grads)

def head_pass(operands):
    query_head, joined_head, grad_head = operands
    length = query_head.shape[0]
    block_count = length // BLOCK
    half_block = BLOCK // 2
    degrees = [degree for degree in range(1, LEVELS + 1) if BLOCK * 2 ** (degree - 1) * 4 <= length]
    coarse = [joined_head]
    for degree in degrees:
        coarse.append(halve_rows(coarse[-1]))
    padded = jnp.pad(joined_head, ((BLOCK, BLOCK), (0, 0)))
    blocks = padded.reshape(block_count + 2, BLOCK, -1)
    keyset = jnp.concatenate([blocks[:-2], blocks[1:-1], blocks[2:]], axis=1)
    block_ids = jnp.arange(block_count, dtype=jnp.int32)
    left_ok = jnp.broadcast_to((block_ids >= 1)[:, None], (block_count, BLOCK))
    right_ok = jnp.broadcast_to((block_ids <= block_count - 2)[:, None], (block_count, BLOCK))
    near_mask = jnp.concatenate([left_ok, jnp.ones((block_count, BLOCK), jnp.bool_), right_ok], axis=1)
    groups = [(block_count, keyset, near_mask)]
    for degree in degrees:
        tile_total = length // (BLOCK * 2 ** (degree - 1))
        tile_table = coarse[degree].reshape(tile_total, half_block, -1)
        padded = jnp.pad(tile_table, ((3, 3), (0, 0), (0, 0)))
        keyset = jnp.concatenate([padded[3 + offset:3 + offset + tile_total] for offset in OFFSETS], axis=1)
        groups.append((tile_total, keyset, tile_mask(0, tile_total, tile_total)))
    attended32, query_acc, group_grads = attend_groups(query_head, grad_head, groups)
    near_grad = group_grads[0]
    padded = jnp.zeros((block_count + 2, BLOCK, 2 * HEAD_DIM), jnp.float32)
    padded = padded.at[:-2].add(near_grad[:, :BLOCK])
    padded = padded.at[1:-1].add(near_grad[:, BLOCK:2 * BLOCK])
    padded = padded.at[2:].add(near_grad[:, 2 * BLOCK:])
    level_grads = [padded.reshape(-1, 2 * HEAD_DIM)[BLOCK:BLOCK + length]]
    for degree, cand_grad in zip(degrees, group_grads[1:]):
        tile_total = cand_grad.shape[0]
        padded = jnp.zeros((tile_total + 6, half_block, 2 * HEAD_DIM), jnp.float32)
        for slot_index, offset in enumerate(OFFSETS):
            padded = padded.at[3 + offset:3 + offset + tile_total].add(cand_grad[:, slot_index * half_block:(slot_index + 1) * half_block])
        level_grads.append(padded[3:-3].reshape(-1, 2 * HEAD_DIM))
    for degree in reversed(degrees):
        level_grads[degree - 1] = level_grads[degree - 1] + spread(level_grads[degree])
    return (attended32.astype(jnp.bfloat16), query_acc.astype(jnp.bfloat16), level_grads[0][:, :HEAD_DIM].astype(jnp.bfloat16), level_grads[0][:, HEAD_DIM:].astype(jnp.bfloat16))

def reference(queries, keys, values, grad_out, proj_weight):
    length = queries.shape[0]

    def to_heads(rows):
        return rows.reshape(length, HEADS, HEAD_DIM).transpose(1, 0, 2)

    def from_heads(rows):
        return rows.transpose(1, 0, 2).reshape(length, HEADS * HEAD_DIM)
    attn_grad = jnp.dot(grad_out, proj_weight.T, preferred_element_type=jnp.float32).astype(jnp.bfloat16)
    joined = jnp.concatenate([to_heads(keys), to_heads(values)], axis=2)
    attended, query_grad, key_grad, value_grad = lax.map(head_pass, (to_heads(queries), joined, to_heads(attn_grad)))
    attended = from_heads(attended)
    projected = jnp.dot(attended, proj_weight, preferred_element_type=jnp.float32).astype(jnp.bfloat16)
    proj_grad = jnp.dot(attended.T, grad_out, preferred_element_type=jnp.float32)
    return (projected, from_heads(query_grad), from_heads(key_grad), from_heads(value_grad), proj_grad)
```

```python
import functools
import math

import jax
import jax.numpy as jnp
from jax import lax
from jax.experimental import pallas as pl
from jax.experimental.pallas import tpu as pltpu
from jax.sharding import PartitionSpec as P

HEAD_DIM = 128
BLOCK = 128
HALF = BLOCK // 2
ROWS = 256
FEAT = 256
HEADS_HERE = FEAT // HEAD_DIM
NEAR = 3 * BLOCK
OWN_KEYS = NEAR + 3 * HALF
UPPER = 9 * HALF
NEG = -1e30
SCALE = 1.0 / math.sqrt(HEAD_DIM)
EXP2_SCALE = SCALE * math.log2(math.e)
MESH = pl.DeviceIdType.MESH
F32 = jnp.float32
BF16 = jnp.bfloat16


def dot(a, b):
    return lax.dot_general(a, b, (((1,), (0,)), ((), ())), preferred_element_type=F32)


def dot_nt(a, b):
    return lax.dot_general(a, b, (((1,), (1,)), ((), ())), preferred_element_type=F32)


def dot_tn(a, b):
    return lax.dot_general(a, b, (((0,), (0,)), ((), ())), preferred_element_type=F32)


def pair_average(rows):
    row = lax.broadcasted_iota(jnp.int32, (rows // 2, rows), 0)
    column = lax.broadcasted_iota(jnp.int32, (rows // 2, rows), 1)
    return jnp.where((column >= 2 * row) & (column < 2 * row + 2), 0.5, 0.0).astype(BF16)


def spread_matrix():
    parts = []
    for level in range(1, 5):
        count = ROWS >> level
        token = lax.broadcasted_iota(jnp.int32, (ROWS, count), 0)
        first = lax.broadcasted_iota(jnp.int32, (ROWS, count), 1) * (1 << level)
        inside = (token >= first) & (token < first + (1 << level))
        parts.append(jnp.where(inside, 0.5**level, 0.0).astype(BF16))
    return parts


def kernel(
    devices, heads, zs, ys,
    q_ref, k_ref, v_ref, go_ref, w_ref,
    proj_ref, dq_ref, dk_ref, dv_ref, pg_ref,
    ext, lv1, own, up, gfull, gext, g1, gu, got_near, got1, got2, got3, got4,
    part, got_part, s_own, s_up, e_near, pg32, pg16, got_half, mine, got_z, cross, got_y, final,
    row_send, row_recv, grad_send, grad_recv, x_send, x_recv, red_send, red_recv,
):
    d = lax.axis_index("seq")
    h = lax.axis_index("head")
    core = lax.rem(d, 2)
    y = lax.rem(d // 2, ys)
    z = d // (2 * ys)
    sibling = d + 1 - 2 * core

    def at(target):
        return (lax.rem(target + 2 * devices, devices), h)

    def send(src, dst, send_sem, recv_sem, target):
        copy = pltpu.make_async_remote_copy(
            src_ref=src, dst_ref=dst, send_sem=send_sem, recv_sem=recv_sem,
            device_id=target, device_id_type=MESH,
        )
        copy.start()

    def arrived(ref, sem):
        pltpu.make_async_copy(ref, ref, sem).wait()

    def far(index, total):
        parity = lax.rem(index, 2)
        wide = 3 - 6 * parity
        return [lax.rem(index + o + total, total) for o in (2, -2, wide)]

    two = [(at(t)) for t in far(d, devices)]
    chip = d // 2
    three = [[(2 * t + c, h) for c in range(2)] for t in far(chip, devices // 2)]
    quad = d // 4
    place = lax.rem(d, 4)
    four = [[(4 * t + i, h) for i in range(4)] for t in far(quad, devices // 4)]
    left, right = at(d - 1), at(d + 1)
    across = [(d, lax.rem(h + r, heads)) for r in range(1, heads)]
    z_peers = [(lax.rem(z + r, zs) * (2 * ys) + 2 * y + core, h) for r in range(1, zs)]
    y_peers = [(z * (2 * ys) + 2 * lax.rem(y + r, ys) + core, h) for r in range(1, ys)]

    barrier = pltpu.get_barrier_semaphore()
    everyone = [left, right, *two, *sum(three, []), *sum(four, []), *across, *z_peers, *y_peers]
    everyone.append((sibling, h))
    for target in everyone:
        pl.semaphore_signal(barrier, inc=1, device_id=target, device_id_type=MESH)

    own_rows = slice(BLOCK, BLOCK + ROWS)
    ext[own_rows, :FEAT] = k_ref[...]
    ext[own_rows, FEAT:] = v_ref[...]
    gfull[h] = go_ref[...]
    rows = jnp.concatenate([k_ref[...], v_ref[...]], axis=1)
    offset = 0
    for level in range(1, 5):
        rows = dot(pair_average(rows.shape[0]), rows).astype(BF16)
        own[offset : offset + rows.shape[0]] = rows
        offset += rows.shape[0]
    pl.semaphore_wait(barrier, len(everyone))

    for slot in range(3):
        dst = up.at[pl.ds(pl.multiple_of(6 * HALF + slot * HALF + place * 16, 16), 16)]
        for target in four[slot]:
            send(own.at[224:240], dst, row_send, row_recv.at[4], target)
    for slot in range(3):
        dst = up.at[pl.ds(pl.multiple_of(3 * HALF + slot * HALF + core * 32, 16), 32)]
        for target in three[slot]:
            send(own.at[192:224], dst, row_send, row_recv.at[3], target)
    for r, target in enumerate(across):
        send(go_ref, gfull.at[h], x_send, x_recv.at[0], target)
    for slot in range(3):
        send(own.at[128:192], up.at[slot * HALF : (slot + 1) * HALF], row_send, row_recv.at[2], two[slot])
    send(ext.at[BLOCK : 2 * BLOCK], ext.at[3 * BLOCK :], row_send, row_recv.at[0], left)
    send(ext.at[2 * BLOCK : 3 * BLOCK], ext.at[:BLOCK], row_send, row_recv.at[0], right)
    for tile in range(2):
        tile_rows = own.at[tile * HALF : (tile + 1) * HALF]
        send(tile_rows, lv1.at[2 * tile * HALF : (2 * tile + 1) * HALF], row_send, row_recv.at[1], left)
        send(tile_rows, lv1.at[(2 * tile + 1) * HALF : (2 * tile + 2) * HALF], row_send, row_recv.at[1], right)

    if heads > 1:
        arrived(gfull.at[0 : heads - 1], x_recv.at[0])
    grad_full = jnp.concatenate([gfull[r] for r in range(heads)], axis=1)
    grad = dot_nt(grad_full, w_ref[...]).astype(BF16)
    grad_t = dot_nt(w_ref[...], grad_full).astype(BF16)

    def bias(valid):
        return jnp.where(valid, 0.0, NEG).astype(F32)

    left_bias, right_bias = bias(d >= 1), bias(d <= devices - 2)

    def far_bias(index, total):
        wide = index + 3 - 6 * lax.rem(index, 2)
        return [bias(index >= 2), bias(index + 2 < total), bias((wide >= 0) & (wide < total))]

    up_bias = far_bias(d, devices) + far_bias(chip, devices // 2) + far_bias(quad, devices // 4)

    def head_cols(head):
        return slice(head * HEAD_DIM, (head + 1) * HEAD_DIM)

    def value_cols(head):
        return slice(FEAT + head * HEAD_DIM, FEAT + (head + 1) * HEAD_DIM)

    def block_keys(block, cols):
        near = ext[block * BLOCK : block * BLOCK + NEAR, cols]
        return jnp.concatenate([near, lv1[block * HALF : block * HALF + 3 * HALF, cols]], axis=0)

    def block_queries(block, head):
        return q_ref[block * BLOCK : (block + 1) * BLOCK, head_cols(head)]

    arrived(ext.at[: 2 * BLOCK], row_recv.at[0])
    arrived(lv1, row_recv.at[1])
    own_peak = [[None] * 2 for _ in range(HEADS_HERE)]
    for head in range(HEADS_HERE):
        for block in range(2):
            scores = dot_nt(block_keys(block, head_cols(head)), block_queries(block, head))
            if block == 0:
                pieces = [
                    scores[:BLOCK] + left_bias,
                    scores[BLOCK:NEAR],
                    scores[NEAR : NEAR + HALF] + right_bias,
                    scores[NEAR + HALF : NEAR + 2 * HALF] + left_bias,
                    scores[NEAR + 2 * HALF :] + right_bias,
                ]
            else:
                pieces = [
                    scores[: 2 * BLOCK],
                    scores[2 * BLOCK : NEAR] + right_bias,
                    scores[NEAR : NEAR + HALF] + left_bias,
                    scores[NEAR + HALF : NEAR + 2 * HALF] + right_bias,
                    scores[NEAR + 2 * HALF :] + left_bias,
                ]
            scores = jnp.concatenate(pieces, axis=0)
            s_own[head, block] = scores
            own_peak[head][block] = scores.max(axis=0, keepdims=True)
    arrived(up.at[: 3 * HALF], row_recv.at[2])
    arrived(up.at[3 * HALF : 6 * HALF], row_recv.at[3])
    arrived(up.at[6 * HALF :], row_recv.at[4])
    att_t = []
    inverse = []
    for head in range(HEADS_HERE):
        raw = dot_nt(up[:, head_cols(head)], q_ref[:, head_cols(head)])
        raw = jnp.concatenate(
            [raw[i * HALF : (i + 1) * HALF] + up_bias[i] for i in range(9)], axis=0
        )
        peak = jnp.maximum(jnp.concatenate(own_peak[head], axis=1), raw.max(axis=0, keepdims=True))
        lifted_up = jnp.exp2((raw - peak) * EXP2_SCALE)
        total = lifted_up.sum(axis=0, keepdims=True)
        own_total = []
        for block in range(2):
            block_peak = peak[:, block * BLOCK : (block + 1) * BLOCK]
            lifted = jnp.exp2((s_own[head, block] - block_peak) * EXP2_SCALE)
            s_own[head, block] = lifted
            own_total.append(lifted.sum(axis=0, keepdims=True))
        inv = 1.0 / (total + jnp.concatenate(own_total, axis=1))
        prob_up = lifted_up * inv
        s_up[head] = prob_up
        up_att = dot_tn(up[:, value_cols(head)], prob_up.astype(BF16))
        own_att = []
        for block in range(2):
            prob = s_own[head, block] * inv[:, block * BLOCK : (block + 1) * BLOCK]
            s_own[head, block] = prob
            own_att.append(dot_tn(block_keys(block, value_cols(head)), prob.astype(BF16)))
        att_t.append(up_att + jnp.concatenate(own_att, axis=1))
    att32_t = jnp.concatenate(att_t, axis=0)
    att16_t = att32_t.astype(BF16)

    for side in range(2):
        half = dot(att16_t[side * BLOCK : (side + 1) * BLOCK], grad_full)
        pg32[side] = half
        pg16[side] = half.astype(BF16)
    send(pg16.at[1 - core], got_half, red_send, red_recv.at[0], (sibling, h))

    att16 = att16_t.T
    partial = dot(att16, w_ref[...])
    for r in range(heads):
        part[r] = partial[:, r * FEAT : (r + 1) * FEAT].astype(BF16)
    for r, target in enumerate(across):
        send(part.at[target[1]], got_part.at[r], x_send, x_recv.at[1], target)

    delta = []
    dq_t = []
    for head in range(HEADS_HERE):
        g_t = grad_t[head_cols(head)]
        delta.append((g_t.astype(F32) * att_t[head]).sum(axis=0, keepdims=True))
        prob = s_up[head]
        dprob = dot(up[:, value_cols(head)], g_t)
        dscore = (prob * (dprob - delta[head]) * SCALE).astype(BF16)
        dq_t.append(dot_tn(up[:, head_cols(head)], dscore))
        gu[:, head_cols(head)] = dot(dscore, q_ref[:, head_cols(head)]).astype(BF16)
        gu[:, value_cols(head)] = dot(prob.astype(BF16), grad[:, head_cols(head)]).astype(BF16)
    for slot in range(3):
        for i, target in enumerate(four[(1, 0, 2)[slot]]):
            src = gu.at[6 * HALF + slot * HALF + i * 16 : 6 * HALF + slot * HALF + (i + 1) * 16]
            send(src, got4.at[slot * 4 + place], grad_send, grad_recv.at[4], target)
    for slot in range(3):
        for c, target in enumerate(three[(1, 0, 2)[slot]]):
            src = gu.at[3 * HALF + slot * HALF + c * 32 : 3 * HALF + slot * HALF + (c + 1) * 32]
            send(src, got3.at[slot * 2 + core], grad_send, grad_recv.at[3], target)
    for slot in range(3):
        src = gu.at[slot * HALF : (slot + 1) * HALF]
        send(src, got2.at[slot], grad_send, grad_recv.at[2], two[(1, 0, 2)[slot]])

    arrived(got_half, red_recv.at[0])
    chunk = BLOCK // zs
    for i in range(zs):
        window = slice(i * chunk, (i + 1) * chunk)
        mine[i] = (pg32[core, window] + got_half[window].astype(F32)).astype(BF16)
    for r, target in enumerate(z_peers):
        send(mine.at[lax.rem(z + r + 1, zs)], got_z.at[r], red_send, red_recv.at[1], target)

    for head in range(HEADS_HERE):
        own_dq = []
        for block in range(2):
            cols = slice(block * BLOCK, (block + 1) * BLOCK)
            prob = s_own[head, block]
            dprob = dot(block_keys(block, value_cols(head)), grad_t[head_cols(head), cols])
            dscore = (prob * (dprob - delta[head][:, cols]) * SCALE).astype(BF16)
            own_dq.append(dot_tn(block_keys(block, head_cols(head)), dscore))
            dkey = dot(dscore, block_queries(block, head))
            dval = dot(prob.astype(BF16), grad[cols, head_cols(head)])
            for grads, column in ((dkey, head_cols(head)), (dval, value_cols(head))):
                if block == 0:
                    gext[:BLOCK, column] = grads[:BLOCK].astype(BF16)
                    e_near[:, column] = grads[BLOCK:NEAR]
                    g1[: 3 * HALF, column] = grads[NEAR:]
                else:
                    e_near[:, column] = e_near[:, column] + grads[: 2 * BLOCK]
                    gext[BLOCK : 2 * BLOCK, column] = grads[2 * BLOCK : NEAR].astype(BF16)
                    g1[HALF : 3 * HALF, column] = g1[HALF : 3 * HALF, column] + grads[NEAR : NEAR + 2 * HALF]
                    g1[3 * HALF :, column] = grads[NEAR + 2 * HALF :]
        dq_t[head] = dq_t[head] + jnp.concatenate(own_dq, axis=1)
    for tile in range(2):
        gext[2 * BLOCK + tile * HALF : 2 * BLOCK + (tile + 1) * HALF] = g1[
            (2 * tile + 1) * HALF : (2 * tile + 2) * HALF
        ].astype(BF16)
        gext[3 * BLOCK + tile * HALF : 3 * BLOCK + (tile + 1) * HALF] = g1[
            2 * tile * HALF : (2 * tile + 1) * HALF
        ].astype(BF16)
    send(gext.at[:BLOCK], got_near.at[1], grad_send, grad_recv.at[0], left)
    send(gext.at[BLOCK : 2 * BLOCK], got_near.at[0], grad_send, grad_recv.at[0], right)
    send(gext.at[2 * BLOCK : 3 * BLOCK], got1.at[1], grad_send, grad_recv.at[1], left)
    send(gext.at[3 * BLOCK :], got1.at[0], grad_send, grad_recv.at[1], right)
    dq_ref[...] = jnp.concatenate(dq_t, axis=0).T.astype(BF16)

    arrived(got_z, red_recv.at[1])
    total = mine[z].astype(F32)
    for r in range(zs - 1):
        total = total + got_z[r].astype(F32)
    width = cross.shape[2]
    for i in range(ys):
        cross[i] = total[:, i * width : (i + 1) * width].astype(BF16)
    for r, target in enumerate(y_peers):
        send(cross.at[lax.rem(y + r + 1, ys)], got_y.at[r], red_send, red_recv.at[2], target)

    if heads > 1:
        arrived(got_part, x_recv.at[1])
    projected = part[h].astype(F32)
    for r in range(heads - 1):
        projected = projected + got_part[r].astype(F32)
    proj_ref[...] = projected.astype(BF16)

    arrived(got_y, red_recv.at[2])
    total = cross[y].astype(F32)
    for r in range(ys - 1):
        total = total + got_y[r].astype(F32)
    final[core, z, y] = total.astype(BF16)
    for r, target in enumerate(y_peers):
        send(final.at[core, z, y], final.at[core, z, y], red_send, red_recv.at[3], target)

    arrived(got4, grad_recv.at[4])
    arrived(got3, grad_recv.at[3])
    arrived(got2, grad_recv.at[2])
    arrived(got1, grad_recv.at[1])
    arrived(got_near, grad_recv.at[0])
    levels = spread_matrix()
    rows_grad = e_near[...] + jnp.concatenate([got_near[0], got_near[1]], axis=0).astype(F32)
    for level, got in enumerate((got1, got2, got3, got4)):
        total = got[0].astype(F32)
        for i in range(1, got.shape[0]):
            total = total + got[i].astype(F32)
        rows_grad = rows_grad + dot(levels[level], total.astype(BF16))
    dk_ref[...] = rows_grad[:, :FEAT].astype(BF16)
    dv_ref[...] = rows_grad[:, FEAT:].astype(BF16)

    arrived(got_y, red_recv.at[3])
    for r, target in enumerate(z_peers):
        send(final.at[core, z], final.at[core, z], red_send, red_recv.at[4], target)
    arrived(final.at[0, 0 : zs - 1], red_recv.at[4])
    send(final.at[core], final.at[core], red_send, red_recv.at[5], (sibling, h))
    arrived(final.at[0], red_recv.at[5])
    for c in range(2):
        for zz in range(zs):
            first = c * BLOCK + zz * chunk
            for yy in range(ys):
                pg_ref[first : first + chunk, yy * width : (yy + 1) * width] = final[c, zz, yy].astype(F32)

    arrived(ext.at[: 2 * BLOCK], row_send)
    arrived(lv1, row_send)
    arrived(up, row_send)
    arrived(gext, grad_send)
    arrived(gu, grad_send)
    if heads > 1:
        arrived(gfull.at[0 : heads - 1], x_send)
        arrived(got_part, x_send)
    arrived(got_half, red_send)
    arrived(got_z, red_send)
    arrived(got_y, red_send)
    arrived(got_y, red_send)
    arrived(final.at[0, 0 : zs - 1], red_send)
    arrived(final.at[0], red_send)


def body(zs, ys, queries, keys, values, grad_out, proj_weight):
    devices = lax.axis_size("seq")
    heads = lax.axis_size("head")
    model = proj_weight.shape[1]
    chunk, width = BLOCK // zs, model // ys
    vmem = pl.BlockSpec(memory_space=pltpu.VMEM)
    wide = 2 * FEAT
    scratch = [
        ((4 * BLOCK, wide), BF16),
        ((4 * HALF, wide), BF16),
        ((240, wide), BF16),
        ((UPPER, wide), BF16),
        ((heads, ROWS, FEAT), BF16),
        ((4 * BLOCK, wide), BF16),
        ((4 * HALF, wide), F32),
        ((UPPER, wide), BF16),
        ((2, BLOCK, wide), BF16),
        ((2, BLOCK, wide), BF16),
        ((3, HALF, wide), BF16),
        ((6, HALF // 2, wide), BF16),
        ((12, HALF // 4, wide), BF16),
        ((heads, ROWS, FEAT), BF16),
        ((max(heads - 1, 1), ROWS, FEAT), BF16),
        ((HEADS_HERE, 2, OWN_KEYS, BLOCK), F32),
        ((HEADS_HERE, UPPER, ROWS), F32),
        ((ROWS, wide), F32),
        ((2, BLOCK, model), F32),
        ((2, BLOCK, model), BF16),
        ((BLOCK, model), BF16),
        ((zs, chunk, model), BF16),
        ((zs - 1, chunk, model), BF16),
        ((ys, chunk, width), BF16),
        ((ys - 1, chunk, width), BF16),
        ((2, zs, ys, chunk, width), BF16),
    ]
    like = jax.ShapeDtypeStruct
    return pl.pallas_call(
        functools.partial(kernel, devices, heads, zs, ys),
        out_shape=(
            like((ROWS, FEAT), BF16),
            like((ROWS, FEAT), BF16),
            like((ROWS, FEAT), BF16),
            like((ROWS, FEAT), BF16),
            like((FEAT, model), F32),
        ),
        in_specs=[vmem] * 5,
        out_specs=[vmem] * 5,
        scratch_shapes=[pltpu.VMEM(shape, kind) for shape, kind in scratch]
        + [
            pltpu.SemaphoreType.DMA,
            pltpu.SemaphoreType.DMA((5,)),
            pltpu.SemaphoreType.DMA,
            pltpu.SemaphoreType.DMA((5,)),
            pltpu.SemaphoreType.DMA,
            pltpu.SemaphoreType.DMA((2,)),
            pltpu.SemaphoreType.DMA,
            pltpu.SemaphoreType.DMA((6,)),
        ],
        compiler_params=pltpu.CompilerParams(
            collective_id=0, has_side_effects=True, vmem_limit_bytes=40 * 1024 * 1024
        ),
        name="attention",
    )(queries, keys, values, grad_out, proj_weight)


def solution(mesh):
    devices = mesh.shape["seq"]
    zs = 8 if devices == 128 else 2
    ys = devices // (2 * zs)
    spec = P("seq", "head")
    return jax.shard_map(
        functools.partial(body, zs, ys),
        mesh=mesh,
        in_specs=(spec, spec, spec, spec, P("head", None)),
        out_specs=(spec, spec, spec, spec, P("head", None)),
        check_vma=False,
    )
```

```python
import functools
import math

import jax
import jax.numpy as jnp
from jax import lax
from jax.experimental import pallas as pl
from jax.experimental.pallas import tpu as pltpu
from jax.sharding import PartitionSpec as P

HEAD_DIM = 128
BLOCK = 128
HALF = BLOCK // 2
ROWS = 256
FEAT = 256
HEADS_HERE = FEAT // HEAD_DIM
NEAR = 3 * BLOCK
OWN_KEYS = NEAR + 3 * HALF
UPPER = 9 * HALF
PART = 3 * 32 + 6 * 16
NEG = -1e30
SCALE = 1.0 / math.sqrt(HEAD_DIM)
EXP2_SCALE = SCALE * math.log2(math.e)
MESH = pl.DeviceIdType.MESH
F32 = jnp.float32
BF16 = jnp.bfloat16


def dot(a, b):
    return lax.dot_general(a, b, (((1,), (0,)), ((), ())), preferred_element_type=F32)


def dot_nt(a, b):
    return lax.dot_general(a, b, (((1,), (1,)), ((), ())), preferred_element_type=F32)


def dot_tn(a, b):
    return lax.dot_general(a, b, (((0,), (0,)), ((), ())), preferred_element_type=F32)


def pair_average(rows):
    row = lax.broadcasted_iota(jnp.int32, (rows // 2, rows), 0)
    column = lax.broadcasted_iota(jnp.int32, (rows // 2, rows), 1)
    return jnp.where((column >= 2 * row) & (column < 2 * row + 2), 0.5, 0.0).astype(BF16)


def spread_matrix():
    parts = []
    for level in range(1, 5):
        count = ROWS >> level
        token = lax.broadcasted_iota(jnp.int32, (ROWS, count), 0)
        first = lax.broadcasted_iota(jnp.int32, (ROWS, count), 1) * (1 << level)
        inside = (token >= first) & (token < first + (1 << level))
        parts.append(jnp.where(inside, 0.5**level, 0.0).astype(BF16))
    return parts


def kernel(
    devices, heads, zs, ys,
    q_in, k_in, v_in, go_in, w_in,
    proj_ref, dq_ref, dk_ref, dv_ref, final,
    q_ref, w_ref, ext, lv1, own, up, gfull,
    edge, e_near, g1, near_out, gu, from_sib, gsum, from_mate, got_near, got2, got3, got4,
    part, got_part, s_own, s_up, pg32, pg16, got_half, mine, got_z, cross, got_y,
    in_sem, row_send, row_recv, grad_send, grad_recv, x_send, x_recv, red_send, red_recv, last_recv,
):
    d = lax.axis_index("seq")
    h = lax.axis_index("head")
    core = lax.rem(d, 2)
    y = lax.rem(d // 2, ys)
    z = d // (2 * ys)
    chip = d // 2
    quad = d // 4
    side = lax.rem(chip, 2)

    def at(target):
        return (lax.rem(target + 2 * devices, devices), h)

    def send(src, dst, send_sem, recv_sem, target):
        copy = pltpu.make_async_remote_copy(
            src_ref=src, dst_ref=dst, send_sem=send_sem, recv_sem=recv_sem,
            device_id=target, device_id_type=MESH,
        )
        copy.start()

    def arrived(ref, sem):
        pltpu.make_async_copy(ref, ref, sem).wait()

    def rows_of(ref, first, count):
        return ref.at[pl.ds(pl.multiple_of(first, 16), count)]

    def far(index, total):
        wide = 3 - 6 * lax.rem(index, 2)
        return [lax.rem(index + o + total, total) for o in (2, -2, wide)]

    sibling = (d + 1 - 2 * core, h)
    mate = (4 * quad + 2 * (1 - side) + core, h)
    left, right = at(d - 1), at(d + 1)
    two = [at(d + 2), at(d - 2)]
    three = [(2 * t + core, h) for t in far(chip, devices // 2)]
    four = [(4 * t + 2 * (1 - side) + core, h) for t in far(quad, devices // 4)]
    across = [(d, lax.rem(h + r, heads)) for r in range(1, heads)]

    def z_peer(r):
        return lax.rem(z + r, zs) * (2 * ys) + 2 * y + core

    def y_peer(r):
        return z * (2 * ys) + 2 * lax.rem(y + r, ys) + core

    z_peers = [(z_peer(r), h) for r in range(1, zs)]
    y_peers = [(y_peer(r), h) for r in range(1, ys)]

    barrier = pltpu.get_barrier_semaphore()
    everyone = [left, right, mate, *two, *three, *four, *across, *z_peers, *y_peers]
    for target in everyone:
        pl.semaphore_signal(barrier, inc=1, device_id=target, device_id_type=MESH)

    own_rows = ext.at[BLOCK : BLOCK + ROWS]
    loads = [
        (k_in, own_rows.at[:, :FEAT]), (v_in, own_rows.at[:, FEAT:]),
        (go_in, gfull.at[h]), (q_in, q_ref), (w_in, w_ref),
    ]
    loads = [pltpu.make_async_copy(src, dst, in_sem.at[i]) for i, (src, dst) in enumerate(loads)]
    for load in loads:
        load.start()
    loads[0].wait()
    loads[1].wait()

    rows = ext[BLOCK : BLOCK + ROWS]
    offset = 0
    for level in range(1, 5):
        rows = dot(pair_average(rows.shape[0]), rows).astype(BF16)
        own[offset : offset + rows.shape[0]] = rows
        offset += rows.shape[0]
    for load in loads[2:]:
        load.wait()
    pl.semaphore_wait(barrier, len(everyone))

    mine_part = 3 * HALF + core * PART
    for slot in range(3):
        dst = rows_of(up, mine_part + 96 + side * 48 + slot * 16, 16)
        send(own.at[224:240], dst, row_send, row_recv.at[4], four[slot])
    for slot in range(3):
        dst = rows_of(up, mine_part + slot * 32, 32)
        send(own.at[192:224], dst, row_send, row_recv.at[3], three[slot])
    for slot in range(2):
        send(own.at[128:192], up.at[slot * HALF : (slot + 1) * HALF], row_send, row_recv.at[2], two[slot])
    send(ext.at[BLOCK : 2 * BLOCK], ext.at[3 * BLOCK :], row_send, row_recv.at[0], left)
    send(ext.at[2 * BLOCK : 3 * BLOCK], ext.at[:BLOCK], row_send, row_recv.at[0], right)
    send(own.at[HALF : 2 * HALF], lv1.at[2 * HALF : 3 * HALF], row_send, row_recv.at[1], left)
    send(own.at[:HALF], lv1.at[HALF : 2 * HALF], row_send, row_recv.at[1], right)
    for target in across:
        send(gfull.at[h], gfull.at[h], x_send, x_recv.at[0], target)

    taken = rows_of(up, mine_part + 96 + (1 - side) * 48, 48)
    arrived(taken, row_recv.at[4])
    send(taken, taken, row_send, row_recv.at[5], mate)
    send(taken, taken, row_send, row_recv.at[6], sibling)
    level3 = rows_of(up, mine_part, 96)
    arrived(level3, row_recv.at[3])
    send(level3, level3, row_send, row_recv.at[6], sibling)
    arrived(up.at[: 2 * HALF], row_recv.at[2])
    send(rows_of(up, core * HALF, HALF), up.at[2 * HALF : 3 * HALF], row_send, row_recv.at[6], sibling)
    handed = rows_of(up, mine_part + 96 + side * 48, 48)
    arrived(handed, row_recv.at[5])
    send(handed, handed, row_send, row_recv.at[6], sibling)

    def bias(valid):
        return jnp.where(valid, 0.0, NEG).astype(F32)

    left_bias, right_bias = bias(d >= 1), bias(d <= devices - 2)

    def far_bias(index, total):
        wide = index + 3 - 6 * lax.rem(index, 2)
        return [bias(index >= 2), bias(index + 2 < total), bias((wide >= 0) & (wide < total))]

    bias2, bias3, bias4 = far_bias(d, devices), far_bias(chip, devices // 2), far_bias(quad, devices // 4)
    up_bias = [(HALF, b) for b in bias2]
    for _ in range(2):
        up_bias += [(32, b) for b in bias3] + [(16, b) for b in bias4 + bias4]

    def head_cols(head):
        return slice(head * HEAD_DIM, (head + 1) * HEAD_DIM)

    def value_cols(head):
        return slice(FEAT + head * HEAD_DIM, FEAT + (head + 1) * HEAD_DIM)

    def block_keys(block, cols):
        near = ext[block * BLOCK : block * BLOCK + NEAR, cols]
        return jnp.concatenate([near, lv1[block * HALF : block * HALF + 3 * HALF, cols]], axis=0)

    def block_queries(block, head):
        return q_ref[block * BLOCK : (block + 1) * BLOCK, head_cols(head)]

    arrived(ext.at[: 2 * BLOCK], row_recv.at[0])
    lv1[:HALF] = dot(pair_average(BLOCK), ext[3 * BLOCK :]).astype(BF16)
    lv1[3 * HALF :] = dot(pair_average(BLOCK), ext[:BLOCK]).astype(BF16)
    arrived(lv1.at[: 2 * HALF], row_recv.at[1])
    own_peak = [[None] * 2 for _ in range(HEADS_HERE)]
    for head in range(HEADS_HERE):
        for block in range(2):
            scores = dot_nt(block_keys(block, head_cols(head)), block_queries(block, head))
            if block == 0:
                pieces = [
                    scores[:BLOCK] + left_bias,
                    scores[BLOCK:NEAR],
                    scores[NEAR : NEAR + HALF] + right_bias,
                    scores[NEAR + HALF : NEAR + 2 * HALF] + left_bias,
                    scores[NEAR + 2 * HALF :] + right_bias,
                ]
            else:
                pieces = [
                    scores[: 2 * BLOCK],
                    scores[2 * BLOCK : NEAR] + right_bias,
                    scores[NEAR : NEAR + HALF] + left_bias,
                    scores[NEAR + HALF : NEAR + 2 * HALF] + right_bias,
                    scores[NEAR + 2 * HALF :] + left_bias,
                ]
            scores = jnp.concatenate(pieces, axis=0)
            s_own[head, block] = scores
            own_peak[head][block] = scores.max(axis=0, keepdims=True)

    if heads > 1:
        arrived(gfull.at[0 : heads - 1], x_recv.at[0])
    grad_full = jnp.concatenate([gfull[r] for r in range(heads)], axis=1)
    grad = dot_nt(grad_full, w_ref[...]).astype(BF16)
    grad_t = dot_nt(w_ref[...], grad_full).astype(BF16)

    arrived(up.at[: HALF + PART], row_recv.at[6])
    att_t = []
    for head in range(HEADS_HERE):
        raw = dot_nt(up[:, head_cols(head)], q_ref[:, head_cols(head)])
        pieces, first = [], 0
        for count, piece_bias in up_bias:
            pieces.append(raw[first : first + count] + piece_bias)
            first += count
        raw = jnp.concatenate(pieces, axis=0)
        peak = jnp.maximum(jnp.concatenate(own_peak[head], axis=1), raw.max(axis=0, keepdims=True))
        lifted_up = jnp.exp2((raw - peak) * EXP2_SCALE)
        total = lifted_up.sum(axis=0, keepdims=True)
        own_total = []
        for block in range(2):
            block_peak = peak[:, block * BLOCK : (block + 1) * BLOCK]
            lifted = jnp.exp2((s_own[head, block] - block_peak) * EXP2_SCALE)
            s_own[head, block] = lifted
            own_total.append(lifted.sum(axis=0, keepdims=True))
        inv = 1.0 / (total + jnp.concatenate(own_total, axis=1))
        prob_up = lifted_up * inv
        s_up[head] = prob_up
        up_att = dot_tn(up[:, value_cols(head)], prob_up.astype(BF16))
        own_att = []
        for block in range(2):
            prob = s_own[head, block] * inv[:, block * BLOCK : (block + 1) * BLOCK]
            s_own[head, block] = prob
            own_att.append(dot_tn(block_keys(block, value_cols(head)), prob.astype(BF16)))
        att_t.append(up_att + jnp.concatenate(own_att, axis=1))
    att16_t = jnp.concatenate(att_t, axis=0).astype(BF16)

    for c in range(2):
        half = dot(att16_t[c * BLOCK : (c + 1) * BLOCK], grad_full)
        pg32[c] = half
        pg16[c] = half.astype(BF16)
    send(pg16.at[1 - core], got_half, red_send, red_recv.at[0], sibling)

    delta = []
    dq_t = []
    for head in range(HEADS_HERE):
        g_t = grad_t[head_cols(head)]
        delta.append((g_t.astype(F32) * att_t[head]).sum(axis=0, keepdims=True))
        prob = s_up[head]
        dprob = dot(up[:, value_cols(head)], g_t)
        dscore = (prob * (dprob - delta[head]) * SCALE).astype(BF16)
        dq_t.append(dot_tn(up[:, head_cols(head)], dscore))
        gu[:, head_cols(head)] = dot(dscore, q_ref[:, head_cols(head)]).astype(BF16)
        gu[:, value_cols(head)] = dot(prob.astype(BF16), grad[:, head_cols(head)]).astype(BF16)
    send(rows_of(gu, 3 * HALF + (1 - core) * PART, PART), from_sib.at[HALF:], grad_send, grad_recv.at[5], sibling)
    send(gu.at[2 * HALF : 3 * HALF], from_sib.at[:HALF], grad_send, grad_recv.at[5], sibling)

    arrived(got_half, red_recv.at[0])
    chunk = BLOCK // zs
    for i in range(zs):
        window = slice(i * chunk, (i + 1) * chunk)
        mine[i] = (pg32[core, window] + got_half[window].astype(F32)).astype(BF16)
    for r, target in enumerate(z_peers):
        send(mine.at[lax.rem(z + r + 1, zs)], got_z.at[r], red_send, red_recv.at[1], target)

    arrived(from_sib, grad_recv.at[5])
    gsum[2 * HALF :] = (gu[pl.ds(pl.multiple_of(mine_part, 16), PART)].astype(F32) + from_sib[HALF:].astype(F32)).astype(BF16)
    send(rows_of(gsum, 2 * HALF + 96 + side * 48, 48), from_mate, grad_send, grad_recv.at[6], mate)
    for slot in range(3):
        src = gsum.at[2 * HALF + slot * 32 : 2 * HALF + (slot + 1) * 32]
        send(src, got3.at[slot], grad_send, grad_recv.at[3], three[(1, 0, 2)[slot]])
    gsum[: 2 * HALF] = gu[: 2 * HALF]
    shared = pl.ds(pl.multiple_of(core * HALF, 16), HALF)
    gsum[shared] = (gu[shared].astype(F32) + from_sib[:HALF].astype(F32)).astype(BF16)
    for slot in range(2):
        src = gsum.at[slot * HALF : (slot + 1) * HALF]
        send(src, got2.at[slot], grad_send, grad_recv.at[2], two[1 - slot])

    for head in range(HEADS_HERE):
        own_dq = []
        for block in range(2):
            cols = slice(block * BLOCK, (block + 1) * BLOCK)
            prob = s_own[head, block]
            dprob = dot(block_keys(block, value_cols(head)), grad_t[head_cols(head), cols])
            dscore = (prob * (dprob - delta[head][:, cols]) * SCALE).astype(BF16)
            own_dq.append(dot_tn(block_keys(block, head_cols(head)), dscore))
            dkey = dot(dscore, block_queries(block, head))
            dval = dot(prob.astype(BF16), grad[cols, head_cols(head)])
            for grads, column in ((dkey, head_cols(head)), (dval, value_cols(head))):
                if block == 0:
                    edge[0, :, column] = grads[:BLOCK]
                    e_near[:, column] = grads[BLOCK:NEAR]
                    g1[: 3 * HALF, column] = grads[NEAR:]
                else:
                    e_near[:, column] = e_near[:, column] + grads[: 2 * BLOCK]
                    edge[1, :, column] = grads[2 * BLOCK : NEAR]
                    g1[HALF : 3 * HALF, column] = g1[HALF : 3 * HALF, column] + grads[NEAR : NEAR + 2 * HALF]
                    g1[3 * HALF :, column] = grads[NEAR + 2 * HALF :]
        dq_t[head] = dq_t[head] + jnp.concatenate(own_dq, axis=1)
    levels = spread_matrix()
    pairs = levels[0][:BLOCK, :HALF]
    near_out[0, :BLOCK] = (edge[0] + dot(pairs, g1[3 * HALF :].astype(BF16))).astype(BF16)
    near_out[0, BLOCK:] = g1[HALF : 2 * HALF].astype(BF16)
    near_out[1, :BLOCK] = (edge[1] + dot(pairs, g1[:HALF].astype(BF16))).astype(BF16)
    near_out[1, BLOCK:] = g1[2 * HALF : 3 * HALF].astype(BF16)
    send(near_out.at[0], got_near.at[1], grad_send, grad_recv.at[0], left)
    send(near_out.at[1], got_near.at[0], grad_send, grad_recv.at[0], right)

    arrived(from_mate, grad_recv.at[6])
    kept = pl.ds(pl.multiple_of(2 * HALF + 96 + (1 - side) * 48, 16), 48)
    gsum[kept] = (gsum[kept].astype(F32) + from_mate[...].astype(F32)).astype(BF16)
    for slot in range(3):
        src = rows_of(gsum, 2 * HALF + 96 + (1 - side) * 48 + slot * 16, 16)
        send(src, got4.at[slot], grad_send, grad_recv.at[4], four[(1, 0, 2)[slot]])

    arrived(got_z, red_recv.at[1])
    total = mine[z].astype(F32)
    for r in range(zs - 1):
        total = total + got_z[r].astype(F32)
    width = cross.shape[2]
    for i in range(ys):
        cross[i] = total[:, i * width : (i + 1) * width].astype(BF16)
    for r, target in enumerate(y_peers):
        send(cross.at[lax.rem(y + r + 1, ys)], got_y.at[r], red_send, red_recv.at[2], target)

    partial = dot(att16_t.T, w_ref[...])
    for r in range(heads):
        part[r] = partial[:, r * FEAT : (r + 1) * FEAT].astype(BF16)
    for r, target in enumerate(across):
        send(part.at[target[1]], got_part.at[r], x_send, x_recv.at[1], target)
    dq_ref[...] = jnp.concatenate(dq_t, axis=0).T.astype(BF16)

    arrived(got_y, red_recv.at[2])
    total = cross[y].astype(F32)
    for r in range(ys - 1):
        total = total + got_y[r].astype(F32)
    swap = core == 1
    first, second = jnp.where(swap, z, y), jnp.where(swap, y, z)
    block = final.at[core, second, first]
    final[core, second, first] = total.astype(BF16)
    for r in range(1, ys):
        send(block, block, red_send, red_recv.at[3], (jnp.where(swap, z_peer(r), y_peer(r)), h))
    arrived(got_y, red_recv.at[3])
    line = final.at[core, second]
    for r in range(1, zs):
        send(line, line, red_send, last_recv.at[r - 1], (jnp.where(swap, y_peer(r), z_peer(r)), h))
    send(line, line, red_send, red_recv.at[4], sibling)

    if heads > 1:
        arrived(got_part, x_recv.at[1])
    projected = part[h].astype(F32)
    for r in range(heads - 1):
        projected = projected + got_part[r].astype(F32)
    proj_ref[...] = projected.astype(BF16)

    arrived(got4, grad_recv.at[4])
    arrived(got3, grad_recv.at[3])
    arrived(got2, grad_recv.at[2])
    arrived(got_near, grad_recv.at[0])
    rows_grad = e_near[...] + jnp.concatenate([got_near[0, :BLOCK], got_near[1, :BLOCK]], axis=0).astype(F32)
    rows_grad = rows_grad + dot(levels[0], jnp.concatenate([got_near[1, BLOCK:], got_near[0, BLOCK:]], axis=0))
    for level, got in ((1, got2), (2, got3), (3, got4)):
        total = got[0].astype(F32)
        for i in range(1, got.shape[0]):
            total = total + got[i].astype(F32)
        rows_grad = rows_grad + dot(levels[level], total.astype(BF16))
    dk_ref[...] = rows_grad[:, :FEAT].astype(BF16)
    dv_ref[...] = rows_grad[:, FEAT:].astype(BF16)

    for r in range(1, zs):
        arrived(line, last_recv.at[r - 1])
        piece = final.at[core, lax.rem(second + zs - r, zs)]
        send(piece, piece, red_send, red_recv.at[4], sibling)
    arrived(final.at[0], red_recv.at[4])

    arrived(up.at[: 48 + 96 + 2 * HALF], row_send)
    arrived(up.at[: 2 * BLOCK + 2 * HALF], row_send)
    arrived(up.at[: 48 + HALF + PART], row_send)
    arrived(from_sib, grad_send)
    arrived(up.at[: 48 + 96 + 2 * HALF + 48], grad_send)
    arrived(near_out, grad_send)
    if heads > 1:
        arrived(gfull.at[0 : heads - 1], x_send)
        arrived(got_part, x_send)
    arrived(got_half, red_send)
    arrived(got_z, red_send)
    arrived(got_y, red_send)
    arrived(got_y, red_send)
    arrived(final.at[0, 0 : zs - 1], red_send)
    arrived(final.at[0], red_send)


def finish(proj, dq, dk, dv, final, proj_out, dq_out, dk_out, dv_out, pg_out, pg, sems):
    small = ((proj, proj_out), (dq, dq_out), (dk, dk_out), (dv, dv_out))
    copies = [pltpu.make_async_copy(src, dst, sems.at[i]) for i, (src, dst) in enumerate(small)]
    for copy in copies:
        copy.start()
    _, zs, ys, chunk, width = final.shape
    for c in range(2):
        for zz in range(zs):
            first = c * BLOCK + zz * chunk
            for yy in range(ys):
                piece = final[0, zz, yy] if c == 0 else final[1, yy, zz]
                pg[first : first + chunk, yy * width : (yy + 1) * width] = piece.astype(F32)
        half = slice(c * BLOCK, (c + 1) * BLOCK)
        copies.append(pltpu.make_async_copy(pg.at[half], pg_out.at[half], sems.at[4 + c]))
        copies[-1].start()
    for copy in copies:
        copy.wait()


def body(zs, ys, queries, keys, values, grad_out, proj_weight):
    devices = lax.axis_size("seq")
    heads = lax.axis_size("head")
    model = proj_weight.shape[1]
    chunk, width = BLOCK // zs, model // ys
    vmem = pl.BlockSpec(memory_space=pltpu.VMEM)
    hbm = pl.BlockSpec(memory_space=pltpu.HBM)
    wide = 2 * FEAT
    scratch = [
        ((ROWS, FEAT), BF16),
        ((FEAT, model), BF16),
        ((4 * BLOCK, wide), BF16),
        ((4 * HALF, wide), BF16),
        ((240, wide), BF16),
        ((UPPER, wide), BF16),
        ((heads, ROWS, FEAT), BF16),
        ((2, BLOCK, wide), F32),
        ((ROWS, wide), F32),
        ((4 * HALF, wide), F32),
        ((2, BLOCK + HALF, wide), BF16),
        ((UPPER, wide), BF16),
        ((HALF + PART, wide), BF16),
        ((2 * HALF + PART, wide), BF16),
        ((48, wide), BF16),
        ((2, BLOCK + HALF, wide), BF16),
        ((2, HALF, wide), BF16),
        ((3, HALF // 2, wide), BF16),
        ((3, HALF // 4, wide), BF16),
        ((heads, ROWS, FEAT), BF16),
        ((max(heads - 1, 1), ROWS, FEAT), BF16),
        ((HEADS_HERE, 2, OWN_KEYS, BLOCK), F32),
        ((HEADS_HERE, UPPER, ROWS), F32),
        ((2, BLOCK, model), F32),
        ((2, BLOCK, model), BF16),
        ((BLOCK, model), BF16),
        ((zs, chunk, model), BF16),
        ((zs - 1, chunk, model), BF16),
        ((ys, chunk, width), BF16),
        ((ys - 1, chunk, width), BF16),
    ]
    like = jax.ShapeDtypeStruct
    dma = pltpu.SemaphoreType.DMA
    small = like((ROWS, FEAT), BF16)
    results = pl.pallas_call(
        functools.partial(kernel, devices, heads, zs, ys),
        out_shape=(small, small, small, small, like((2, zs, ys, chunk, width), BF16)),
        in_specs=[hbm] * 5,
        out_specs=[vmem] * 5,
        scratch_shapes=[pltpu.VMEM(shape, kind) for shape, kind in scratch]
        + [dma((5,)), dma, dma((7,)), dma, dma((7,)), dma, dma((2,)), dma, dma((5,)), dma((zs - 1,))],
        compiler_params=pltpu.CompilerParams(
            collective_id=0, has_side_effects=True, vmem_limit_bytes=63 * 1024 * 1024
        ),
        name="attention",
    )(queries, keys, values, grad_out, proj_weight)
    return pl.pallas_call(
        finish,
        out_shape=(small, small, small, small, like((FEAT, model), F32)),
        in_specs=[vmem] * 5,
        out_specs=[hbm] * 5,
        scratch_shapes=[pltpu.VMEM((FEAT, model), F32), dma((6,))],
        name="finish",
    )(*results)


def solution(mesh):
    devices = mesh.shape["seq"]
    zs = math.isqrt(devices // 2)
    ys = devices // (2 * zs)
    spec = P("seq", "head")
    return jax.shard_map(
        functools.partial(body, zs, ys),
        mesh=mesh,
        in_specs=(spec, spec, spec, spec, P("head", None)),
        out_specs=(spec, spec, spec, spec, P("head", None)),
        check_vma=False,
    )
```

```python
import functools
import math

import jax
import jax.numpy as jnp
from jax import lax
from jax.experimental import pallas as pl
from jax.experimental.pallas import tpu as pltpu
from jax.sharding import PartitionSpec as P

HEAD_DIM = 128
BLOCK = 128
HALF = BLOCK // 2
ROWS = 256
FEAT = 256
HEADS_HERE = FEAT // HEAD_DIM
NEAR = 3 * BLOCK
OWN_KEYS = NEAR + 3 * HALF
UPPER = 9 * HALF
PART = 3 * 32 + 6 * 16
NEG = -1e30
SCALE = 1.0 / math.sqrt(HEAD_DIM)
EXP2_SCALE = SCALE * math.log2(math.e)
MESH = pl.DeviceIdType.MESH
F32 = jnp.float32
BF16 = jnp.bfloat16


def dot(a, b):
    return lax.dot_general(a, b, (((1,), (0,)), ((), ())), preferred_element_type=F32)


def dot_nt(a, b):
    return lax.dot_general(a, b, (((1,), (1,)), ((), ())), preferred_element_type=F32)


def dot_tn(a, b):
    return lax.dot_general(a, b, (((0,), (0,)), ((), ())), preferred_element_type=F32)


def pair_average(rows):
    row = lax.broadcasted_iota(jnp.int32, (rows // 2, rows), 0)
    column = lax.broadcasted_iota(jnp.int32, (rows // 2, rows), 1)
    return jnp.where((column >= 2 * row) & (column < 2 * row + 2), 0.5, 0.0).astype(BF16)


def spread_matrix():
    parts = []
    for level in range(1, 5):
        count = ROWS >> level
        token = lax.broadcasted_iota(jnp.int32, (ROWS, count), 0)
        first = lax.broadcasted_iota(jnp.int32, (ROWS, count), 1) * (1 << level)
        inside = (token >= first) & (token < first + (1 << level))
        parts.append(jnp.where(inside, 0.5**level, 0.0).astype(BF16))
    return parts


def kernel(
    devices, heads, zs, ys,
    q_in, k_in, v_in, go_in, w_in,
    proj_ref, dq_ref, dk_ref, dv_ref, pg_ref,
    q_ref, w_ref, ext, lv1, own, up, gfull,
    edge, e_near, g1, near_out, gu, from_sib, gsum, from_mate, got_near, got2, got3, got4,
    part, got_part, s_own, s_up, pg32, pg16, got_half, mine, got_major, lines, final,
    in_sem, row_send, row_recv, grad_send, grad_recv, x_send, x_recv, red_send, red_recv, last_recv,
):
    d = lax.axis_index("seq")
    h = lax.axis_index("head")
    core = lax.rem(d, 2)
    y = lax.rem(d // 2, ys)
    z = d // (2 * ys)
    chip = d // 2
    quad = d // 4
    side = lax.rem(chip, 2)

    def at(target):
        return (lax.rem(target + 2 * devices, devices), h)

    def send(src, dst, send_sem, recv_sem, target):
        copy = pltpu.make_async_remote_copy(
            src_ref=src, dst_ref=dst, send_sem=send_sem, recv_sem=recv_sem,
            device_id=target, device_id_type=MESH,
        )
        copy.start()

    def arrived(ref, sem):
        pltpu.make_async_copy(ref, ref, sem).wait()

    def rows_of(ref, first, count):
        return ref.at[pl.ds(pl.multiple_of(first, 16), count)]

    def far(index, total):
        wide = 3 - 6 * lax.rem(index, 2)
        return [lax.rem(index + o + total, total) for o in (2, -2, wide)]

    sibling = (d + 1 - 2 * core, h)
    mate = (4 * quad + 2 * (1 - side) + core, h)
    left, right = at(d - 1), at(d + 1)
    two = [at(d + 2), at(d - 2)]
    three = [(2 * t + core, h) for t in far(chip, devices // 2)]
    four = [(4 * t + 2 * (1 - side) + core, h) for t in far(quad, devices // 4)]
    across = [(d, lax.rem(h + r, heads)) for r in range(1, heads)]

    def z_peer(r):
        return lax.rem(z + r, zs) * (2 * ys) + 2 * y + core

    def y_peer(r):
        return z * (2 * ys) + 2 * lax.rem(y + r, ys) + core

    swap = core == 1
    major, minor = jnp.where(swap, y, z), jnp.where(swap, z, y)
    firsts = [(jnp.where(swap, y_peer(r), z_peer(r)), h) for r in range(1, zs)]
    seconds = [(jnp.where(swap, z_peer(r), y_peer(r)), h) for r in range(1, ys)]

    barrier = pltpu.get_barrier_semaphore()
    everyone = [left, right, mate, *two, *three, *four, *across, *firsts, *seconds]
    for target in everyone:
        pl.semaphore_signal(barrier, inc=1, device_id=target, device_id_type=MESH)

    own_rows = ext.at[BLOCK : BLOCK + ROWS]
    loads = [
        (k_in, own_rows.at[:, :FEAT]), (v_in, own_rows.at[:, FEAT:]),
        (go_in, gfull.at[h]), (q_in, q_ref), (w_in, w_ref),
    ]
    loads = [pltpu.make_async_copy(src, dst, in_sem.at[i]) for i, (src, dst) in enumerate(loads)]
    for load in loads:
        load.start()
    loads[0].wait()
    loads[1].wait()

    rows = ext[BLOCK : BLOCK + ROWS]
    offset = 0
    for level in range(1, 5):
        rows = dot(pair_average(rows.shape[0]), rows).astype(BF16)
        own[offset : offset + rows.shape[0]] = rows
        offset += rows.shape[0]
    for load in loads[2:]:
        load.wait()
    pl.semaphore_wait(barrier, len(everyone))

    mine_part = 3 * HALF + core * PART
    for slot in range(3):
        dst = rows_of(up, mine_part + 96 + side * 48 + slot * 16, 16)
        send(own.at[224:240], dst, row_send, row_recv.at[4], four[slot])
    for slot in range(3):
        dst = rows_of(up, mine_part + slot * 32, 32)
        send(own.at[192:224], dst, row_send, row_recv.at[3], three[slot])
    for slot in range(2):
        send(own.at[128:192], up.at[slot * HALF : (slot + 1) * HALF], row_send, row_recv.at[2], two[slot])
    send(ext.at[BLOCK : 2 * BLOCK], ext.at[3 * BLOCK :], row_send, row_recv.at[0], left)
    send(ext.at[2 * BLOCK : 3 * BLOCK], ext.at[:BLOCK], row_send, row_recv.at[0], right)
    send(own.at[HALF : 2 * HALF], lv1.at[2 * HALF : 3 * HALF], row_send, row_recv.at[1], left)
    send(own.at[:HALF], lv1.at[HALF : 2 * HALF], row_send, row_recv.at[1], right)
    for target in across:
        send(gfull.at[h], gfull.at[h], x_send, x_recv.at[0], target)

    taken = rows_of(up, mine_part + 96 + (1 - side) * 48, 48)
    arrived(taken, row_recv.at[4])
    send(taken, taken, row_send, row_recv.at[5], mate)
    send(taken, taken, row_send, row_recv.at[6], sibling)
    level3 = rows_of(up, mine_part, 96)
    arrived(level3, row_recv.at[3])
    send(level3, level3, row_send, row_recv.at[6], sibling)
    arrived(up.at[: 2 * HALF], row_recv.at[2])
    send(rows_of(up, core * HALF, HALF), up.at[2 * HALF : 3 * HALF], row_send, row_recv.at[6], sibling)
    handed = rows_of(up, mine_part + 96 + side * 48, 48)
    arrived(handed, row_recv.at[5])
    send(handed, handed, row_send, row_recv.at[6], sibling)

    def bias(valid):
        return jnp.where(valid, 0.0, NEG).astype(F32)

    left_bias, right_bias = bias(d >= 1), bias(d <= devices - 2)

    def far_bias(index, total):
        wide = index + 3 - 6 * lax.rem(index, 2)
        return [bias(index >= 2), bias(index + 2 < total), bias((wide >= 0) & (wide < total))]

    bias2, bias3, bias4 = far_bias(d, devices), far_bias(chip, devices // 2), far_bias(quad, devices // 4)
    up_bias = [(HALF, b) for b in bias2]
    for _ in range(2):
        up_bias += [(32, b) for b in bias3] + [(16, b) for b in bias4 + bias4]

    def head_cols(head):
        return slice(head * HEAD_DIM, (head + 1) * HEAD_DIM)

    def value_cols(head):
        return slice(FEAT + head * HEAD_DIM, FEAT + (head + 1) * HEAD_DIM)

    def block_keys(block, cols):
        near = ext[block * BLOCK : block * BLOCK + NEAR, cols]
        return jnp.concatenate([near, lv1[block * HALF : block * HALF + 3 * HALF, cols]], axis=0)

    def block_queries(block, head):
        return q_ref[block * BLOCK : (block + 1) * BLOCK, head_cols(head)]

    arrived(ext.at[: 2 * BLOCK], row_recv.at[0])
    lv1[:HALF] = dot(pair_average(BLOCK), ext[3 * BLOCK :]).astype(BF16)
    lv1[3 * HALF :] = dot(pair_average(BLOCK), ext[:BLOCK]).astype(BF16)
    arrived(lv1.at[: 2 * HALF], row_recv.at[1])
    own_peak = [[None] * 2 for _ in range(HEADS_HERE)]
    for head in range(HEADS_HERE):
        for block in range(2):
            scores = dot_nt(block_keys(block, head_cols(head)), block_queries(block, head))
            if block == 0:
                pieces = [
                    scores[:BLOCK] + left_bias,
                    scores[BLOCK:NEAR],
                    scores[NEAR : NEAR + HALF] + right_bias,
                    scores[NEAR + HALF : NEAR + 2 * HALF] + left_bias,
                    scores[NEAR + 2 * HALF :] + right_bias,
                ]
            else:
                pieces = [
                    scores[: 2 * BLOCK],
                    scores[2 * BLOCK : NEAR] + right_bias,
                    scores[NEAR : NEAR + HALF] + left_bias,
                    scores[NEAR + HALF : NEAR + 2 * HALF] + right_bias,
                    scores[NEAR + 2 * HALF :] + left_bias,
                ]
            scores = jnp.concatenate(pieces, axis=0)
            s_own[head, block] = scores
            own_peak[head][block] = scores.max(axis=0, keepdims=True)

    if heads > 1:
        arrived(gfull.at[0 : heads - 1], x_recv.at[0])
    grad_full = jnp.concatenate([gfull[r] for r in range(heads)], axis=1)
    grad = dot_nt(grad_full, w_ref[...]).astype(BF16)
    grad_t = dot_nt(w_ref[...], grad_full).astype(BF16)

    arrived(up.at[: HALF + PART], row_recv.at[6])
    att_t = []
    for head in range(HEADS_HERE):
        raw = dot_nt(up[:, head_cols(head)], q_ref[:, head_cols(head)])
        pieces, first = [], 0
        for count, piece_bias in up_bias:
            pieces.append(raw[first : first + count] + piece_bias)
            first += count
        raw = jnp.concatenate(pieces, axis=0)
        peak = jnp.maximum(jnp.concatenate(own_peak[head], axis=1), raw.max(axis=0, keepdims=True))
        lifted_up = jnp.exp2((raw - peak) * EXP2_SCALE)
        total = lifted_up.sum(axis=0, keepdims=True)
        own_total = []
        for block in range(2):
            block_peak = peak[:, block * BLOCK : (block + 1) * BLOCK]
            lifted = jnp.exp2((s_own[head, block] - block_peak) * EXP2_SCALE)
            s_own[head, block] = lifted
            own_total.append(lifted.sum(axis=0, keepdims=True))
        inv = 1.0 / (total + jnp.concatenate(own_total, axis=1))
        prob_up = lifted_up * inv
        s_up[head] = prob_up
        up_att = dot_tn(up[:, value_cols(head)], prob_up.astype(BF16))
        own_att = []
        for block in range(2):
            prob = s_own[head, block] * inv[:, block * BLOCK : (block + 1) * BLOCK]
            s_own[head, block] = prob
            own_att.append(dot_tn(block_keys(block, value_cols(head)), prob.astype(BF16)))
        att_t.append(up_att + jnp.concatenate(own_att, axis=1))
    att16_t = jnp.concatenate(att_t, axis=0).astype(BF16)

    for c in range(2):
        half = dot(att16_t[c * BLOCK : (c + 1) * BLOCK], grad_full)
        pg32[c] = half
        pg16[c] = half.astype(BF16)
    send(pg16.at[1 - core], got_half, red_send, red_recv.at[0], sibling)

    delta = []
    dq_t = []
    for head in range(HEADS_HERE):
        g_t = grad_t[head_cols(head)]
        delta.append((g_t.astype(F32) * att_t[head]).sum(axis=0, keepdims=True))
        prob = s_up[head]
        dprob = dot(up[:, value_cols(head)], g_t)
        dscore = (prob * (dprob - delta[head]) * SCALE).astype(BF16)
        dq_t.append(dot_tn(up[:, head_cols(head)], dscore))
        gu[:, head_cols(head)] = dot(dscore, q_ref[:, head_cols(head)]).astype(BF16)
        gu[:, value_cols(head)] = dot(prob.astype(BF16), grad[:, head_cols(head)]).astype(BF16)
    send(rows_of(gu, 3 * HALF + (1 - core) * PART, PART), from_sib.at[HALF:], grad_send, grad_recv.at[5], sibling)
    send(gu.at[2 * HALF : 3 * HALF], from_sib.at[:HALF], grad_send, grad_recv.at[5], sibling)

    arrived(got_half, red_recv.at[0])
    chunk = BLOCK // zs
    for i in range(zs):
        window = slice(i * chunk, (i + 1) * chunk)
        mine[i] = (pg32[core, window] + got_half[window].astype(F32)).astype(BF16)
    for r, target in enumerate(firsts):
        send(mine.at[lax.rem(major + r + 1, zs)], got_major.at[r], red_send, red_recv.at[1], target)

    arrived(from_sib, grad_recv.at[5])
    gsum[2 * HALF :] = (gu[pl.ds(pl.multiple_of(mine_part, 16), PART)].astype(F32) + from_sib[HALF:].astype(F32)).astype(BF16)
    send(rows_of(gsum, 2 * HALF + 96 + side * 48, 48), from_mate, grad_send, grad_recv.at[6], mate)
    for slot in range(3):
        src = gsum.at[2 * HALF + slot * 32 : 2 * HALF + (slot + 1) * 32]
        send(src, got3.at[slot], grad_send, grad_recv.at[3], three[(1, 0, 2)[slot]])
    gsum[: 2 * HALF] = gu[: 2 * HALF]
    shared = pl.ds(pl.multiple_of(core * HALF, 16), HALF)
    gsum[shared] = (gu[shared].astype(F32) + from_sib[:HALF].astype(F32)).astype(BF16)
    for slot in range(2):
        src = gsum.at[slot * HALF : (slot + 1) * HALF]
        send(src, got2.at[slot], grad_send, grad_recv.at[2], two[1 - slot])

    for head in range(HEADS_HERE):
        own_dq = []
        for block in range(2):
            cols = slice(block * BLOCK, (block + 1) * BLOCK)
            prob = s_own[head, block]
            dprob = dot(block_keys(block, value_cols(head)), grad_t[head_cols(head), cols])
            dscore = (prob * (dprob - delta[head][:, cols]) * SCALE).astype(BF16)
            own_dq.append(dot_tn(block_keys(block, head_cols(head)), dscore))
            dkey = dot(dscore, block_queries(block, head))
            dval = dot(prob.astype(BF16), grad[cols, head_cols(head)])
            for grads, column in ((dkey, head_cols(head)), (dval, value_cols(head))):
                if block == 0:
                    edge[0, :, column] = grads[:BLOCK]
                    e_near[:, column] = grads[BLOCK:NEAR]
                    g1[: 3 * HALF, column] = grads[NEAR:]
                else:
                    e_near[:, column] = e_near[:, column] + grads[: 2 * BLOCK]
                    edge[1, :, column] = grads[2 * BLOCK : NEAR]
                    g1[HALF : 3 * HALF, column] = g1[HALF : 3 * HALF, column] + grads[NEAR : NEAR + 2 * HALF]
                    g1[3 * HALF :, column] = grads[NEAR + 2 * HALF :]
        dq_t[head] = dq_t[head] + jnp.concatenate(own_dq, axis=1)
    levels = spread_matrix()
    pairs = levels[0][:BLOCK, :HALF]
    near_out[0, :BLOCK] = (edge[0] + dot(pairs, g1[3 * HALF :].astype(BF16))).astype(BF16)
    near_out[0, BLOCK:] = g1[HALF : 2 * HALF].astype(BF16)
    near_out[1, :BLOCK] = (edge[1] + dot(pairs, g1[:HALF].astype(BF16))).astype(BF16)
    near_out[1, BLOCK:] = g1[2 * HALF : 3 * HALF].astype(BF16)
    send(near_out.at[0], got_near.at[1], grad_send, grad_recv.at[0], left)
    send(near_out.at[1], got_near.at[0], grad_send, grad_recv.at[0], right)
    dq_ref[...] = jnp.concatenate(dq_t, axis=0).T.astype(BF16)

    partial = dot(att16_t.T, w_ref[...])
    for r in range(heads):
        part[r] = partial[:, r * FEAT : (r + 1) * FEAT].astype(BF16)
    for r, target in enumerate(across):
        send(part.at[target[1]], got_part.at[r], x_send, x_recv.at[1], target)

    arrived(got_major, red_recv.at[1])
    total = mine[major].astype(F32)
    for r in range(zs - 1):
        total = total + got_major[r].astype(F32)
    lines[minor] = total.astype(BF16)
    for target in seconds:
        send(lines.at[minor], lines.at[minor], red_send, red_recv.at[2], target)
    arrived(from_mate, grad_recv.at[6])
    kept = pl.ds(pl.multiple_of(2 * HALF + 96 + (1 - side) * 48, 16), 48)
    gsum[kept] = (gsum[kept].astype(F32) + from_mate[...].astype(F32)).astype(BF16)
    for slot in range(3):
        src = rows_of(gsum, 2 * HALF + 96 + (1 - side) * 48 + slot * 16, 16)
        send(src, got4.at[slot], grad_send, grad_recv.at[4], four[(1, 0, 2)[slot]])
    arrived(lines.at[: ys - 1], red_recv.at[2])
    total = lines[0].astype(F32)
    for i in range(1, ys):
        total = total + lines[i].astype(F32)
    line = final.at[core, major]
    final[core, major] = total.astype(BF16)
    for r, target in enumerate(firsts):
        send(line, line, red_send, last_recv.at[r], target)
    send(line, line, red_send, red_recv.at[3], sibling)

    if heads > 1:
        arrived(got_part, x_recv.at[1])
    projected = part[h].astype(F32)
    for r in range(heads - 1):
        projected = projected + got_part[r].astype(F32)
    proj_ref[...] = projected.astype(BF16)

    arrived(got4, grad_recv.at[4])
    arrived(got3, grad_recv.at[3])
    arrived(got2, grad_recv.at[2])
    arrived(got_near, grad_recv.at[0])
    rows_grad = e_near[...] + jnp.concatenate([got_near[0, :BLOCK], got_near[1, :BLOCK]], axis=0).astype(F32)
    rows_grad = rows_grad + dot(levels[0], jnp.concatenate([got_near[1, BLOCK:], got_near[0, BLOCK:]], axis=0))
    for level, got in ((1, got2), (2, got3), (3, got4)):
        total = got[0].astype(F32)
        for i in range(1, got.shape[0]):
            total = total + got[i].astype(F32)
        rows_grad = rows_grad + dot(levels[level], total.astype(BF16))
    dk_ref[...] = rows_grad[:, :FEAT].astype(BF16)
    dv_ref[...] = rows_grad[:, FEAT:].astype(BF16)

    for r in sorted(range(1, zs), key=lambda r: min(r, zs - r)):
        arrived(line, last_recv.at[r - 1])
        piece = final.at[core, lax.rem(major + zs - r, zs)]
        send(piece, piece, red_send, red_recv.at[3], sibling)
    arrived(final.at[0], red_recv.at[3])
    for c in range(2):
        for i in range(zs):
            pg_ref[c * BLOCK + i * chunk : c * BLOCK + (i + 1) * chunk] = final[c, i].astype(F32)

    arrived(up.at[: 48 + 96 + 2 * HALF], row_send)
    arrived(up.at[: 2 * BLOCK + 2 * HALF], row_send)
    arrived(up.at[: 48 + HALF + PART], row_send)
    arrived(from_sib, grad_send)
    arrived(up.at[: 48 + 96 + 2 * HALF + 48], grad_send)
    arrived(near_out, grad_send)
    if heads > 1:
        arrived(gfull.at[0 : heads - 1], x_send)
        arrived(got_part, x_send)
    arrived(got_half, red_send)
    arrived(got_major, red_send)
    arrived(lines.at[: ys - 1], red_send)
    arrived(final.at[0, 0 : zs - 1], red_send)
    arrived(final.at[0], red_send)


def finish(*refs):
    results, outs, sems = refs[:5], refs[5:10], refs[10]
    copies = [pltpu.make_async_copy(src, dst, sems.at[i]) for i, (src, dst) in enumerate(zip(results, outs))]
    for copy in reversed(copies):
        copy.start()
    for copy in copies:
        copy.wait()


def body(zs, ys, queries, keys, values, grad_out, proj_weight):
    devices = lax.axis_size("seq")
    heads = lax.axis_size("head")
    model = proj_weight.shape[1]
    chunk = BLOCK // zs
    vmem = pl.BlockSpec(memory_space=pltpu.VMEM)
    hbm = pl.BlockSpec(memory_space=pltpu.HBM)
    wide = 2 * FEAT
    scratch = [
        ((ROWS, FEAT), BF16),
        ((FEAT, model), BF16),
        ((4 * BLOCK, wide), BF16),
        ((4 * HALF, wide), BF16),
        ((240, wide), BF16),
        ((UPPER, wide), BF16),
        ((heads, ROWS, FEAT), BF16),
        ((2, BLOCK, wide), F32),
        ((ROWS, wide), F32),
        ((4 * HALF, wide), F32),
        ((2, BLOCK + HALF, wide), BF16),
        ((UPPER, wide), BF16),
        ((HALF + PART, wide), BF16),
        ((2 * HALF + PART, wide), BF16),
        ((48, wide), BF16),
        ((2, BLOCK + HALF, wide), BF16),
        ((2, HALF, wide), BF16),
        ((3, HALF // 2, wide), BF16),
        ((3, HALF // 4, wide), BF16),
        ((heads, ROWS, FEAT), BF16),
        ((max(heads - 1, 1), ROWS, FEAT), BF16),
        ((HEADS_HERE, 2, OWN_KEYS, BLOCK), F32),
        ((HEADS_HERE, UPPER, ROWS), F32),
        ((2, BLOCK, model), F32),
        ((2, BLOCK, model), BF16),
        ((BLOCK, model), BF16),
        ((zs, chunk, model), BF16),
        ((zs - 1, chunk, model), BF16),
        ((ys, chunk, model), BF16),
        ((2, zs, chunk, model), BF16),
    ]
    like = jax.ShapeDtypeStruct
    dma = pltpu.SemaphoreType.DMA
    small = like((ROWS, FEAT), BF16)
    results = pl.pallas_call(
        functools.partial(kernel, devices, heads, zs, ys),
        out_shape=(small, small, small, small, like((FEAT, model), F32)),
        in_specs=[hbm] * 5,
        out_specs=[vmem] * 5,
        scratch_shapes=[pltpu.VMEM(shape, kind) for shape, kind in scratch]
        + [dma((5,)), dma, dma((7,)), dma, dma((7,)), dma, dma((2,)), dma, dma((4,)), dma((zs - 1,))],
        compiler_params=pltpu.CompilerParams(
            collective_id=0, has_side_effects=True, vmem_limit_bytes=63 * 1024 * 1024
        ),
        name="attention",
    )(queries, keys, values, grad_out, proj_weight)
    return pl.pallas_call(
        finish,
        out_shape=(small, small, small, small, like((FEAT, model), F32)),
        in_specs=[vmem] * 5,
        out_specs=[hbm] * 5,
        scratch_shapes=[dma((5,))],
        name="finish",
    )(*results)


def solution(mesh):
    devices = mesh.shape["seq"]
    zs = math.isqrt(devices // 2)
    ys = devices // (2 * zs)
    spec = P("seq", "head")
    return jax.shard_map(
        functools.partial(body, zs, ys),
        mesh=mesh,
        in_specs=(spec, spec, spec, spec, P("head", None)),
        out_specs=(spec, spec, spec, spec, P("head", None)),
        check_vma=False,
    )
```

```python
import functools
import math

import jax
import jax.numpy as jnp
from jax import lax
from jax.experimental import pallas as pl
from jax.experimental.pallas import tpu as pltpu
from jax.sharding import PartitionSpec as P

HEAD_DIM = 128
BLOCK = 128
HALF = BLOCK // 2
ROWS = 256
FEAT = 256
HEADS_HERE = FEAT // HEAD_DIM
NEAR = 3 * BLOCK
OWN_KEYS = NEAR + 3 * HALF
UPPER = 9 * HALF
PART = 3 * 32 + 6 * 16
NEG = -1e30
SCALE = 1.0 / math.sqrt(HEAD_DIM)
EXP2_SCALE = SCALE * math.log2(math.e)
MESH = pl.DeviceIdType.MESH
F32 = jnp.float32
BF16 = jnp.bfloat16


def dot(a, b):
    return lax.dot_general(a, b, (((1,), (0,)), ((), ())), preferred_element_type=F32)


def dot_nt(a, b):
    return lax.dot_general(a, b, (((1,), (1,)), ((), ())), preferred_element_type=F32)


def dot_tn(a, b):
    return lax.dot_general(a, b, (((0,), (0,)), ((), ())), preferred_element_type=F32)


def pair_average(rows):
    row = lax.broadcasted_iota(jnp.int32, (rows // 2, rows), 0)
    column = lax.broadcasted_iota(jnp.int32, (rows // 2, rows), 1)
    return jnp.where((column >= 2 * row) & (column < 2 * row + 2), 0.5, 0.0).astype(BF16)


def averages():
    parts = []
    for level in range(1, 5):
        count = ROWS >> level
        token = lax.broadcasted_iota(jnp.int32, (count, ROWS), 1)
        first = lax.broadcasted_iota(jnp.int32, (count, ROWS), 0) * (1 << level)
        inside = (token >= first) & (token < first + (1 << level))
        parts.append(jnp.where(inside, 0.5**level, 0.0).astype(BF16))
    return jnp.concatenate(parts, axis=0)


def spread_matrix():
    parts = []
    for level in range(1, 5):
        count = ROWS >> level
        token = lax.broadcasted_iota(jnp.int32, (ROWS, count), 0)
        first = lax.broadcasted_iota(jnp.int32, (ROWS, count), 1) * (1 << level)
        inside = (token >= first) & (token < first + (1 << level))
        parts.append(jnp.where(inside, 0.5**level, 0.0).astype(BF16))
    return parts


def kernel(
    devices, heads, zs, ys,
    q_in, k_in, v_in, go_in, w_in,
    proj_ref, dq_ref, dk_ref, dv_ref, pg_ref,
    q_ref, w_ref, ext, lv1, own, up, gfull,
    edge, e_near, g1, near_out, gu, from_sib, gsum, from_mate, got_near, got2, got3, got4,
    part, got_part, s_own, s_up, pg32, pg16, got_half, mine, got_major, lines, final,
    in_sem, row_send, row_recv, grad_send, grad_recv, x_send, x_recv, red_send, red_recv, last_recv,
):
    d = lax.axis_index("seq")
    h = lax.axis_index("head")
    core = lax.rem(d, 2)
    y = lax.rem(d // 2, ys)
    z = d // (2 * ys)
    chip = d // 2
    quad = d // 4
    side = lax.rem(chip, 2)

    def at(target):
        return (lax.rem(target + 2 * devices, devices), h)

    def send(src, dst, send_sem, recv_sem, target):
        copy = pltpu.make_async_remote_copy(
            src_ref=src, dst_ref=dst, send_sem=send_sem, recv_sem=recv_sem,
            device_id=target, device_id_type=MESH,
        )
        copy.start()

    def arrived(ref, sem):
        pltpu.make_async_copy(ref, ref, sem).wait()

    def rows_of(ref, first, count):
        return ref.at[pl.ds(pl.multiple_of(first, 16), count)]

    def far(index, total):
        wide = 3 - 6 * lax.rem(index, 2)
        return [lax.rem(index + o + total, total) for o in (2, -2, wide)]

    sibling = (d + 1 - 2 * core, h)
    mate = (4 * quad + 2 * (1 - side) + core, h)
    left, right = at(d - 1), at(d + 1)
    two = [at(d + 2), at(d - 2)]
    three = [(2 * t + core, h) for t in far(chip, devices // 2)]
    four = [(4 * t + 2 * (1 - side) + core, h) for t in far(quad, devices // 4)]
    across = [(d, lax.rem(h + r, heads)) for r in range(1, heads)]

    def z_peer(r):
        return lax.rem(z + r, zs) * (2 * ys) + 2 * y + core

    def y_peer(r):
        return z * (2 * ys) + 2 * lax.rem(y + r, ys) + core

    swap = core == 1
    major, minor = jnp.where(swap, y, z), jnp.where(swap, z, y)
    firsts = [(jnp.where(swap, y_peer(r), z_peer(r)), h) for r in range(1, zs)]
    seconds = [(jnp.where(swap, z_peer(r), y_peer(r)), h) for r in range(1, ys)]

    own_rows = ext.at[BLOCK : BLOCK + ROWS]
    loads = [
        (k_in, own_rows.at[:, :FEAT]), (v_in, own_rows.at[:, FEAT:]),
        (go_in, gfull.at[h]), (q_in, q_ref), (w_in, w_ref),
    ]
    loads = [pltpu.make_async_copy(src, dst, in_sem.at[i]) for i, (src, dst) in enumerate(loads)]
    for load in loads:
        load.start()

    barrier = pltpu.get_barrier_semaphore()
    everyone = [*four, *three, left, right, *two, mate, *across, *firsts, *seconds]
    for target in everyone:
        pl.semaphore_signal(barrier, inc=1, device_id=target, device_id_type=MESH)

    loads[0].wait()
    loads[1].wait()

    own[...] = dot(averages(), ext[BLOCK : BLOCK + ROWS]).astype(BF16)
    for load in loads[2:]:
        load.wait()
    pl.semaphore_wait(barrier, len(everyone))

    mine_part = 3 * HALF + core * PART
    for slot in range(3):
        dst = rows_of(up, mine_part + 96 + side * 48 + slot * 16, 16)
        send(own.at[224:240], dst, row_send, row_recv.at[4], four[slot])
    for slot in range(3):
        dst = rows_of(up, mine_part + slot * 32, 32)
        send(own.at[192:224], dst, row_send, row_recv.at[3], three[slot])
    for slot in range(2):
        send(own.at[128:192], up.at[slot * HALF : (slot + 1) * HALF], row_send, row_recv.at[2], two[slot])
    send(ext.at[BLOCK : 2 * BLOCK], ext.at[3 * BLOCK :], row_send, row_recv.at[0], left)
    send(ext.at[2 * BLOCK : 3 * BLOCK], ext.at[:BLOCK], row_send, row_recv.at[0], right)
    send(own.at[HALF : 2 * HALF], lv1.at[2 * HALF : 3 * HALF], row_send, row_recv.at[1], left)
    send(own.at[:HALF], lv1.at[HALF : 2 * HALF], row_send, row_recv.at[1], right)
    for target in across:
        send(gfull.at[h], gfull.at[h], x_send, x_recv.at[0], target)

    taken = rows_of(up, mine_part + 96 + (1 - side) * 48, 48)
    arrived(taken, row_recv.at[4])
    send(taken, taken, row_send, row_recv.at[5], mate)
    send(taken, taken, row_send, row_recv.at[6], sibling)
    level3 = rows_of(up, mine_part, 96)
    arrived(level3, row_recv.at[3])
    send(level3, level3, row_send, row_recv.at[6], sibling)
    arrived(up.at[: 2 * HALF], row_recv.at[2])
    send(rows_of(up, core * HALF, HALF), up.at[2 * HALF : 3 * HALF], row_send, row_recv.at[6], sibling)
    handed = rows_of(up, mine_part + 96 + side * 48, 48)
    arrived(handed, row_recv.at[5])
    send(handed, handed, row_send, row_recv.at[6], sibling)

    def bias(valid):
        return jnp.where(valid, 0.0, NEG).astype(F32)

    left_bias, right_bias = bias(d >= 1), bias(d <= devices - 2)

    def far_bias(index, total):
        wide = index + 3 - 6 * lax.rem(index, 2)
        return [bias(index >= 2), bias(index + 2 < total), bias((wide >= 0) & (wide < total))]

    bias2, bias3, bias4 = far_bias(d, devices), far_bias(chip, devices // 2), far_bias(quad, devices // 4)
    up_bias = [(HALF, b) for b in bias2]
    for _ in range(2):
        up_bias += [(32, b) for b in bias3] + [(16, b) for b in bias4 + bias4]

    def head_cols(head):
        return slice(head * HEAD_DIM, (head + 1) * HEAD_DIM)

    def value_cols(head):
        return slice(FEAT + head * HEAD_DIM, FEAT + (head + 1) * HEAD_DIM)

    def block_keys(block, cols):
        near = ext[block * BLOCK : block * BLOCK + NEAR, cols]
        return jnp.concatenate([near, lv1[block * HALF : block * HALF + 3 * HALF, cols]], axis=0)

    def block_queries(block, head):
        return q_ref[block * BLOCK : (block + 1) * BLOCK, head_cols(head)]

    arrived(ext.at[: 2 * BLOCK], row_recv.at[0])
    lv1[:HALF] = dot(pair_average(BLOCK), ext[3 * BLOCK :]).astype(BF16)
    lv1[3 * HALF :] = dot(pair_average(BLOCK), ext[:BLOCK]).astype(BF16)
    arrived(lv1.at[: 2 * HALF], row_recv.at[1])
    own_peak = [[None] * 2 for _ in range(HEADS_HERE)]
    for head in range(HEADS_HERE):
        for block in range(2):
            scores = dot_nt(block_keys(block, head_cols(head)), block_queries(block, head))
            if block == 0:
                pieces = [
                    scores[:BLOCK] + left_bias,
                    scores[BLOCK:NEAR],
                    scores[NEAR : NEAR + HALF] + right_bias,
                    scores[NEAR + HALF : NEAR + 2 * HALF] + left_bias,
                    scores[NEAR + 2 * HALF :] + right_bias,
                ]
            else:
                pieces = [
                    scores[: 2 * BLOCK],
                    scores[2 * BLOCK : NEAR] + right_bias,
                    scores[NEAR : NEAR + HALF] + left_bias,
                    scores[NEAR + HALF : NEAR + 2 * HALF] + right_bias,
                    scores[NEAR + 2 * HALF :] + left_bias,
                ]
            scores = jnp.concatenate(pieces, axis=0)
            s_own[head, block] = scores
            own_peak[head][block] = scores.max(axis=0, keepdims=True)

    if heads > 1:
        arrived(gfull.at[0 : heads - 1], x_recv.at[0])
    grad_full = jnp.concatenate([gfull[r] for r in range(heads)], axis=1)
    grad = dot_nt(grad_full, w_ref[...]).astype(BF16)
    grad_t = dot_nt(w_ref[...], grad_full).astype(BF16)

    arrived(up.at[: HALF + PART], row_recv.at[6])
    att_t = []
    for head in range(HEADS_HERE):
        raw = dot_nt(up[:, head_cols(head)], q_ref[:, head_cols(head)])
        pieces, first = [], 0
        for count, piece_bias in up_bias:
            pieces.append(raw[first : first + count] + piece_bias)
            first += count
        raw = jnp.concatenate(pieces, axis=0)
        peak = jnp.maximum(jnp.concatenate(own_peak[head], axis=1), raw.max(axis=0, keepdims=True))
        lifted_up = jnp.exp2((raw - peak) * EXP2_SCALE)
        total = lifted_up.sum(axis=0, keepdims=True)
        own_total = []
        for block in range(2):
            block_peak = peak[:, block * BLOCK : (block + 1) * BLOCK]
            lifted = jnp.exp2((s_own[head, block] - block_peak) * EXP2_SCALE)
            s_own[head, block] = lifted
            own_total.append(lifted.sum(axis=0, keepdims=True))
        inv = 1.0 / (total + jnp.concatenate(own_total, axis=1))
        prob_up = lifted_up * inv
        s_up[head] = prob_up
        up_att = dot_tn(up[:, value_cols(head)], prob_up.astype(BF16))
        own_att = []
        for block in range(2):
            prob = s_own[head, block] * inv[:, block * BLOCK : (block + 1) * BLOCK]
            s_own[head, block] = prob
            own_att.append(dot_tn(block_keys(block, value_cols(head)), prob.astype(BF16)))
        att_t.append(up_att + jnp.concatenate(own_att, axis=1))
    att16_t = jnp.concatenate(att_t, axis=0).astype(BF16)

    for c in range(2):
        half = dot(att16_t[c * BLOCK : (c + 1) * BLOCK], grad_full)
        pg32[c] = half
        pg16[c] = half.astype(BF16)
    send(pg16.at[1 - core], got_half, red_send, red_recv.at[0], sibling)

    delta = []
    dq_t = []
    for head in range(HEADS_HERE):
        g_t = grad_t[head_cols(head)]
        delta.append((g_t.astype(F32) * att_t[head]).sum(axis=0, keepdims=True))
        prob = s_up[head]
        dprob = dot(up[:, value_cols(head)], g_t)
        dscore = (prob * (dprob - delta[head]) * SCALE).astype(BF16)
        dq_t.append(dot_tn(up[:, head_cols(head)], dscore))
        gu[:, head_cols(head)] = dot(dscore, q_ref[:, head_cols(head)]).astype(BF16)
        gu[:, value_cols(head)] = dot(prob.astype(BF16), grad[:, head_cols(head)]).astype(BF16)
    send(rows_of(gu, 3 * HALF + (1 - core) * PART, PART), from_sib.at[HALF:], grad_send, grad_recv.at[5], sibling)
    send(gu.at[2 * HALF : 3 * HALF], from_sib.at[:HALF], grad_send, grad_recv.at[5], sibling)

    arrived(got_half, red_recv.at[0])
    chunk = BLOCK // zs
    for i in range(zs):
        window = slice(i * chunk, (i + 1) * chunk)
        mine[i] = (pg32[core, window] + got_half[window].astype(F32)).astype(BF16)
    for r, target in enumerate(firsts):
        send(mine.at[lax.rem(major + r + 1, zs)], got_major.at[r], red_send, red_recv.at[1], target)

    arrived(from_sib, grad_recv.at[5])
    gsum[2 * HALF :] = (gu[pl.ds(pl.multiple_of(mine_part, 16), PART)].astype(F32) + from_sib[HALF:].astype(F32)).astype(BF16)
    send(rows_of(gsum, 2 * HALF + 96 + side * 48, 48), from_mate, grad_send, grad_recv.at[6], mate)
    for slot in range(3):
        src = gsum.at[2 * HALF + slot * 32 : 2 * HALF + (slot + 1) * 32]
        send(src, got3.at[slot], grad_send, grad_recv.at[3], three[(1, 0, 2)[slot]])
    gsum[: 2 * HALF] = gu[: 2 * HALF]
    shared = pl.ds(pl.multiple_of(core * HALF, 16), HALF)
    gsum[shared] = (gu[shared].astype(F32) + from_sib[:HALF].astype(F32)).astype(BF16)
    for slot in range(2):
        src = gsum.at[slot * HALF : (slot + 1) * HALF]
        send(src, got2.at[slot], grad_send, grad_recv.at[2], two[1 - slot])

    for head in range(HEADS_HERE):
        own_dq = []
        for block in range(2):
            cols = slice(block * BLOCK, (block + 1) * BLOCK)
            prob = s_own[head, block]
            dprob = dot(block_keys(block, value_cols(head)), grad_t[head_cols(head), cols])
            dscore = (prob * (dprob - delta[head][:, cols]) * SCALE).astype(BF16)
            own_dq.append(dot_tn(block_keys(block, head_cols(head)), dscore))
            dkey = dot(dscore, block_queries(block, head))
            dval = dot(prob.astype(BF16), grad[cols, head_cols(head)])
            for grads, column in ((dkey, head_cols(head)), (dval, value_cols(head))):
                if block == 0:
                    edge[0, :, column] = grads[:BLOCK]
                    e_near[:, column] = grads[BLOCK:NEAR]
                    g1[: 3 * HALF, column] = grads[NEAR:]
                else:
                    e_near[:, column] = e_near[:, column] + grads[: 2 * BLOCK]
                    edge[1, :, column] = grads[2 * BLOCK : NEAR]
                    g1[HALF : 3 * HALF, column] = g1[HALF : 3 * HALF, column] + grads[NEAR : NEAR + 2 * HALF]
                    g1[3 * HALF :, column] = grads[NEAR + 2 * HALF :]
        dq_t[head] = dq_t[head] + jnp.concatenate(own_dq, axis=1)
    levels = spread_matrix()
    pairs = levels[0][:BLOCK, :HALF]
    near_out[0, :BLOCK] = (edge[0] + dot(pairs, g1[3 * HALF :].astype(BF16))).astype(BF16)
    near_out[0, BLOCK:] = g1[HALF : 2 * HALF].astype(BF16)
    near_out[1, :BLOCK] = (edge[1] + dot(pairs, g1[:HALF].astype(BF16))).astype(BF16)
    near_out[1, BLOCK:] = g1[2 * HALF : 3 * HALF].astype(BF16)
    dq_ref[...] = jnp.concatenate(dq_t, axis=0).T.astype(BF16)

    partial = dot(att16_t.T, w_ref[...])
    for r in range(heads):
        part[r] = partial[:, r * FEAT : (r + 1) * FEAT].astype(BF16)
    for r, target in enumerate(across):
        send(part.at[target[1]], got_part.at[r], x_send, x_recv.at[1], target)

    arrived(got_major, red_recv.at[1])
    total = mine[major].astype(F32)
    for r in range(zs - 1):
        total = total + got_major[r].astype(F32)
    lines[minor] = total.astype(BF16)
    for target in seconds:
        send(lines.at[minor], lines.at[minor], red_send, red_recv.at[2], target)
    send(near_out.at[0], got_near.at[1], grad_send, grad_recv.at[0], left)
    send(near_out.at[1], got_near.at[0], grad_send, grad_recv.at[0], right)
    arrived(from_mate, grad_recv.at[6])
    kept = pl.ds(pl.multiple_of(2 * HALF + 96 + (1 - side) * 48, 16), 48)
    gsum[kept] = (gsum[kept].astype(F32) + from_mate[...].astype(F32)).astype(BF16)
    for slot in range(3):
        src = rows_of(gsum, 2 * HALF + 96 + (1 - side) * 48 + slot * 16, 16)
        send(src, got4.at[slot], grad_send, grad_recv.at[4], four[(1, 0, 2)[slot]])
    arrived(lines.at[: ys - 1], red_recv.at[2])
    total = lines[0].astype(F32)
    for i in range(1, ys):
        total = total + lines[i].astype(F32)
    line = final.at[core, major]
    final[core, major] = total.astype(BF16)
    for r, target in enumerate(firsts):
        send(line, line, red_send, last_recv.at[r], target)
    send(line, line, red_send, red_recv.at[3], sibling)

    if heads > 1:
        arrived(got_part, x_recv.at[1])
    projected = part[h].astype(F32)
    for r in range(heads - 1):
        projected = projected + got_part[r].astype(F32)
    proj_ref[...] = projected.astype(BF16)

    arrived(got4, grad_recv.at[4])
    arrived(got3, grad_recv.at[3])
    arrived(got2, grad_recv.at[2])
    arrived(got_near, grad_recv.at[0])
    rows_grad = e_near[...] + jnp.concatenate([got_near[0, :BLOCK], got_near[1, :BLOCK]], axis=0).astype(F32)
    rows_grad = rows_grad + dot(levels[0], jnp.concatenate([got_near[1, BLOCK:], got_near[0, BLOCK:]], axis=0))
    for level, got in ((1, got2), (2, got3), (3, got4)):
        total = got[0].astype(F32)
        for i in range(1, got.shape[0]):
            total = total + got[i].astype(F32)
        rows_grad = rows_grad + dot(levels[level], total.astype(BF16))
    dk_ref[...] = rows_grad[:, :FEAT].astype(BF16)
    dv_ref[...] = rows_grad[:, FEAT:].astype(BF16)

    for r in sorted(range(1, zs), key=lambda r: min(r, zs - r)):
        arrived(line, last_recv.at[r - 1])
        piece = final.at[core, lax.rem(major + zs - r, zs)]
        send(piece, piece, red_send, red_recv.at[3], sibling)
    arrived(final.at[0], red_recv.at[3])
    for c in range(2):
        for i in range(zs):
            pg_ref[c * BLOCK + i * chunk : c * BLOCK + (i + 1) * chunk] = final[c, i].astype(F32)

    arrived(up.at[: 48 + 96 + 2 * HALF], row_send)
    arrived(up.at[: 2 * BLOCK + 2 * HALF], row_send)
    arrived(up.at[: 48 + HALF + PART], row_send)
    arrived(from_sib, grad_send)
    arrived(up.at[: 48 + 96 + 2 * HALF + 48], grad_send)
    arrived(near_out, grad_send)
    if heads > 1:
        arrived(gfull.at[0 : heads - 1], x_send)
        arrived(got_part, x_send)
    arrived(got_half, red_send)
    arrived(got_major, red_send)
    arrived(lines.at[: ys - 1], red_send)
    arrived(final.at[0, 0 : zs - 1], red_send)
    arrived(final.at[0], red_send)


def finish(*refs):
    results, outs, sems = refs[:5], refs[5:10], refs[10]
    copies = [pltpu.make_async_copy(src, dst, sems.at[i]) for i, (src, dst) in enumerate(zip(results, outs))]
    for copy in reversed(copies):
        copy.start()
    for copy in copies:
        copy.wait()


def body(zs, ys, queries, keys, values, grad_out, proj_weight):
    devices = lax.axis_size("seq")
    heads = lax.axis_size("head")
    model = proj_weight.shape[1]
    chunk = BLOCK // zs
    vmem = pl.BlockSpec(memory_space=pltpu.VMEM)
    hbm = pl.BlockSpec(memory_space=pltpu.HBM)
    wide = 2 * FEAT
    scratch = [
        ((ROWS, FEAT), BF16),
        ((FEAT, model), BF16),
        ((4 * BLOCK, wide), BF16),
        ((4 * HALF, wide), BF16),
        ((240, wide), BF16),
        ((UPPER, wide), BF16),
        ((heads, ROWS, FEAT), BF16),
        ((2, BLOCK, wide), F32),
        ((ROWS, wide), F32),
        ((4 * HALF, wide), F32),
        ((2, BLOCK + HALF, wide), BF16),
        ((UPPER, wide), BF16),
        ((HALF + PART, wide), BF16),
        ((2 * HALF + PART, wide), BF16),
        ((48, wide), BF16),
        ((2, BLOCK + HALF, wide), BF16),
        ((2, HALF, wide), BF16),
        ((3, HALF // 2, wide), BF16),
        ((3, HALF // 4, wide), BF16),
        ((heads, ROWS, FEAT), BF16),
        ((max(heads - 1, 1), ROWS, FEAT), BF16),
        ((HEADS_HERE, 2, OWN_KEYS, BLOCK), F32),
        ((HEADS_HERE, UPPER, ROWS), F32),
        ((2, BLOCK, model), F32),
        ((2, BLOCK, model), BF16),
        ((BLOCK, model), BF16),
        ((zs, chunk, model), BF16),
        ((zs - 1, chunk, model), BF16),
        ((ys, chunk, model), BF16),
        ((2, zs, chunk, model), BF16),
    ]
    like = jax.ShapeDtypeStruct
    dma = pltpu.SemaphoreType.DMA
    small = like((ROWS, FEAT), BF16)
    results = pl.pallas_call(
        functools.partial(kernel, devices, heads, zs, ys),
        out_shape=(small, small, small, small, like((FEAT, model), F32)),
        in_specs=[hbm] * 5,
        out_specs=[vmem] * 5,
        scratch_shapes=[pltpu.VMEM(shape, kind) for shape, kind in scratch]
        + [dma((5,)), dma, dma((7,)), dma, dma((7,)), dma, dma((2,)), dma, dma((4,)), dma((zs - 1,))],
        compiler_params=pltpu.CompilerParams(
            collective_id=0, has_side_effects=True, vmem_limit_bytes=63 * 1024 * 1024
        ),
        name="attention",
    )(queries, keys, values, grad_out, proj_weight)
    return pl.pallas_call(
        finish,
        out_shape=(small, small, small, small, like((FEAT, model), F32)),
        in_specs=[vmem] * 5,
        out_specs=[hbm] * 5,
        scratch_shapes=[dma((5,))],
        name="finish",
    )(*results)


def solution(mesh):
    devices = mesh.shape["seq"]
    zs = math.isqrt(devices // 2)
    ys = devices // (2 * zs)
    spec = P("seq", "head")
    return jax.shard_map(
        functools.partial(body, zs, ys),
        mesh=mesh,
        in_specs=(spec, spec, spec, spec, P("head", None)),
        out_specs=(spec, spec, spec, spec, P("head", None)),
        check_vma=False,
    )
```

```python
import functools
import math

import jax
import jax.numpy as jnp
from jax import lax
from jax.experimental import pallas as pl
from jax.experimental.pallas import tpu as pltpu
from jax.sharding import PartitionSpec as P

HEAD_DIM = 128
BLOCK = 128
HALF = BLOCK // 2
ROWS = 256
FEAT = 256
HEADS_HERE = FEAT // HEAD_DIM
NEAR = 3 * BLOCK
OWN_KEYS = NEAR + 3 * HALF
UPPER = 9 * HALF
PART = 3 * 32 + 6 * 16
NEG = -1e30
SCALE = 1.0 / math.sqrt(HEAD_DIM)
EXP2_SCALE = SCALE * math.log2(math.e)
MESH = pl.DeviceIdType.MESH
F32 = jnp.float32
BF16 = jnp.bfloat16


def dot(a, b):
    return lax.dot_general(a, b, (((1,), (0,)), ((), ())), preferred_element_type=F32)


def dot_nt(a, b):
    return lax.dot_general(a, b, (((1,), (1,)), ((), ())), preferred_element_type=F32)


def dot_tn(a, b):
    return lax.dot_general(a, b, (((0,), (0,)), ((), ())), preferred_element_type=F32)


def pair_average(rows):
    row = lax.broadcasted_iota(jnp.int32, (rows // 2, rows), 0)
    column = lax.broadcasted_iota(jnp.int32, (rows // 2, rows), 1)
    return jnp.where((column >= 2 * row) & (column < 2 * row + 2), 0.5, 0.0).astype(BF16)


def averages():
    parts = []
    for level in range(1, 5):
        count = ROWS >> level
        token = lax.broadcasted_iota(jnp.int32, (count, ROWS), 1)
        first = lax.broadcasted_iota(jnp.int32, (count, ROWS), 0) * (1 << level)
        inside = (token >= first) & (token < first + (1 << level))
        parts.append(jnp.where(inside, 0.5**level, 0.0).astype(BF16))
    return jnp.concatenate(parts, axis=0)


def spread_matrix():
    parts = []
    for level in range(1, 5):
        count = ROWS >> level
        token = lax.broadcasted_iota(jnp.int32, (ROWS, count), 0)
        first = lax.broadcasted_iota(jnp.int32, (ROWS, count), 1) * (1 << level)
        inside = (token >= first) & (token < first + (1 << level))
        parts.append(jnp.where(inside, 0.5**level, 0.0).astype(BF16))
    return parts


def kernel(
    devices, heads, zs, ys,
    q_in, k_in, v_in, go_in, w_in,
    proj_out, dq_out, dk_out, dv_out, pg_out,
    proj_ref, dq_ref, dk_ref, dv_ref, pg_ref, q_ref, w_ref, ext, lv1, own, up, gfull,
    edge, e_near, g1, near_out, gu, from_sib, gsum, from_mate, got_near, got2, got3, got4,
    part, got_part, s_own, s_up, pg32, pg16, got_half, mine, got_major, lines, final,
    in_sem, out_sem, row_send, row_recv, grad_send, grad_recv, x_send, x_recv, red_send, red_recv, last_recv, sib_recv,
):
    d = lax.axis_index("seq")
    h = lax.axis_index("head")
    core = lax.rem(d, 2)
    y = lax.rem(d // 2, ys)
    z = d // (2 * ys)
    chip = d // 2
    quad = d // 4
    side = lax.rem(chip, 2)

    def at(target):
        return (lax.rem(target + 2 * devices, devices), h)

    def send(src, dst, send_sem, recv_sem, target):
        copy = pltpu.make_async_remote_copy(
            src_ref=src, dst_ref=dst, send_sem=send_sem, recv_sem=recv_sem,
            device_id=target, device_id_type=MESH,
        )
        copy.start()

    def arrived(ref, sem):
        pltpu.make_async_copy(ref, ref, sem).wait()

    def write(src, dst):
        pltpu.make_async_copy(src, dst, out_sem).start()

    def rows_of(ref, first, count):
        return ref.at[pl.ds(pl.multiple_of(first, 16), count)]

    def far(index, total):
        wide = 3 - 6 * lax.rem(index, 2)
        return [lax.rem(index + o + total, total) for o in (2, -2, wide)]

    sibling = (d + 1 - 2 * core, h)
    mate = (4 * quad + 2 * (1 - side) + core, h)
    left, right = at(d - 1), at(d + 1)
    two = [at(d + 2), at(d - 2)]
    three = [(2 * t + core, h) for t in far(chip, devices // 2)]
    four = [(4 * t + 2 * (1 - side) + core, h) for t in far(quad, devices // 4)]
    across = [(d, lax.rem(h + r, heads)) for r in range(1, heads)]

    def z_peer(r):
        return lax.rem(z + r, zs) * (2 * ys) + 2 * y + core

    def y_peer(r):
        return z * (2 * ys) + 2 * lax.rem(y + r, ys) + core

    swap = core == 1
    major, minor = jnp.where(swap, y, z), jnp.where(swap, z, y)
    firsts = [(jnp.where(swap, y_peer(r), z_peer(r)), h) for r in range(1, zs)]
    seconds = [(jnp.where(swap, z_peer(r), y_peer(r)), h) for r in range(1, ys)]

    own_rows = ext.at[BLOCK : BLOCK + ROWS]
    loads = [
        (k_in, own_rows.at[:, :FEAT]), (v_in, own_rows.at[:, FEAT:]),
        (go_in, gfull.at[h]), (q_in, q_ref), (w_in, w_ref),
    ]
    loads = [pltpu.make_async_copy(src, dst, in_sem.at[i]) for i, (src, dst) in enumerate(loads)]
    for load in loads:
        load.start()

    barrier = pltpu.get_barrier_semaphore()
    everyone = [*four, *three, left, right, *two, mate, *across, *firsts, *seconds]
    for target in everyone:
        pl.semaphore_signal(barrier, inc=1, device_id=target, device_id_type=MESH)

    loads[0].wait()
    loads[1].wait()

    own[...] = dot(averages(), ext[BLOCK : BLOCK + ROWS]).astype(BF16)
    for load in loads[2:]:
        load.wait()
    pl.semaphore_wait(barrier, len(everyone))

    mine_part = 3 * HALF + core * PART
    for slot in range(3):
        dst = rows_of(up, mine_part + 96 + side * 48 + slot * 16, 16)
        send(own.at[224:240], dst, row_send, row_recv.at[4], four[slot])
    for slot in range(3):
        dst = rows_of(up, mine_part + slot * 32, 32)
        send(own.at[192:224], dst, row_send, row_recv.at[3], three[slot])
    for slot in range(2):
        send(own.at[128:192], up.at[slot * HALF : (slot + 1) * HALF], row_send, row_recv.at[2], two[slot])
    send(ext.at[BLOCK : 2 * BLOCK], ext.at[3 * BLOCK :], row_send, row_recv.at[0], left)
    send(ext.at[2 * BLOCK : 3 * BLOCK], ext.at[:BLOCK], row_send, row_recv.at[0], right)
    send(own.at[HALF : 2 * HALF], lv1.at[2 * HALF : 3 * HALF], row_send, row_recv.at[1], left)
    send(own.at[:HALF], lv1.at[HALF : 2 * HALF], row_send, row_recv.at[1], right)
    for target in across:
        send(gfull.at[h], gfull.at[h], x_send, x_recv.at[0], target)

    taken = rows_of(up, mine_part + 96 + (1 - side) * 48, 48)
    arrived(taken, row_recv.at[4])
    send(taken, taken, row_send, row_recv.at[5], mate)
    send(taken, taken, row_send, row_recv.at[6], sibling)
    level3 = rows_of(up, mine_part, 96)
    arrived(level3, row_recv.at[3])
    send(level3, level3, row_send, row_recv.at[6], sibling)
    arrived(up.at[: 2 * HALF], row_recv.at[2])
    send(rows_of(up, core * HALF, HALF), up.at[2 * HALF : 3 * HALF], row_send, row_recv.at[6], sibling)
    handed = rows_of(up, mine_part + 96 + side * 48, 48)
    arrived(handed, row_recv.at[5])
    send(handed, handed, row_send, row_recv.at[6], sibling)

    def bias(valid):
        return jnp.where(valid, 0.0, NEG).astype(F32)

    left_bias, right_bias = bias(d >= 1), bias(d <= devices - 2)

    def far_bias(index, total):
        wide = index + 3 - 6 * lax.rem(index, 2)
        return [bias(index >= 2), bias(index + 2 < total), bias((wide >= 0) & (wide < total))]

    bias2, bias3, bias4 = far_bias(d, devices), far_bias(chip, devices // 2), far_bias(quad, devices // 4)
    up_bias = [(HALF, b) for b in bias2]
    for _ in range(2):
        up_bias += [(32, b) for b in bias3] + [(16, b) for b in bias4 + bias4]

    def head_cols(head):
        return slice(head * HEAD_DIM, (head + 1) * HEAD_DIM)

    def value_cols(head):
        return slice(FEAT + head * HEAD_DIM, FEAT + (head + 1) * HEAD_DIM)

    def block_keys(block, cols):
        near = ext[block * BLOCK : block * BLOCK + NEAR, cols]
        return jnp.concatenate([near, lv1[block * HALF : block * HALF + 3 * HALF, cols]], axis=0)

    def block_queries(block, head):
        return q_ref[block * BLOCK : (block + 1) * BLOCK, head_cols(head)]

    arrived(ext.at[: 2 * BLOCK], row_recv.at[0])
    lv1[:HALF] = dot(pair_average(BLOCK), ext[3 * BLOCK :]).astype(BF16)
    lv1[3 * HALF :] = dot(pair_average(BLOCK), ext[:BLOCK]).astype(BF16)
    arrived(lv1.at[: 2 * HALF], row_recv.at[1])
    own_peak = [[None] * 2 for _ in range(HEADS_HERE)]
    for head in range(HEADS_HERE):
        for block in range(2):
            scores = dot_nt(block_keys(block, head_cols(head)), block_queries(block, head))
            if block == 0:
                pieces = [
                    scores[:BLOCK] + left_bias,
                    scores[BLOCK:NEAR],
                    scores[NEAR : NEAR + HALF] + right_bias,
                    scores[NEAR + HALF : NEAR + 2 * HALF] + left_bias,
                    scores[NEAR + 2 * HALF :] + right_bias,
                ]
            else:
                pieces = [
                    scores[: 2 * BLOCK],
                    scores[2 * BLOCK : NEAR] + right_bias,
                    scores[NEAR : NEAR + HALF] + left_bias,
                    scores[NEAR + HALF : NEAR + 2 * HALF] + right_bias,
                    scores[NEAR + 2 * HALF :] + left_bias,
                ]
            scores = jnp.concatenate(pieces, axis=0)
            s_own[head, block] = scores
            own_peak[head][block] = scores.max(axis=0, keepdims=True)

    if heads > 1:
        arrived(gfull.at[0 : heads - 1], x_recv.at[0])
    grad_full = jnp.concatenate([gfull[r] for r in range(heads)], axis=1)
    grad = dot_nt(grad_full, w_ref[...]).astype(BF16)
    grad_t = dot_nt(w_ref[...], grad_full).astype(BF16)

    arrived(up.at[: HALF + PART], row_recv.at[6])
    att_t = []
    for head in range(HEADS_HERE):
        raw = dot_nt(up[:, head_cols(head)], q_ref[:, head_cols(head)])
        pieces, first = [], 0
        for count, piece_bias in up_bias:
            pieces.append(raw[first : first + count] + piece_bias)
            first += count
        raw = jnp.concatenate(pieces, axis=0)
        peak = jnp.maximum(jnp.concatenate(own_peak[head], axis=1), raw.max(axis=0, keepdims=True))
        lifted_up = jnp.exp2((raw - peak) * EXP2_SCALE)
        total = lifted_up.sum(axis=0, keepdims=True)
        own_total = []
        for block in range(2):
            block_peak = peak[:, block * BLOCK : (block + 1) * BLOCK]
            lifted = jnp.exp2((s_own[head, block] - block_peak) * EXP2_SCALE)
            s_own[head, block] = lifted
            own_total.append(lifted.sum(axis=0, keepdims=True))
        inv = 1.0 / (total + jnp.concatenate(own_total, axis=1))
        prob_up = lifted_up * inv
        s_up[head] = prob_up
        up_att = dot_tn(up[:, value_cols(head)], prob_up.astype(BF16))
        own_att = []
        for block in range(2):
            prob = s_own[head, block] * inv[:, block * BLOCK : (block + 1) * BLOCK]
            s_own[head, block] = prob
            own_att.append(dot_tn(block_keys(block, value_cols(head)), prob.astype(BF16)))
        att_t.append(up_att + jnp.concatenate(own_att, axis=1))
    att16_t = jnp.concatenate(att_t, axis=0).astype(BF16)

    for c in range(2):
        half = dot(att16_t[c * BLOCK : (c + 1) * BLOCK], grad_full)
        pg32[c] = half
        pg16[c] = half.astype(BF16)
    send(pg16.at[1 - core], got_half, red_send, red_recv.at[0], sibling)

    delta = []
    dq_t = []
    for head in range(HEADS_HERE):
        g_t = grad_t[head_cols(head)]
        delta.append((g_t.astype(F32) * att_t[head]).sum(axis=0, keepdims=True))
        prob = s_up[head]
        dprob = dot(up[:, value_cols(head)], g_t)
        dscore = (prob * (dprob - delta[head]) * SCALE).astype(BF16)
        dq_t.append(dot_tn(up[:, head_cols(head)], dscore))
        gu[:, head_cols(head)] = dot(dscore, q_ref[:, head_cols(head)]).astype(BF16)
        gu[:, value_cols(head)] = dot(prob.astype(BF16), grad[:, head_cols(head)]).astype(BF16)
    send(rows_of(gu, 3 * HALF + (1 - core) * PART, PART), from_sib.at[HALF:], grad_send, grad_recv.at[5], sibling)
    send(gu.at[2 * HALF : 3 * HALF], from_sib.at[:HALF], grad_send, grad_recv.at[5], sibling)

    arrived(got_half, red_recv.at[0])
    chunk = BLOCK // zs
    for i in range(zs):
        window = slice(i * chunk, (i + 1) * chunk)
        mine[i] = (pg32[core, window] + got_half[window].astype(F32)).astype(BF16)
    for r, target in enumerate(firsts):
        send(mine.at[lax.rem(major + r + 1, zs)], got_major.at[r], red_send, red_recv.at[1], target)

    arrived(from_sib, grad_recv.at[5])
    gsum[2 * HALF :] = (gu[pl.ds(pl.multiple_of(mine_part, 16), PART)].astype(F32) + from_sib[HALF:].astype(F32)).astype(BF16)
    send(rows_of(gsum, 2 * HALF + 96 + side * 48, 48), from_mate, grad_send, grad_recv.at[6], mate)
    for slot in range(3):
        src = gsum.at[2 * HALF + slot * 32 : 2 * HALF + (slot + 1) * 32]
        send(src, got3.at[slot], grad_send, grad_recv.at[3], three[(1, 0, 2)[slot]])
    gsum[: 2 * HALF] = gu[: 2 * HALF]
    shared = pl.ds(pl.multiple_of(core * HALF, 16), HALF)
    gsum[shared] = (gu[shared].astype(F32) + from_sib[:HALF].astype(F32)).astype(BF16)
    for slot in range(2):
        src = gsum.at[slot * HALF : (slot + 1) * HALF]
        send(src, got2.at[slot], grad_send, grad_recv.at[2], two[1 - slot])

    for head in range(HEADS_HERE):
        own_dq = []
        for block in range(2):
            cols = slice(block * BLOCK, (block + 1) * BLOCK)
            prob = s_own[head, block]
            dprob = dot(block_keys(block, value_cols(head)), grad_t[head_cols(head), cols])
            dscore = (prob * (dprob - delta[head][:, cols]) * SCALE).astype(BF16)
            own_dq.append(dot_tn(block_keys(block, head_cols(head)), dscore))
            dkey = dot(dscore, block_queries(block, head))
            dval = dot(prob.astype(BF16), grad[cols, head_cols(head)])
            for grads, column in ((dkey, head_cols(head)), (dval, value_cols(head))):
                if block == 0:
                    edge[0, :, column] = grads[:BLOCK]
                    e_near[:, column] = grads[BLOCK:NEAR]
                    g1[: 3 * HALF, column] = grads[NEAR:]
                else:
                    e_near[:, column] = e_near[:, column] + grads[: 2 * BLOCK]
                    edge[1, :, column] = grads[2 * BLOCK : NEAR]
                    g1[HALF : 3 * HALF, column] = g1[HALF : 3 * HALF, column] + grads[NEAR : NEAR + 2 * HALF]
                    g1[3 * HALF :, column] = grads[NEAR + 2 * HALF :]
        dq_t[head] = dq_t[head] + jnp.concatenate(own_dq, axis=1)
    levels = spread_matrix()
    pairs = levels[0][:BLOCK, :HALF]
    near_out[0, :BLOCK] = (edge[0] + dot(pairs, g1[3 * HALF :].astype(BF16))).astype(BF16)
    near_out[0, BLOCK:] = g1[HALF : 2 * HALF].astype(BF16)
    near_out[1, :BLOCK] = (edge[1] + dot(pairs, g1[:HALF].astype(BF16))).astype(BF16)
    near_out[1, BLOCK:] = g1[2 * HALF : 3 * HALF].astype(BF16)
    dq_ref[...] = jnp.concatenate(dq_t, axis=0).T.astype(BF16)
    write(dq_ref, dq_out)

    partial = dot(att16_t.T, w_ref[...])
    for r in range(heads):
        part[r] = partial[:, r * FEAT : (r + 1) * FEAT].astype(BF16)
    for r, target in enumerate(across):
        send(part.at[target[1]], got_part.at[r], x_send, x_recv.at[1], target)

    arrived(got_major, red_recv.at[1])
    total = mine[major].astype(F32)
    for r in range(zs - 1):
        total = total + got_major[r].astype(F32)
    lines[minor] = total.astype(BF16)
    for target in seconds:
        send(lines.at[minor], lines.at[minor], red_send, red_recv.at[2], target)
    send(near_out.at[0], got_near.at[1], grad_send, grad_recv.at[0], left)
    send(near_out.at[1], got_near.at[0], grad_send, grad_recv.at[0], right)
    arrived(from_mate, grad_recv.at[6])
    kept = pl.ds(pl.multiple_of(2 * HALF + 96 + (1 - side) * 48, 16), 48)
    gsum[kept] = (gsum[kept].astype(F32) + from_mate[...].astype(F32)).astype(BF16)
    for slot in range(3):
        src = rows_of(gsum, 2 * HALF + 96 + (1 - side) * 48 + slot * 16, 16)
        send(src, got4.at[slot], grad_send, grad_recv.at[4], four[(1, 0, 2)[slot]])
    arrived(lines.at[: ys - 1], red_recv.at[2])
    total = lines[0].astype(F32)
    for i in range(1, ys):
        total = total + lines[i].astype(F32)

    def store_piece(half, i):
        window = pl.ds(pl.multiple_of(half * BLOCK + i * chunk, chunk), chunk)
        pg_ref[window] = final[half, i].astype(F32)
        write(pg_ref.at[window], pg_out.at[window])

    line = final.at[core, major]
    final[core, major] = total.astype(BF16)
    for r, target in enumerate(firsts):
        send(line, line, red_send, last_recv.at[r], target)
    send(line, line, red_send, sib_recv.at[0], sibling)
    store_piece(core, major)

    if heads > 1:
        arrived(got_part, x_recv.at[1])
    projected = part[h].astype(F32)
    for r in range(heads - 1):
        projected = projected + got_part[r].astype(F32)
    proj_ref[...] = projected.astype(BF16)
    write(proj_ref, proj_out)

    order = sorted(range(1, zs), key=lambda r: min(r, zs - r))

    def hand_on(distances):
        for r in distances:
            arrived(line, last_recv.at[r - 1])
            piece = final.at[core, lax.rem(major + zs - r, zs)]
            send(piece, piece, red_send, sib_recv.at[r], sibling)
            store_piece(core, lax.rem(major + zs - r, zs))

    hand_on(order[:4])

    arrived(got4, grad_recv.at[4])
    arrived(got3, grad_recv.at[3])
    arrived(got2, grad_recv.at[2])
    arrived(got_near, grad_recv.at[0])
    rows_grad = e_near[...] + jnp.concatenate([got_near[0, :BLOCK], got_near[1, :BLOCK]], axis=0).astype(F32)
    rows_grad = rows_grad + dot(levels[0], jnp.concatenate([got_near[1, BLOCK:], got_near[0, BLOCK:]], axis=0))
    for level, got in ((1, got2), (2, got3), (3, got4)):
        total = got[0].astype(F32)
        for i in range(1, got.shape[0]):
            total = total + got[i].astype(F32)
        rows_grad = rows_grad + dot(levels[level], total.astype(BF16))
    dk_ref[...] = rows_grad[:, :FEAT].astype(BF16)
    dv_ref[...] = rows_grad[:, FEAT:].astype(BF16)
    write(dk_ref, dk_out)
    write(dv_ref, dv_out)

    hand_on(order[4:])
    for r in [0, *order]:
        arrived(line, sib_recv.at[r])
        store_piece(1 - core, lax.rem(minor + zs - r, zs))

    arrived(up.at[: 48 + 96 + 2 * HALF], row_send)
    arrived(up.at[: 2 * BLOCK + 2 * HALF], row_send)
    arrived(up.at[: 48 + HALF + PART], row_send)
    arrived(from_sib, grad_send)
    arrived(up.at[: 48 + 96 + 2 * HALF + 48], grad_send)
    arrived(near_out, grad_send)
    if heads > 1:
        arrived(gfull.at[0 : heads - 1], x_send)
        arrived(got_part, x_send)
    arrived(got_half, red_send)
    arrived(got_major, red_send)
    arrived(lines.at[: ys - 1], red_send)
    arrived(final.at[0, 0 : zs - 1], red_send)
    arrived(final.at[0], red_send)
    for result in (proj_ref, dq_ref, dk_ref, dv_ref, pg_ref):
        arrived(result, out_sem)


def finish(*refs):
    results, outs, held, load_sems, store_sem = refs[:5], refs[5:10], refs[10:15], refs[15], refs[16]
    whole = pl.ds(0, ROWS)
    parts = [(4, pl.ds(i * ROWS // 4, ROWS // 4)) for i in range(4)] + [(i, whole) for i in range(4)]
    loads = [
        pltpu.make_async_copy(results[i].at[rows], held[i].at[rows], load_sems.at[n])
        for n, (i, rows) in enumerate(parts)
    ]
    for load in loads:
        load.start()
    for load, (i, rows) in zip(loads, parts):
        load.wait()
        pltpu.make_async_copy(held[i].at[rows], outs[i].at[rows], store_sem).start()
    for ref in held:
        pltpu.make_async_copy(ref, ref, store_sem).wait()


def body(zs, ys, queries, keys, values, grad_out, proj_weight):
    devices = lax.axis_size("seq")
    heads = lax.axis_size("head")
    model = proj_weight.shape[1]
    chunk = BLOCK // zs
    hbm = pl.BlockSpec(memory_space=pltpu.HBM)
    wide = 2 * FEAT
    scratch = [
        ((ROWS, FEAT), BF16),
        ((ROWS, FEAT), BF16),
        ((ROWS, FEAT), BF16),
        ((ROWS, FEAT), BF16),
        ((FEAT, model), F32),
        ((ROWS, FEAT), BF16),
        ((FEAT, model), BF16),
        ((4 * BLOCK, wide), BF16),
        ((4 * HALF, wide), BF16),
        ((240, wide), BF16),
        ((UPPER, wide), BF16),
        ((heads, ROWS, FEAT), BF16),
        ((2, BLOCK, wide), F32),
        ((ROWS, wide), F32),
        ((4 * HALF, wide), F32),
        ((2, BLOCK + HALF, wide), BF16),
        ((UPPER, wide), BF16),
        ((HALF + PART, wide), BF16),
        ((2 * HALF + PART, wide), BF16),
        ((48, wide), BF16),
        ((2, BLOCK + HALF, wide), BF16),
        ((2, HALF, wide), BF16),
        ((3, HALF // 2, wide), BF16),
        ((3, HALF // 4, wide), BF16),
        ((heads, ROWS, FEAT), BF16),
        ((max(heads - 1, 1), ROWS, FEAT), BF16),
        ((HEADS_HERE, 2, OWN_KEYS, BLOCK), F32),
        ((HEADS_HERE, UPPER, ROWS), F32),
        ((2, BLOCK, model), F32),
        ((2, BLOCK, model), BF16),
        ((BLOCK, model), BF16),
        ((zs, chunk, model), BF16),
        ((zs - 1, chunk, model), BF16),
        ((ys, chunk, model), BF16),
        ((2, zs, chunk, model), BF16),
    ]
    like = jax.ShapeDtypeStruct
    dma = pltpu.SemaphoreType.DMA
    small = like((ROWS, FEAT), BF16)
    results = pl.pallas_call(
        functools.partial(kernel, devices, heads, zs, ys),
        out_shape=(small, small, small, small, like((FEAT, model), F32)),
        in_specs=[hbm] * 5,
        out_specs=[hbm] * 5,
        scratch_shapes=[pltpu.VMEM(shape, kind) for shape, kind in scratch]
        + [dma((5,)), dma, dma, dma((7,)), dma, dma((7,)), dma, dma((2,)), dma, dma((3,)), dma((zs - 1,)), dma((zs,))],
        compiler_params=pltpu.CompilerParams(
            collective_id=0, has_side_effects=True, vmem_limit_bytes=63 * 1024 * 1024
        ),
        name="attention",
    )(queries, keys, values, grad_out, proj_weight)
    return pl.pallas_call(
        finish,
        out_shape=(small, small, small, small, like((FEAT, model), F32)),
        in_specs=[hbm] * 5,
        out_specs=[hbm] * 5,
        scratch_shapes=[pltpu.VMEM((ROWS, FEAT), BF16)] * 4 + [pltpu.VMEM((FEAT, model), F32), dma((8,)), dma],
        name="finish",
    )(*results)


def solution(mesh):
    devices = mesh.shape["seq"]
    zs = math.isqrt(devices // 2)
    ys = devices // (2 * zs)
    spec = P("seq", "head")
    return jax.shard_map(
        functools.partial(body, zs, ys),
        mesh=mesh,
        in_specs=(spec, spec, spec, spec, P("head", None)),
        out_specs=(spec, spec, spec, spec, P("head", None)),
        check_vma=False,
    )
```

```python
import functools
import math

import jax
import jax.numpy as jnp
from jax import lax
from jax.experimental import pallas as pl
from jax.experimental.pallas import tpu as pltpu
from jax.sharding import PartitionSpec as P

HEAD_DIM = 128
BLOCK = 128
HALF = BLOCK // 2
ROWS = 256
FEAT = 256
HEADS_HERE = FEAT // HEAD_DIM
NEAR = 3 * BLOCK
OWN_KEYS = NEAR + 3 * HALF
UPPER = 9 * HALF
PART = 3 * 32 + 6 * 16
NEG = -1e30
SCALE = 1.0 / math.sqrt(HEAD_DIM)
EXP2_SCALE = SCALE * math.log2(math.e)
MESH = pl.DeviceIdType.MESH
F32 = jnp.float32
BF16 = jnp.bfloat16


def dot(a, b):
    return lax.dot_general(a, b, (((1,), (0,)), ((), ())), preferred_element_type=F32)


def dot_nt(a, b):
    return lax.dot_general(a, b, (((1,), (1,)), ((), ())), preferred_element_type=F32)


def dot_tn(a, b):
    return lax.dot_general(a, b, (((0,), (0,)), ((), ())), preferred_element_type=F32)


def pair_average(rows):
    row = lax.broadcasted_iota(jnp.int32, (rows // 2, rows), 0)
    column = lax.broadcasted_iota(jnp.int32, (rows // 2, rows), 1)
    return jnp.where((column >= 2 * row) & (column < 2 * row + 2), 0.5, 0.0).astype(BF16)


def averages():
    parts = []
    for level in range(1, 5):
        count = ROWS >> level
        token = lax.broadcasted_iota(jnp.int32, (count, ROWS), 1)
        first = lax.broadcasted_iota(jnp.int32, (count, ROWS), 0) * (1 << level)
        inside = (token >= first) & (token < first + (1 << level))
        parts.append(jnp.where(inside, 0.5**level, 0.0).astype(BF16))
    return jnp.concatenate(parts, axis=0)


def spread_matrix():
    parts = []
    for level in range(1, 5):
        count = ROWS >> level
        token = lax.broadcasted_iota(jnp.int32, (ROWS, count), 0)
        first = lax.broadcasted_iota(jnp.int32, (ROWS, count), 1) * (1 << level)
        inside = (token >= first) & (token < first + (1 << level))
        parts.append(jnp.where(inside, 0.5**level, 0.0).astype(BF16))
    return parts


def kernel(
    devices, heads, zs, ys,
    q_in, k_in, v_in, go_in, w_in,
    proj_out, dq_out, dk_out, dv_out, pg_out,
    proj_ref, dq_ref, dk_ref, dv_ref, pg_ref, q_ref, w_ref, ext, lv1, own, up, gfull,
    edge, e_near, g1, near_out, gu, from_sib, gsum, from_mate, got_near, got2, got3, got4,
    part, got_part, s_own, s_up, pg32, pg16, got_half, mine, got_major, lines, final,
    in_sem, out_sem, row_send, row_recv, grad_send, grad_recv, x_send, x_recv, red_send, red_recv, last_recv, sib_recv,
):
    d = lax.axis_index("seq")
    h = lax.axis_index("head")
    core = lax.rem(d, 2)
    y = lax.rem(d // 2, ys)
    z = d // (2 * ys)
    chip = d // 2
    quad = d // 4
    side = lax.rem(chip, 2)

    def at(target):
        return (lax.rem(target + 2 * devices, devices), h)

    def send(src, dst, send_sem, recv_sem, target):
        copy = pltpu.make_async_remote_copy(
            src_ref=src, dst_ref=dst, send_sem=send_sem, recv_sem=recv_sem,
            device_id=target, device_id_type=MESH,
        )
        copy.start()

    def arrived(ref, sem):
        pltpu.make_async_copy(ref, ref, sem).wait()

    def write(src, dst):
        pltpu.make_async_copy(src, dst, out_sem).start()

    def rows_of(ref, first, count):
        return ref.at[pl.ds(pl.multiple_of(first, 16), count)]

    def far(index, total):
        wide = 3 - 6 * lax.rem(index, 2)
        return [lax.rem(index + o + total, total) for o in (2, -2, wide)]

    sibling = (d + 1 - 2 * core, h)
    mate = (4 * quad + 2 * (1 - side) + core, h)
    left, right = at(d - 1), at(d + 1)
    two = [at(d + 2), at(d - 2)]
    three = [(2 * t + core, h) for t in far(chip, devices // 2)]
    four = [(4 * t + 2 * (1 - side) + core, h) for t in far(quad, devices // 4)]
    across = [(d, lax.rem(h + r, heads)) for r in range(1, heads)]

    def z_peer(r):
        return lax.rem(z + r, zs) * (2 * ys) + 2 * y + core

    def y_peer(r):
        return z * (2 * ys) + 2 * lax.rem(y + r, ys) + core

    swap = core == 1
    major, minor = jnp.where(swap, y, z), jnp.where(swap, z, y)
    firsts = [(jnp.where(swap, y_peer(r), z_peer(r)), h) for r in range(1, zs)]
    seconds = [(jnp.where(swap, z_peer(r), y_peer(r)), h) for r in range(1, ys)]

    own_rows = ext.at[BLOCK : BLOCK + ROWS]
    loads = [
        (k_in, own_rows.at[:, :FEAT]), (v_in, own_rows.at[:, FEAT:]),
        (go_in, gfull.at[h]), (q_in, q_ref), (w_in, w_ref),
    ]
    loads = [pltpu.make_async_copy(src, dst, in_sem.at[i]) for i, (src, dst) in enumerate(loads)]
    for load in loads:
        load.start()

    barrier = pltpu.get_barrier_semaphore()
    everyone = [*four, *three, left, right, *two, mate, *across, *firsts, *seconds]
    for target in everyone:
        pl.semaphore_signal(barrier, inc=1, device_id=target, device_id_type=MESH)

    loads[0].wait()
    loads[1].wait()

    own[...] = dot(averages(), ext[BLOCK : BLOCK + ROWS]).astype(BF16)
    for load in loads[2:]:
        load.wait()
    pl.semaphore_wait(barrier, len(everyone))

    mine_part = 3 * HALF + core * PART
    for slot in range(3):
        dst = rows_of(up, mine_part + 96 + side * 48 + slot * 16, 16)
        send(own.at[224:240], dst, row_send, row_recv.at[4], four[slot])
    for slot in range(3):
        dst = rows_of(up, mine_part + slot * 32, 32)
        send(own.at[192:224], dst, row_send, row_recv.at[3], three[slot])
    for slot in range(2):
        send(own.at[128:192], up.at[slot * HALF : (slot + 1) * HALF], row_send, row_recv.at[2], two[slot])
    send(ext.at[BLOCK : 2 * BLOCK], ext.at[3 * BLOCK :], row_send, row_recv.at[0], left)
    send(ext.at[2 * BLOCK : 3 * BLOCK], ext.at[:BLOCK], row_send, row_recv.at[0], right)
    send(own.at[HALF : 2 * HALF], lv1.at[2 * HALF : 3 * HALF], row_send, row_recv.at[1], left)
    send(own.at[:HALF], lv1.at[HALF : 2 * HALF], row_send, row_recv.at[1], right)
    for target in across:
        send(gfull.at[h], gfull.at[h], x_send, x_recv.at[0], target)

    taken = rows_of(up, mine_part + 96 + (1 - side) * 48, 48)
    arrived(taken, row_recv.at[4])
    send(taken, taken, row_send, row_recv.at[5], mate)
    send(taken, taken, row_send, row_recv.at[6], sibling)
    level3 = rows_of(up, mine_part, 96)
    arrived(level3, row_recv.at[3])
    send(level3, level3, row_send, row_recv.at[6], sibling)
    arrived(up.at[: 2 * HALF], row_recv.at[2])
    send(rows_of(up, core * HALF, HALF), up.at[2 * HALF : 3 * HALF], row_send, row_recv.at[6], sibling)
    handed = rows_of(up, mine_part + 96 + side * 48, 48)
    arrived(handed, row_recv.at[5])
    send(handed, handed, row_send, row_recv.at[6], sibling)

    def bias(valid):
        return jnp.where(valid, 0.0, NEG).astype(F32)

    left_bias, right_bias = bias(d >= 1), bias(d <= devices - 2)

    def far_bias(index, total):
        wide = index + 3 - 6 * lax.rem(index, 2)
        return [bias(index >= 2), bias(index + 2 < total), bias((wide >= 0) & (wide < total))]

    bias2, bias3, bias4 = far_bias(d, devices), far_bias(chip, devices // 2), far_bias(quad, devices // 4)
    up_bias = [(HALF, b) for b in bias2]
    for _ in range(2):
        up_bias += [(32, b) for b in bias3] + [(16, b) for b in bias4 + bias4]

    def head_cols(head):
        return slice(head * HEAD_DIM, (head + 1) * HEAD_DIM)

    def value_cols(head):
        return slice(FEAT + head * HEAD_DIM, FEAT + (head + 1) * HEAD_DIM)

    def block_keys(block, cols):
        near = ext[block * BLOCK : block * BLOCK + NEAR, cols]
        return jnp.concatenate([near, lv1[block * HALF : block * HALF + 3 * HALF, cols]], axis=0)

    def block_queries(block, head):
        return q_ref[block * BLOCK : (block + 1) * BLOCK, head_cols(head)]

    arrived(ext.at[: 2 * BLOCK], row_recv.at[0])
    lv1[:HALF] = dot(pair_average(BLOCK), ext[3 * BLOCK :]).astype(BF16)
    lv1[3 * HALF :] = dot(pair_average(BLOCK), ext[:BLOCK]).astype(BF16)
    arrived(lv1.at[: 2 * HALF], row_recv.at[1])
    own_peak = [[None] * 2 for _ in range(HEADS_HERE)]
    for head in range(HEADS_HERE):
        for block in range(2):
            scores = dot_nt(block_keys(block, head_cols(head)), block_queries(block, head))
            if block == 0:
                pieces = [
                    scores[:BLOCK] + left_bias,
                    scores[BLOCK:NEAR],
                    scores[NEAR : NEAR + HALF] + right_bias,
                    scores[NEAR + HALF : NEAR + 2 * HALF] + left_bias,
                    scores[NEAR + 2 * HALF :] + right_bias,
                ]
            else:
                pieces = [
                    scores[: 2 * BLOCK],
                    scores[2 * BLOCK : NEAR] + right_bias,
                    scores[NEAR : NEAR + HALF] + left_bias,
                    scores[NEAR + HALF : NEAR + 2 * HALF] + right_bias,
                    scores[NEAR + 2 * HALF :] + left_bias,
                ]
            scores = jnp.concatenate(pieces, axis=0)
            s_own[head, block] = scores
            own_peak[head][block] = scores.max(axis=0, keepdims=True)

    if heads > 1:
        arrived(gfull.at[0 : heads - 1], x_recv.at[0])
    grad_full = jnp.concatenate([gfull[r] for r in range(heads)], axis=1)
    grad = dot_nt(grad_full, w_ref[...]).astype(BF16)
    grad_t = dot_nt(w_ref[...], grad_full).astype(BF16)

    arrived(up.at[: HALF + PART], row_recv.at[6])
    att_t = []
    for head in range(HEADS_HERE):
        raw = dot_nt(up[:, head_cols(head)], q_ref[:, head_cols(head)])
        pieces, first = [], 0
        for count, piece_bias in up_bias:
            pieces.append(raw[first : first + count] + piece_bias)
            first += count
        raw = jnp.concatenate(pieces, axis=0)
        peak = jnp.maximum(jnp.concatenate(own_peak[head], axis=1), raw.max(axis=0, keepdims=True))
        lifted_up = jnp.exp2((raw - peak) * EXP2_SCALE)
        total = lifted_up.sum(axis=0, keepdims=True)
        own_total = []
        for block in range(2):
            block_peak = peak[:, block * BLOCK : (block + 1) * BLOCK]
            lifted = jnp.exp2((s_own[head, block] - block_peak) * EXP2_SCALE)
            s_own[head, block] = lifted
            own_total.append(lifted.sum(axis=0, keepdims=True))
        inv = 1.0 / (total + jnp.concatenate(own_total, axis=1))
        prob_up = lifted_up * inv
        s_up[head] = prob_up
        up_att = dot_tn(up[:, value_cols(head)], prob_up.astype(BF16))
        own_att = []
        for block in range(2):
            prob = s_own[head, block] * inv[:, block * BLOCK : (block + 1) * BLOCK]
            s_own[head, block] = prob
            own_att.append(dot_tn(block_keys(block, value_cols(head)), prob.astype(BF16)))
        att_t.append(up_att + jnp.concatenate(own_att, axis=1))
    att16_t = jnp.concatenate(att_t, axis=0).astype(BF16)

    for c in range(2):
        half = dot(att16_t[c * BLOCK : (c + 1) * BLOCK], grad_full)
        pg32[c] = half
        pg16[c] = half.astype(BF16)
    send(pg16.at[1 - core], got_half, red_send, red_recv.at[0], sibling)

    delta = []
    dq_t = []
    for head in range(HEADS_HERE):
        g_t = grad_t[head_cols(head)]
        delta.append((g_t.astype(F32) * att_t[head]).sum(axis=0, keepdims=True))
        prob = s_up[head]
        dprob = dot(up[:, value_cols(head)], g_t)
        dscore = (prob * (dprob - delta[head]) * SCALE).astype(BF16)
        dq_t.append(dot_tn(up[:, head_cols(head)], dscore))
        gu[:, head_cols(head)] = dot(dscore, q_ref[:, head_cols(head)]).astype(BF16)
        gu[:, value_cols(head)] = dot(prob.astype(BF16), grad[:, head_cols(head)]).astype(BF16)
    send(rows_of(gu, 3 * HALF + (1 - core) * PART, PART), from_sib.at[HALF:], grad_send, grad_recv.at[5], sibling)
    send(gu.at[2 * HALF : 3 * HALF], from_sib.at[:HALF], grad_send, grad_recv.at[5], sibling)

    arrived(got_half, red_recv.at[0])
    chunk, width = BLOCK // zs, mine.shape[3]
    for p in range(2):
        cols = slice(p * width, (p + 1) * width)
        for i in range(zs):
            window = slice(i * chunk, (i + 1) * chunk)
            mine[p, i] = (pg32[core, window, cols] + got_half[window, cols].astype(F32)).astype(BF16)
        for r, target in enumerate(firsts):
            src = mine.at[p, lax.rem(major + r + 1, zs)]
            send(src, got_major.at[p, r], red_send, red_recv.at[1 + p], target)

    arrived(from_sib, grad_recv.at[5])
    gsum[2 * HALF :] = (gu[pl.ds(pl.multiple_of(mine_part, 16), PART)].astype(F32) + from_sib[HALF:].astype(F32)).astype(BF16)
    send(rows_of(gsum, 2 * HALF + 96 + side * 48, 48), from_mate, grad_send, grad_recv.at[6], mate)
    for slot in range(3):
        src = gsum.at[2 * HALF + slot * 32 : 2 * HALF + (slot + 1) * 32]
        send(src, got3.at[slot], grad_send, grad_recv.at[3], three[(1, 0, 2)[slot]])
    gsum[: 2 * HALF] = gu[: 2 * HALF]
    shared = pl.ds(pl.multiple_of(core * HALF, 16), HALF)
    gsum[shared] = (gu[shared].astype(F32) + from_sib[:HALF].astype(F32)).astype(BF16)
    for slot in range(2):
        src = gsum.at[slot * HALF : (slot + 1) * HALF]
        send(src, got2.at[slot], grad_send, grad_recv.at[2], two[1 - slot])

    for head in range(HEADS_HERE):
        own_dq = []
        for block in range(2):
            cols = slice(block * BLOCK, (block + 1) * BLOCK)
            prob = s_own[head, block]
            dprob = dot(block_keys(block, value_cols(head)), grad_t[head_cols(head), cols])
            dscore = (prob * (dprob - delta[head][:, cols]) * SCALE).astype(BF16)
            own_dq.append(dot_tn(block_keys(block, head_cols(head)), dscore))
            dkey = dot(dscore, block_queries(block, head))
            dval = dot(prob.astype(BF16), grad[cols, head_cols(head)])
            for grads, column in ((dkey, head_cols(head)), (dval, value_cols(head))):
                if block == 0:
                    edge[0, :, column] = grads[:BLOCK]
                    e_near[:, column] = grads[BLOCK:NEAR]
                    g1[: 3 * HALF, column] = grads[NEAR:]
                else:
                    e_near[:, column] = e_near[:, column] + grads[: 2 * BLOCK]
                    edge[1, :, column] = grads[2 * BLOCK : NEAR]
                    g1[HALF : 3 * HALF, column] = g1[HALF : 3 * HALF, column] + grads[NEAR : NEAR + 2 * HALF]
                    g1[3 * HALF :, column] = grads[NEAR + 2 * HALF :]
        dq_t[head] = dq_t[head] + jnp.concatenate(own_dq, axis=1)
    levels = spread_matrix()
    pairs = levels[0][:BLOCK, :HALF]
    near_out[0, :BLOCK] = (edge[0] + dot(pairs, g1[3 * HALF :].astype(BF16))).astype(BF16)
    near_out[0, BLOCK:] = g1[HALF : 2 * HALF].astype(BF16)
    near_out[1, :BLOCK] = (edge[1] + dot(pairs, g1[:HALF].astype(BF16))).astype(BF16)
    near_out[1, BLOCK:] = g1[2 * HALF : 3 * HALF].astype(BF16)
    dq_ref[...] = jnp.concatenate(dq_t, axis=0).T.astype(BF16)
    write(dq_ref, dq_out)

    partial = dot(att16_t.T, w_ref[...])
    for r in range(heads):
        part[r] = partial[:, r * FEAT : (r + 1) * FEAT].astype(BF16)
    for r, target in enumerate(across):
        send(part.at[target[1]], got_part.at[r], x_send, x_recv.at[1], target)

    for p in range(2):
        arrived(got_major.at[p], red_recv.at[1 + p])
        total = mine[p, major].astype(F32)
        for r in range(zs - 1):
            total = total + got_major[p, r].astype(F32)
        lines[p, minor] = total.astype(BF16)
        for target in seconds:
            send(lines.at[p, minor], lines.at[p, minor], red_send, red_recv.at[3 + p], target)
    send(near_out.at[0], got_near.at[1], grad_send, grad_recv.at[0], left)
    send(near_out.at[1], got_near.at[0], grad_send, grad_recv.at[0], right)
    arrived(from_mate, grad_recv.at[6])
    kept = pl.ds(pl.multiple_of(2 * HALF + 96 + (1 - side) * 48, 16), 48)
    gsum[kept] = (gsum[kept].astype(F32) + from_mate[...].astype(F32)).astype(BF16)
    for slot in range(3):
        src = rows_of(gsum, 2 * HALF + 96 + (1 - side) * 48 + slot * 16, 16)
        send(src, got4.at[slot], grad_send, grad_recv.at[4], four[(1, 0, 2)[slot]])

    def store_piece(half, p, i):
        rows = pl.ds(pl.multiple_of(half * BLOCK + i * chunk, chunk), chunk)
        cols = slice(p * width, (p + 1) * width)
        pg_ref[rows, cols] = final[half, p, i].astype(F32)
        write(pg_ref.at[rows, cols], pg_out.at[rows, cols])

    line = final.at[core, 0, major]
    for p in range(2):
        arrived(lines.at[p, : ys - 1], red_recv.at[3 + p])
        total = lines[p, 0].astype(F32)
        for i in range(1, ys):
            total = total + lines[p, i].astype(F32)
        piece = final.at[core, p, major]
        final[core, p, major] = total.astype(BF16)
        for r, target in enumerate(firsts):
            send(piece, piece, red_send, last_recv.at[p, r], target)
        send(piece, piece, red_send, sib_recv.at[p, 0], sibling)
        store_piece(core, p, major)

    if heads > 1:
        arrived(got_part, x_recv.at[1])
    projected = part[h].astype(F32)
    for r in range(heads - 1):
        projected = projected + got_part[r].astype(F32)
    proj_ref[...] = projected.astype(BF16)
    write(proj_ref, proj_out)

    order = sorted(range(1, zs), key=lambda r: min(r, zs - r))

    def hand_on(distances):
        for r in distances:
            for p in range(2):
                arrived(line, last_recv.at[p, r - 1])
                i = lax.rem(major + zs - r, zs)
                piece = final.at[core, p, i]
                send(piece, piece, red_send, sib_recv.at[p, r], sibling)
                store_piece(core, p, i)

    hand_on(order[:4])

    arrived(got4, grad_recv.at[4])
    arrived(got3, grad_recv.at[3])
    arrived(got2, grad_recv.at[2])
    arrived(got_near, grad_recv.at[0])
    rows_grad = e_near[...] + jnp.concatenate([got_near[0, :BLOCK], got_near[1, :BLOCK]], axis=0).astype(F32)
    rows_grad = rows_grad + dot(levels[0], jnp.concatenate([got_near[1, BLOCK:], got_near[0, BLOCK:]], axis=0))
    for level, got in ((1, got2), (2, got3), (3, got4)):
        total = got[0].astype(F32)
        for i in range(1, got.shape[0]):
            total = total + got[i].astype(F32)
        rows_grad = rows_grad + dot(levels[level], total.astype(BF16))
    dk_ref[...] = rows_grad[:, :FEAT].astype(BF16)
    dv_ref[...] = rows_grad[:, FEAT:].astype(BF16)
    write(dk_ref, dk_out)
    write(dv_ref, dv_out)

    hand_on(order[4:])
    for r in [0, *order]:
        for p in range(2):
            arrived(line, sib_recv.at[p, r])
            store_piece(1 - core, p, lax.rem(minor + zs - r, zs))

    arrived(up.at[: 48 + 96 + 2 * HALF], row_send)
    arrived(up.at[: 2 * BLOCK + 2 * HALF], row_send)
    arrived(up.at[: 48 + HALF + PART], row_send)
    arrived(from_sib, grad_send)
    arrived(up.at[: 48 + 96 + 2 * HALF + 48], grad_send)
    arrived(near_out, grad_send)
    if heads > 1:
        arrived(gfull.at[0 : heads - 1], x_send)
        arrived(got_part, x_send)
    arrived(got_half, red_send)
    arrived(got_major, red_send)
    arrived(lines.at[:, : ys - 1], red_send)
    arrived(final.at[0, :, : zs - 1], red_send)
    arrived(final.at[0], red_send)
    for result in (proj_ref, dq_ref, dk_ref, dv_ref, pg_ref):
        arrived(result, out_sem)


def finish(*refs):
    results, outs, held, load_sems, store_sem = refs[:5], refs[5:10], refs[10:15], refs[15], refs[16]
    whole = pl.ds(0, ROWS)
    parts = [(4, pl.ds(i * ROWS // 4, ROWS // 4)) for i in range(4)] + [(i, whole) for i in range(4)]
    loads = [
        pltpu.make_async_copy(results[i].at[rows], held[i].at[rows], load_sems.at[n])
        for n, (i, rows) in enumerate(parts)
    ]
    for load in loads:
        load.start()
    for load, (i, rows) in zip(loads, parts):
        load.wait()
        pltpu.make_async_copy(held[i].at[rows], outs[i].at[rows], store_sem).start()
    for ref in held:
        pltpu.make_async_copy(ref, ref, store_sem).wait()


def body(zs, ys, queries, keys, values, grad_out, proj_weight):
    devices = lax.axis_size("seq")
    heads = lax.axis_size("head")
    model = proj_weight.shape[1]
    chunk = BLOCK // zs
    hbm = pl.BlockSpec(memory_space=pltpu.HBM)
    wide = 2 * FEAT
    scratch = [
        ((ROWS, FEAT), BF16),
        ((ROWS, FEAT), BF16),
        ((ROWS, FEAT), BF16),
        ((ROWS, FEAT), BF16),
        ((FEAT, model), F32),
        ((ROWS, FEAT), BF16),
        ((FEAT, model), BF16),
        ((4 * BLOCK, wide), BF16),
        ((4 * HALF, wide), BF16),
        ((240, wide), BF16),
        ((UPPER, wide), BF16),
        ((heads, ROWS, FEAT), BF16),
        ((2, BLOCK, wide), F32),
        ((ROWS, wide), F32),
        ((4 * HALF, wide), F32),
        ((2, BLOCK + HALF, wide), BF16),
        ((UPPER, wide), BF16),
        ((HALF + PART, wide), BF16),
        ((2 * HALF + PART, wide), BF16),
        ((48, wide), BF16),
        ((2, BLOCK + HALF, wide), BF16),
        ((2, HALF, wide), BF16),
        ((3, HALF // 2, wide), BF16),
        ((3, HALF // 4, wide), BF16),
        ((heads, ROWS, FEAT), BF16),
        ((max(heads - 1, 1), ROWS, FEAT), BF16),
        ((HEADS_HERE, 2, OWN_KEYS, BLOCK), F32),
        ((HEADS_HERE, UPPER, ROWS), F32),
        ((2, BLOCK, model), F32),
        ((2, BLOCK, model), BF16),
        ((BLOCK, model), BF16),
        ((2, zs, chunk, model // 2), BF16),
        ((2, zs - 1, chunk, model // 2), BF16),
        ((2, ys, chunk, model // 2), BF16),
        ((2, 2, zs, chunk, model // 2), BF16),
    ]
    like = jax.ShapeDtypeStruct
    dma = pltpu.SemaphoreType.DMA
    small = like((ROWS, FEAT), BF16)
    results = pl.pallas_call(
        functools.partial(kernel, devices, heads, zs, ys),
        out_shape=(small, small, small, small, like((FEAT, model), F32)),
        in_specs=[hbm] * 5,
        out_specs=[hbm] * 5,
        scratch_shapes=[pltpu.VMEM(shape, kind) for shape, kind in scratch]
        + [dma((5,)), dma, dma, dma((7,)), dma, dma((7,)), dma, dma((2,)), dma, dma((5,)), dma((2, zs - 1)), dma((2, zs))],
        compiler_params=pltpu.CompilerParams(
            collective_id=0, has_side_effects=True, vmem_limit_bytes=63 * 1024 * 1024
        ),
        name="attention",
    )(queries, keys, values, grad_out, proj_weight)
    return pl.pallas_call(
        finish,
        out_shape=(small, small, small, small, like((FEAT, model), F32)),
        in_specs=[hbm] * 5,
        out_specs=[hbm] * 5,
        scratch_shapes=[pltpu.VMEM((ROWS, FEAT), BF16)] * 4 + [pltpu.VMEM((FEAT, model), F32), dma((8,)), dma],
        name="finish",
    )(*results)


def solution(mesh):
    devices = mesh.shape["seq"]
    zs = math.isqrt(devices // 2)
    ys = devices // (2 * zs)
    spec = P("seq", "head")
    return jax.shard_map(
        functools.partial(body, zs, ys),
        mesh=mesh,
        in_specs=(spec, spec, spec, spec, P("head", None)),
        out_specs=(spec, spec, spec, spec, P("head", None)),
        check_vma=False,
    )
```

```python
import functools
import math

import jax
import jax.numpy as jnp
from jax import lax
from jax.experimental import pallas as pl
from jax.experimental.pallas import tpu as pltpu
from jax.sharding import PartitionSpec as P

HEAD_DIM = 128
BLOCK = 128
HALF = BLOCK // 2
ROWS = 256
FEAT = 256
HEADS_HERE = FEAT // HEAD_DIM
NEAR = 3 * BLOCK
OWN_KEYS = NEAR + 3 * HALF
UPPER = 9 * HALF
PART = 3 * 32 + 6 * 16
NEG = -1e30
SCALE = 1.0 / math.sqrt(HEAD_DIM)
EXP2_SCALE = SCALE * math.log2(math.e)
MESH = pl.DeviceIdType.MESH
F32 = jnp.float32
BF16 = jnp.bfloat16


def dot(a, b):
    return lax.dot_general(a, b, (((1,), (0,)), ((), ())), preferred_element_type=F32)


def dot_nt(a, b):
    return lax.dot_general(a, b, (((1,), (1,)), ((), ())), preferred_element_type=F32)


def dot_tn(a, b):
    return lax.dot_general(a, b, (((0,), (0,)), ((), ())), preferred_element_type=F32)


def pair_average(rows):
    row = lax.broadcasted_iota(jnp.int32, (rows // 2, rows), 0)
    column = lax.broadcasted_iota(jnp.int32, (rows // 2, rows), 1)
    return jnp.where((column >= 2 * row) & (column < 2 * row + 2), 0.5, 0.0).astype(BF16)


def averages():
    parts = []
    for level in range(1, 5):
        count = ROWS >> level
        token = lax.broadcasted_iota(jnp.int32, (count, ROWS), 1)
        first = lax.broadcasted_iota(jnp.int32, (count, ROWS), 0) * (1 << level)
        inside = (token >= first) & (token < first + (1 << level))
        parts.append(jnp.where(inside, 0.5**level, 0.0).astype(BF16))
    return jnp.concatenate(parts, axis=0)


def spread_matrix():
    parts = []
    for level in range(1, 5):
        count = ROWS >> level
        token = lax.broadcasted_iota(jnp.int32, (ROWS, count), 0)
        first = lax.broadcasted_iota(jnp.int32, (ROWS, count), 1) * (1 << level)
        inside = (token >= first) & (token < first + (1 << level))
        parts.append(jnp.where(inside, 0.5**level, 0.0).astype(BF16))
    return parts


def kernel(
    devices, heads, zs, ys,
    q_in, k_in, v_in, go_in, w_in,
    proj_out, dq_out, dk_out, dv_out, pg_out,
    proj_ref, dq_ref, dk_ref, dv_ref, pg_ref, q_ref, w_ref, ext, lv1, own, up, gfull,
    edge, e_near, g1, near_out, gu, from_sib, gsum, from_mate, got_near, got2, got3, got4,
    part, got_part, s_own, s_up, pg32, pg16, got_half, mine, got_major, lines, final,
    in_sem, out_sem, row_send, row_recv, grad_send, grad_recv, x_send, x_recv, red_send, red_recv, last_recv, sib_recv,
):
    d = lax.axis_index("seq")
    h = lax.axis_index("head")
    core = lax.rem(d, 2)
    y = lax.rem(d // 2, ys)
    z = d // (2 * ys)
    chip = d // 2
    quad = d // 4
    side = lax.rem(chip, 2)

    def at(target):
        return (lax.rem(target + 2 * devices, devices), h)

    def send(src, dst, send_sem, recv_sem, target):
        copy = pltpu.make_async_remote_copy(
            src_ref=src, dst_ref=dst, send_sem=send_sem, recv_sem=recv_sem,
            device_id=target, device_id_type=MESH,
        )
        copy.start()

    def arrived(ref, sem):
        pltpu.make_async_copy(ref, ref, sem).wait()

    def write(src, dst):
        pltpu.make_async_copy(src, dst, out_sem).start()

    def rows_of(ref, first, count):
        return ref.at[pl.ds(pl.multiple_of(first, 16), count)]

    def far(index, total):
        wide = 3 - 6 * lax.rem(index, 2)
        return [lax.rem(index + o + total, total) for o in (2, -2, wide)]

    sibling = (d + 1 - 2 * core, h)
    mate = (4 * quad + 2 * (1 - side) + core, h)
    left, right = at(d - 1), at(d + 1)
    two = [at(d + 2), at(d - 2)]
    three = [(2 * t + core, h) for t in far(chip, devices // 2)]
    four = [(4 * t + 2 * (1 - side) + core, h) for t in far(quad, devices // 4)]
    across = [(d, lax.rem(h + r, heads)) for r in range(1, heads)]

    def z_peer(r):
        return lax.rem(z + r, zs) * (2 * ys) + 2 * y + core

    def y_peer(r):
        return z * (2 * ys) + 2 * lax.rem(y + r, ys) + core

    swap = core == 1
    major, minor = jnp.where(swap, y, z), jnp.where(swap, z, y)
    firsts = [(jnp.where(swap, y_peer(r), z_peer(r)), h) for r in range(1, zs)]
    seconds = [(jnp.where(swap, z_peer(r), y_peer(r)), h) for r in range(1, ys)]
    far_first = sorted(range(1, zs), key=lambda r: -min(r, zs - r))

    own_rows = ext.at[BLOCK : BLOCK + ROWS]
    loads = [
        (k_in, own_rows.at[:, :FEAT]), (v_in, own_rows.at[:, FEAT:]),
        (go_in, gfull.at[h]), (q_in, q_ref), (w_in, w_ref),
    ]
    loads = [pltpu.make_async_copy(src, dst, in_sem.at[i]) for i, (src, dst) in enumerate(loads)]
    for load in loads:
        load.start()

    barrier = pltpu.get_barrier_semaphore()
    rings = [peer for r in far_first for peer in (firsts[r - 1], seconds[r - 1])]
    everyone = [*rings[:2], *four, *three, *rings[2:6], *two, left, right, mate, *across, *rings[6:]]
    for target in everyone:
        pl.semaphore_signal(barrier, inc=1, device_id=target, device_id_type=MESH)

    loads[0].wait()
    loads[1].wait()

    own[...] = dot(averages(), ext[BLOCK : BLOCK + ROWS]).astype(BF16)
    for load in loads[2:]:
        load.wait()
    pl.semaphore_wait(barrier, len(everyone))

    mine_part = 3 * HALF + core * PART
    for slot in range(3):
        dst = rows_of(up, mine_part + 96 + side * 48 + slot * 16, 16)
        send(own.at[224:240], dst, row_send, row_recv.at[4], four[slot])
    for slot in (2, 0, 1):
        dst = rows_of(up, mine_part + slot * 32, 32)
        send(own.at[192:224], dst, row_send, row_recv.at[3], three[slot])
    for slot in range(2):
        send(own.at[128:192], up.at[slot * HALF : (slot + 1) * HALF], row_send, row_recv.at[2], two[slot])
    send(ext.at[BLOCK : 2 * BLOCK], ext.at[3 * BLOCK :], row_send, row_recv.at[0], left)
    send(ext.at[2 * BLOCK : 3 * BLOCK], ext.at[:BLOCK], row_send, row_recv.at[0], right)
    send(own.at[HALF : 2 * HALF], lv1.at[2 * HALF : 3 * HALF], row_send, row_recv.at[1], left)
    send(own.at[:HALF], lv1.at[HALF : 2 * HALF], row_send, row_recv.at[1], right)
    for target in across:
        send(gfull.at[h], gfull.at[h], x_send, x_recv.at[0], target)

    taken = rows_of(up, mine_part + 96 + (1 - side) * 48, 48)
    arrived(taken, row_recv.at[4])
    send(taken, taken, row_send, row_recv.at[5], mate)
    send(taken, taken, row_send, row_recv.at[6], sibling)
    level3 = rows_of(up, mine_part, 96)
    arrived(level3, row_recv.at[3])
    send(level3, level3, row_send, row_recv.at[6], sibling)
    arrived(up.at[: 2 * HALF], row_recv.at[2])
    send(rows_of(up, core * HALF, HALF), up.at[2 * HALF : 3 * HALF], row_send, row_recv.at[6], sibling)
    handed = rows_of(up, mine_part + 96 + side * 48, 48)
    arrived(handed, row_recv.at[5])
    send(handed, handed, row_send, row_recv.at[6], sibling)

    def bias(valid):
        return jnp.where(valid, 0.0, NEG).astype(F32)

    left_bias, right_bias = bias(d >= 1), bias(d <= devices - 2)

    def far_bias(index, total):
        wide = index + 3 - 6 * lax.rem(index, 2)
        return [bias(index >= 2), bias(index + 2 < total), bias((wide >= 0) & (wide < total))]

    bias2, bias3, bias4 = far_bias(d, devices), far_bias(chip, devices // 2), far_bias(quad, devices // 4)
    up_bias = [(HALF, b) for b in bias2]
    for _ in range(2):
        up_bias += [(32, b) for b in bias3] + [(16, b) for b in bias4 + bias4]

    def head_cols(head):
        return slice(head * HEAD_DIM, (head + 1) * HEAD_DIM)

    def value_cols(head):
        return slice(FEAT + head * HEAD_DIM, FEAT + (head + 1) * HEAD_DIM)

    def block_keys(block, cols):
        near = ext[block * BLOCK : block * BLOCK + NEAR, cols]
        return jnp.concatenate([near, lv1[block * HALF : block * HALF + 3 * HALF, cols]], axis=0)

    def block_queries(block, head):
        return q_ref[block * BLOCK : (block + 1) * BLOCK, head_cols(head)]

    arrived(ext.at[: 2 * BLOCK], row_recv.at[0])
    lv1[:HALF] = dot(pair_average(BLOCK), ext[3 * BLOCK :]).astype(BF16)
    lv1[3 * HALF :] = dot(pair_average(BLOCK), ext[:BLOCK]).astype(BF16)
    arrived(lv1.at[: 2 * HALF], row_recv.at[1])
    own_peak = [[None] * 2 for _ in range(HEADS_HERE)]
    for head in range(HEADS_HERE):
        for block in range(2):
            scores = dot_nt(block_keys(block, head_cols(head)), block_queries(block, head))
            if block == 0:
                pieces = [
                    scores[:BLOCK] + left_bias,
                    scores[BLOCK:NEAR],
                    scores[NEAR : NEAR + HALF] + right_bias,
                    scores[NEAR + HALF : NEAR + 2 * HALF] + left_bias,
                    scores[NEAR + 2 * HALF :] + right_bias,
                ]
            else:
                pieces = [
                    scores[: 2 * BLOCK],
                    scores[2 * BLOCK : NEAR] + right_bias,
                    scores[NEAR : NEAR + HALF] + left_bias,
                    scores[NEAR + HALF : NEAR + 2 * HALF] + right_bias,
                    scores[NEAR + 2 * HALF :] + left_bias,
                ]
            scores = jnp.concatenate(pieces, axis=0)
            s_own[head, block] = scores
            own_peak[head][block] = scores.max(axis=0, keepdims=True)

    if heads > 1:
        arrived(gfull.at[0 : heads - 1], x_recv.at[0])
    grad_full = jnp.concatenate([gfull[r] for r in range(heads)], axis=1)
    grad = dot_nt(grad_full, w_ref[...]).astype(BF16)
    grad_t = dot_nt(w_ref[...], grad_full).astype(BF16)

    arrived(up.at[: HALF + PART], row_recv.at[6])
    att_t = []
    for head in range(HEADS_HERE):
        raw = dot_nt(up[:, head_cols(head)], q_ref[:, head_cols(head)])
        pieces, first = [], 0
        for count, piece_bias in up_bias:
            pieces.append(raw[first : first + count] + piece_bias)
            first += count
        raw = jnp.concatenate(pieces, axis=0)
        peak = jnp.maximum(jnp.concatenate(own_peak[head], axis=1), raw.max(axis=0, keepdims=True))
        lifted_up = jnp.exp2((raw - peak) * EXP2_SCALE)
        total = lifted_up.sum(axis=0, keepdims=True)
        own_total = []
        for block in range(2):
            block_peak = peak[:, block * BLOCK : (block + 1) * BLOCK]
            lifted = jnp.exp2((s_own[head, block] - block_peak) * EXP2_SCALE)
            s_own[head, block] = lifted
            own_total.append(lifted.sum(axis=0, keepdims=True))
        inv = 1.0 / (total + jnp.concatenate(own_total, axis=1))
        prob_up = lifted_up * inv
        s_up[head] = prob_up
        up_att = dot_tn(up[:, value_cols(head)], prob_up.astype(BF16))
        own_att = []
        for block in range(2):
            prob = s_own[head, block] * inv[:, block * BLOCK : (block + 1) * BLOCK]
            s_own[head, block] = prob
            own_att.append(dot_tn(block_keys(block, value_cols(head)), prob.astype(BF16)))
        att_t.append(up_att + jnp.concatenate(own_att, axis=1))
    att16_t = jnp.concatenate(att_t, axis=0).astype(BF16)

    for c in range(2):
        half = dot(att16_t[c * BLOCK : (c + 1) * BLOCK], grad_full)
        pg32[c] = half
        pg16[c] = half.astype(BF16)
    send(pg16.at[1 - core], got_half, red_send, red_recv.at[0], sibling)

    delta = []
    dq_t = []
    for head in range(HEADS_HERE):
        g_t = grad_t[head_cols(head)]
        delta.append((g_t.astype(F32) * att_t[head]).sum(axis=0, keepdims=True))
        prob = s_up[head]
        dprob = dot(up[:, value_cols(head)], g_t)
        dscore = (prob * (dprob - delta[head]) * SCALE).astype(BF16)
        dq_t.append(dot_tn(up[:, head_cols(head)], dscore))
        gu[:, head_cols(head)] = dot(dscore, q_ref[:, head_cols(head)]).astype(BF16)
        gu[:, value_cols(head)] = dot(prob.astype(BF16), grad[:, head_cols(head)]).astype(BF16)
    send(rows_of(gu, 3 * HALF + (1 - core) * PART, PART), from_sib.at[HALF:], grad_send, grad_recv.at[5], sibling)
    send(gu.at[2 * HALF : 3 * HALF], from_sib.at[:HALF], grad_send, grad_recv.at[5], sibling)

    arrived(got_half, red_recv.at[0])
    chunk, width = BLOCK // zs, mine.shape[3]
    for p in range(2):
        cols = slice(p * width, (p + 1) * width)
        for i in range(zs):
            window = slice(i * chunk, (i + 1) * chunk)
            mine[p, i] = (pg32[core, window, cols] + got_half[window, cols].astype(F32)).astype(BF16)
        for r in far_first:
            src = mine.at[p, lax.rem(major + r, zs)]
            send(src, got_major.at[p, r - 1], red_send, red_recv.at[1 + p], firsts[r - 1])

    arrived(from_sib, grad_recv.at[5])
    gsum[2 * HALF :] = (gu[pl.ds(pl.multiple_of(mine_part, 16), PART)].astype(F32) + from_sib[HALF:].astype(F32)).astype(BF16)
    send(rows_of(gsum, 2 * HALF + 96 + side * 48, 48), from_mate, grad_send, grad_recv.at[6], mate)
    for slot in range(3):
        src = gsum.at[2 * HALF + slot * 32 : 2 * HALF + (slot + 1) * 32]
        send(src, got3.at[slot], grad_send, grad_recv.at[3], three[(1, 0, 2)[slot]])
    gsum[: 2 * HALF] = gu[: 2 * HALF]
    shared = pl.ds(pl.multiple_of(core * HALF, 16), HALF)
    gsum[shared] = (gu[shared].astype(F32) + from_sib[:HALF].astype(F32)).astype(BF16)
    for slot in range(2):
        src = gsum.at[slot * HALF : (slot + 1) * HALF]
        send(src, got2.at[slot], grad_send, grad_recv.at[2], two[1 - slot])

    for head in range(HEADS_HERE):
        own_dq = []
        for block in range(2):
            cols = slice(block * BLOCK, (block + 1) * BLOCK)
            prob = s_own[head, block]
            dprob = dot(block_keys(block, value_cols(head)), grad_t[head_cols(head), cols])
            dscore = (prob * (dprob - delta[head][:, cols]) * SCALE).astype(BF16)
            own_dq.append(dot_tn(block_keys(block, head_cols(head)), dscore))
            dkey = dot(dscore, block_queries(block, head))
            dval = dot(prob.astype(BF16), grad[cols, head_cols(head)])
            for grads, column in ((dkey, head_cols(head)), (dval, value_cols(head))):
                if block == 0:
                    edge[0, :, column] = grads[:BLOCK]
                    e_near[:, column] = grads[BLOCK:NEAR]
                    g1[: 3 * HALF, column] = grads[NEAR:]
                else:
                    e_near[:, column] = e_near[:, column] + grads[: 2 * BLOCK]
                    edge[1, :, column] = grads[2 * BLOCK : NEAR]
                    g1[HALF : 3 * HALF, column] = g1[HALF : 3 * HALF, column] + grads[NEAR : NEAR + 2 * HALF]
                    g1[3 * HALF :, column] = grads[NEAR + 2 * HALF :]
        dq_t[head] = dq_t[head] + jnp.concatenate(own_dq, axis=1)
    levels = spread_matrix()
    pairs = levels[0][:BLOCK, :HALF]
    near_out[0, :BLOCK] = (edge[0] + dot(pairs, g1[3 * HALF :].astype(BF16))).astype(BF16)
    near_out[0, BLOCK:] = g1[HALF : 2 * HALF].astype(BF16)
    near_out[1, :BLOCK] = (edge[1] + dot(pairs, g1[:HALF].astype(BF16))).astype(BF16)
    near_out[1, BLOCK:] = g1[2 * HALF : 3 * HALF].astype(BF16)
    dq_ref[...] = jnp.concatenate(dq_t, axis=0).T.astype(BF16)
    write(dq_ref, dq_out)

    partial = dot(att16_t.T, w_ref[...])
    for r in range(heads):
        part[r] = partial[:, r * FEAT : (r + 1) * FEAT].astype(BF16)
    for r, target in enumerate(across):
        send(part.at[target[1]], got_part.at[r], x_send, x_recv.at[1], target)

    for p in range(2):
        arrived(got_major.at[p], red_recv.at[1 + p])
        total = mine[p, major].astype(F32)
        for r in range(zs - 1):
            total = total + got_major[p, r].astype(F32)
        lines[p, minor] = total.astype(BF16)
        for r in far_first:
            send(lines.at[p, minor], lines.at[p, minor], red_send, red_recv.at[3 + p], seconds[r - 1])
    send(near_out.at[0], got_near.at[1], grad_send, grad_recv.at[0], left)
    send(near_out.at[1], got_near.at[0], grad_send, grad_recv.at[0], right)
    arrived(from_mate, grad_recv.at[6])
    kept = pl.ds(pl.multiple_of(2 * HALF + 96 + (1 - side) * 48, 16), 48)
    gsum[kept] = (gsum[kept].astype(F32) + from_mate[...].astype(F32)).astype(BF16)
    for slot in range(3):
        src = rows_of(gsum, 2 * HALF + 96 + (1 - side) * 48 + slot * 16, 16)
        send(src, got4.at[slot], grad_send, grad_recv.at[4], four[(1, 0, 2)[slot]])

    def store_piece(half, p, i):
        rows = pl.ds(pl.multiple_of(half * BLOCK + i * chunk, chunk), chunk)
        cols = slice(p * width, (p + 1) * width)
        pg_ref[rows, cols] = final[half, p, i].astype(F32)
        write(pg_ref.at[rows, cols], pg_out.at[rows, cols])

    line = final.at[core, 0, major]
    for p in range(2):
        arrived(lines.at[p, : ys - 1], red_recv.at[3 + p])
        total = lines[p, 0].astype(F32)
        for i in range(1, ys):
            total = total + lines[p, i].astype(F32)
        piece = final.at[core, p, major]
        final[core, p, major] = total.astype(BF16)
        for r in far_first:
            send(piece, piece, red_send, last_recv.at[p, r - 1], firsts[r - 1])
        send(piece, piece, red_send, sib_recv.at[p, 0], sibling)
        store_piece(core, p, major)

    if heads > 1:
        arrived(got_part, x_recv.at[1])
    projected = part[h].astype(F32)
    for r in range(heads - 1):
        projected = projected + got_part[r].astype(F32)
    proj_ref[...] = projected.astype(BF16)
    write(proj_ref, proj_out)

    order = sorted(range(1, zs), key=lambda r: min(r, zs - r))

    def hand_on(distances):
        for r in distances:
            for p in range(2):
                arrived(line, last_recv.at[p, r - 1])
                i = lax.rem(major + zs - r, zs)
                piece = final.at[core, p, i]
                send(piece, piece, red_send, sib_recv.at[p, r], sibling)
                store_piece(core, p, i)

    hand_on(order[:4])

    arrived(got4, grad_recv.at[4])
    arrived(got3, grad_recv.at[3])
    arrived(got2, grad_recv.at[2])
    arrived(got_near, grad_recv.at[0])
    rows_grad = e_near[...] + jnp.concatenate([got_near[0, :BLOCK], got_near[1, :BLOCK]], axis=0).astype(F32)
    rows_grad = rows_grad + dot(levels[0], jnp.concatenate([got_near[1, BLOCK:], got_near[0, BLOCK:]], axis=0))
    for level, got in ((1, got2), (2, got3), (3, got4)):
        total = got[0].astype(F32)
        for i in range(1, got.shape[0]):
            total = total + got[i].astype(F32)
        rows_grad = rows_grad + dot(levels[level], total.astype(BF16))
    dk_ref[...] = rows_grad[:, :FEAT].astype(BF16)
    dv_ref[...] = rows_grad[:, FEAT:].astype(BF16)
    write(dk_ref, dk_out)
    write(dv_ref, dv_out)

    hand_on(order[4:])
    for r in [0, *order]:
        for p in range(2):
            arrived(line, sib_recv.at[p, r])
            store_piece(1 - core, p, lax.rem(minor + zs - r, zs))

    arrived(up.at[: 48 + 96 + 2 * HALF], row_send)
    arrived(up.at[: 2 * BLOCK + 2 * HALF], row_send)
    arrived(up.at[: 48 + HALF + PART], row_send)
    arrived(from_sib, grad_send)
    arrived(up.at[: 48 + 96 + 2 * HALF + 48], grad_send)
    arrived(near_out, grad_send)
    if heads > 1:
        arrived(gfull.at[0 : heads - 1], x_send)
        arrived(got_part, x_send)
    arrived(got_half, red_send)
    arrived(got_major, red_send)
    arrived(lines.at[:, : ys - 1], red_send)
    arrived(final.at[0, :, : zs - 1], red_send)
    arrived(final.at[0], red_send)
    for result in (proj_ref, dq_ref, dk_ref, dv_ref, pg_ref):
        arrived(result, out_sem)


def finish(*refs):
    results, outs, held, load_sems, store_sem = refs[:5], refs[5:10], refs[10:15], refs[15], refs[16]
    whole = pl.ds(0, ROWS)
    parts = [(4, pl.ds(i * ROWS // 4, ROWS // 4)) for i in range(4)] + [(i, whole) for i in range(4)]
    loads = [
        pltpu.make_async_copy(results[i].at[rows], held[i].at[rows], load_sems.at[n])
        for n, (i, rows) in enumerate(parts)
    ]
    for load in loads:
        load.start()
    for load, (i, rows) in zip(loads, parts):
        load.wait()
        pltpu.make_async_copy(held[i].at[rows], outs[i].at[rows], store_sem).start()
    for ref in held:
        pltpu.make_async_copy(ref, ref, store_sem).wait()


def body(zs, ys, queries, keys, values, grad_out, proj_weight):
    devices = lax.axis_size("seq")
    heads = lax.axis_size("head")
    model = proj_weight.shape[1]
    chunk = BLOCK // zs
    hbm = pl.BlockSpec(memory_space=pltpu.HBM)
    wide = 2 * FEAT
    scratch = [
        ((ROWS, FEAT), BF16),
        ((ROWS, FEAT), BF16),
        ((ROWS, FEAT), BF16),
        ((ROWS, FEAT), BF16),
        ((FEAT, model), F32),
        ((ROWS, FEAT), BF16),
        ((FEAT, model), BF16),
        ((4 * BLOCK, wide), BF16),
        ((4 * HALF, wide), BF16),
        ((240, wide), BF16),
        ((UPPER, wide), BF16),
        ((heads, ROWS, FEAT), BF16),
        ((2, BLOCK, wide), F32),
        ((ROWS, wide), F32),
        ((4 * HALF, wide), F32),
        ((2, BLOCK + HALF, wide), BF16),
        ((UPPER, wide), BF16),
        ((HALF + PART, wide), BF16),
        ((2 * HALF + PART, wide), BF16),
        ((48, wide), BF16),
        ((2, BLOCK + HALF, wide), BF16),
        ((2, HALF, wide), BF16),
        ((3, HALF // 2, wide), BF16),
        ((3, HALF // 4, wide), BF16),
        ((heads, ROWS, FEAT), BF16),
        ((max(heads - 1, 1), ROWS, FEAT), BF16),
        ((HEADS_HERE, 2, OWN_KEYS, BLOCK), F32),
        ((HEADS_HERE, UPPER, ROWS), F32),
        ((2, BLOCK, model), F32),
        ((2, BLOCK, model), BF16),
        ((BLOCK, model), BF16),
        ((2, zs, chunk, model // 2), BF16),
        ((2, zs - 1, chunk, model // 2), BF16),
        ((2, ys, chunk, model // 2), BF16),
        ((2, 2, zs, chunk, model // 2), BF16),
    ]
    like = jax.ShapeDtypeStruct
    dma = pltpu.SemaphoreType.DMA
    small = like((ROWS, FEAT), BF16)
    results = pl.pallas_call(
        functools.partial(kernel, devices, heads, zs, ys),
        out_shape=(small, small, small, small, like((FEAT, model), F32)),
        in_specs=[hbm] * 5,
        out_specs=[hbm] * 5,
        scratch_shapes=[pltpu.VMEM(shape, kind) for shape, kind in scratch]
        + [dma((5,)), dma, dma, dma((7,)), dma, dma((7,)), dma, dma((2,)), dma, dma((5,)), dma((2, zs - 1)), dma((2, zs))],
        compiler_params=pltpu.CompilerParams(
            collective_id=0, has_side_effects=True, vmem_limit_bytes=63 * 1024 * 1024
        ),
        name="attention",
    )(queries, keys, values, grad_out, proj_weight)
    return pl.pallas_call(
        finish,
        out_shape=(small, small, small, small, like((FEAT, model), F32)),
        in_specs=[hbm] * 5,
        out_specs=[hbm] * 5,
        scratch_shapes=[pltpu.VMEM((ROWS, FEAT), BF16)] * 4 + [pltpu.VMEM((FEAT, model), F32), dma((8,)), dma],
        name="finish",
    )(*results)


def solution(mesh):
    devices = mesh.shape["seq"]
    zs = math.isqrt(devices // 2)
    ys = devices // (2 * zs)
    spec = P("seq", "head")
    return jax.shard_map(
        functools.partial(body, zs, ys),
        mesh=mesh,
        in_specs=(spec, spec, spec, spec, P("head", None)),
        out_specs=(spec, spec, spec, spec, P("head", None)),
        check_vma=False,
    )
```

```python
import functools
import math

import jax
import jax.numpy as jnp
from jax import lax
from jax.experimental import pallas as pl
from jax.experimental.pallas import tpu as pltpu
from jax.sharding import PartitionSpec as P

HEAD_DIM = 128
BLOCK = 128
HALF = BLOCK // 2
ROWS = 256
FEAT = 256
HEADS_HERE = FEAT // HEAD_DIM
NEAR = 3 * BLOCK
OWN_KEYS = NEAR + 3 * HALF
UPPER = 9 * HALF
PART = 3 * 32 + 6 * 16
PIECES = 4
NEG = -1e30
SCALE = 1.0 / math.sqrt(HEAD_DIM)
EXP2_SCALE = SCALE * math.log2(math.e)
MESH = pl.DeviceIdType.MESH
F32 = jnp.float32
BF16 = jnp.bfloat16


def dot(a, b):
    return lax.dot_general(a, b, (((1,), (0,)), ((), ())), preferred_element_type=F32)


def dot_nt(a, b):
    return lax.dot_general(a, b, (((1,), (1,)), ((), ())), preferred_element_type=F32)


def dot_tn(a, b):
    return lax.dot_general(a, b, (((0,), (0,)), ((), ())), preferred_element_type=F32)


def pair_average(rows):
    row = lax.broadcasted_iota(jnp.int32, (rows // 2, rows), 0)
    column = lax.broadcasted_iota(jnp.int32, (rows // 2, rows), 1)
    return jnp.where((column >= 2 * row) & (column < 2 * row + 2), 0.5, 0.0).astype(BF16)


def averages():
    parts = []
    for level in range(1, 5):
        count = ROWS >> level
        token = lax.broadcasted_iota(jnp.int32, (count, ROWS), 1)
        first = lax.broadcasted_iota(jnp.int32, (count, ROWS), 0) * (1 << level)
        inside = (token >= first) & (token < first + (1 << level))
        parts.append(jnp.where(inside, 0.5**level, 0.0).astype(BF16))
    return jnp.concatenate(parts, axis=0)


def spread_matrix():
    parts = []
    for level in range(1, 5):
        count = ROWS >> level
        token = lax.broadcasted_iota(jnp.int32, (ROWS, count), 0)
        first = lax.broadcasted_iota(jnp.int32, (ROWS, count), 1) * (1 << level)
        inside = (token >= first) & (token < first + (1 << level))
        parts.append(jnp.where(inside, 0.5**level, 0.0).astype(BF16))
    return parts


def kernel(
    devices, heads, zs, ys,
    q_in, k_in, v_in, go_in, w_in,
    proj_out, dq_out, dk_out, dv_out, pg_out,
    proj_ref, dq_ref, dk_ref, dv_ref, pg_ref, q_ref, w_ref, ext, lv1, own, up, gfull,
    edge, e_near, g1, near_out, gu, from_sib, gsum, from_mate, got_near, got2, got3, got4,
    part, got_part, s_own, s_up, pg32, pg16, got_half, mine, got_major, lines, final,
    in_sem, out_sem, row_send, row_recv, grad_send, grad_recv, x_send, x_recv, red_send, red_recv, last_recv, sib_recv,
):
    d = lax.axis_index("seq")
    h = lax.axis_index("head")
    core = lax.rem(d, 2)
    y = lax.rem(d // 2, ys)
    z = d // (2 * ys)
    chip = d // 2
    quad = d // 4
    side = lax.rem(chip, 2)

    def at(target):
        return (lax.rem(target + 2 * devices, devices), h)

    def send(src, dst, send_sem, recv_sem, target):
        copy = pltpu.make_async_remote_copy(
            src_ref=src, dst_ref=dst, send_sem=send_sem, recv_sem=recv_sem,
            device_id=target, device_id_type=MESH,
        )
        copy.start()

    def arrived(ref, sem):
        pltpu.make_async_copy(ref, ref, sem).wait()

    def write(src, dst):
        pltpu.make_async_copy(src, dst, out_sem).start()

    def rows_of(ref, first, count):
        return ref.at[pl.ds(pl.multiple_of(first, 16), count)]

    def far(index, total):
        wide = 3 - 6 * lax.rem(index, 2)
        return [lax.rem(index + o + total, total) for o in (2, -2, wide)]

    sibling = (d + 1 - 2 * core, h)
    mate = (4 * quad + 2 * (1 - side) + core, h)
    left, right = at(d - 1), at(d + 1)
    two = [at(d + 2), at(d - 2)]
    three = [(2 * t + core, h) for t in far(chip, devices // 2)]
    four = [(4 * t + 2 * (1 - side) + core, h) for t in far(quad, devices // 4)]
    across = [(d, lax.rem(h + r, heads)) for r in range(1, heads)]

    def z_peer(r):
        return lax.rem(z + r, zs) * (2 * ys) + 2 * y + core

    def y_peer(r):
        return z * (2 * ys) + 2 * lax.rem(y + r, ys) + core

    swap = core == 1
    major, minor = jnp.where(swap, y, z), jnp.where(swap, z, y)
    firsts = [(jnp.where(swap, y_peer(r), z_peer(r)), h) for r in range(1, zs)]
    seconds = [(jnp.where(swap, z_peer(r), y_peer(r)), h) for r in range(1, ys)]
    far_first = sorted(range(1, zs), key=lambda r: -min(r, zs - r))

    own_rows = ext.at[BLOCK : BLOCK + ROWS]
    loads = [
        (k_in, own_rows.at[:, :FEAT]), (v_in, own_rows.at[:, FEAT:]),
        (go_in, gfull.at[h]), (q_in, q_ref), (w_in, w_ref),
    ]
    loads = [pltpu.make_async_copy(src, dst, in_sem.at[i]) for i, (src, dst) in enumerate(loads)]
    for load in loads:
        load.start()

    barrier = pltpu.get_barrier_semaphore()
    rings = [peer for r in far_first for peer in (firsts[r - 1], seconds[r - 1])]
    everyone = [*rings[:2], *four, *three, *rings[2:6], *two, left, right, mate, *across, *rings[6:]]
    for target in everyone:
        pl.semaphore_signal(barrier, inc=1, device_id=target, device_id_type=MESH)

    loads[0].wait()
    loads[1].wait()

    own[...] = dot(averages(), ext[BLOCK : BLOCK + ROWS]).astype(BF16)
    for load in loads[2:]:
        load.wait()
    pl.semaphore_wait(barrier, len(everyone))

    mine_part = 3 * HALF + core * PART
    for slot in range(3):
        dst = rows_of(up, mine_part + 96 + side * 48 + slot * 16, 16)
        send(own.at[224:240], dst, row_send, row_recv.at[4], four[slot])
    for slot in (2, 0, 1):
        dst = rows_of(up, mine_part + slot * 32, 32)
        send(own.at[192:224], dst, row_send, row_recv.at[3], three[slot])
    for slot in range(2):
        send(own.at[128:192], up.at[slot * HALF : (slot + 1) * HALF], row_send, row_recv.at[2], two[slot])
    send(ext.at[BLOCK : 2 * BLOCK], ext.at[3 * BLOCK :], row_send, row_recv.at[0], left)
    send(ext.at[2 * BLOCK : 3 * BLOCK], ext.at[:BLOCK], row_send, row_recv.at[0], right)
    send(own.at[HALF : 2 * HALF], lv1.at[2 * HALF : 3 * HALF], row_send, row_recv.at[1], left)
    send(own.at[:HALF], lv1.at[HALF : 2 * HALF], row_send, row_recv.at[1], right)
    for target in across:
        send(gfull.at[h], gfull.at[h], x_send, x_recv.at[0], target)

    taken = rows_of(up, mine_part + 96 + (1 - side) * 48, 48)
    arrived(taken, row_recv.at[4])
    send(taken, taken, row_send, row_recv.at[5], mate)
    send(taken, taken, row_send, row_recv.at[6], sibling)
    level3 = rows_of(up, mine_part, 96)
    arrived(level3, row_recv.at[3])
    send(level3, level3, row_send, row_recv.at[6], sibling)
    arrived(up.at[: 2 * HALF], row_recv.at[2])
    send(rows_of(up, core * HALF, HALF), up.at[2 * HALF : 3 * HALF], row_send, row_recv.at[6], sibling)
    handed = rows_of(up, mine_part + 96 + side * 48, 48)
    arrived(handed, row_recv.at[5])
    send(handed, handed, row_send, row_recv.at[6], sibling)

    def bias(valid):
        return jnp.where(valid, 0.0, NEG).astype(F32)

    left_bias, right_bias = bias(d >= 1), bias(d <= devices - 2)

    def far_bias(index, total):
        wide = index + 3 - 6 * lax.rem(index, 2)
        return [bias(index >= 2), bias(index + 2 < total), bias((wide >= 0) & (wide < total))]

    bias2, bias3, bias4 = far_bias(d, devices), far_bias(chip, devices // 2), far_bias(quad, devices // 4)
    up_bias = [(HALF, b) for b in bias2]
    for _ in range(2):
        up_bias += [(32, b) for b in bias3] + [(16, b) for b in bias4 + bias4]

    def head_cols(head):
        return slice(head * HEAD_DIM, (head + 1) * HEAD_DIM)

    def value_cols(head):
        return slice(FEAT + head * HEAD_DIM, FEAT + (head + 1) * HEAD_DIM)

    def block_keys(block, cols):
        near = ext[block * BLOCK : block * BLOCK + NEAR, cols]
        return jnp.concatenate([near, lv1[block * HALF : block * HALF + 3 * HALF, cols]], axis=0)

    def block_queries(block, head):
        return q_ref[block * BLOCK : (block + 1) * BLOCK, head_cols(head)]

    arrived(ext.at[: 2 * BLOCK], row_recv.at[0])
    lv1[:HALF] = dot(pair_average(BLOCK), ext[3 * BLOCK :]).astype(BF16)
    lv1[3 * HALF :] = dot(pair_average(BLOCK), ext[:BLOCK]).astype(BF16)
    arrived(lv1.at[: 2 * HALF], row_recv.at[1])
    own_peak = [[None] * 2 for _ in range(HEADS_HERE)]
    for head in range(HEADS_HERE):
        for block in range(2):
            scores = dot_nt(block_keys(block, head_cols(head)), block_queries(block, head))
            if block == 0:
                pieces = [
                    scores[:BLOCK] + left_bias,
                    scores[BLOCK:NEAR],
                    scores[NEAR : NEAR + HALF] + right_bias,
                    scores[NEAR + HALF : NEAR + 2 * HALF] + left_bias,
                    scores[NEAR + 2 * HALF :] + right_bias,
                ]
            else:
                pieces = [
                    scores[: 2 * BLOCK],
                    scores[2 * BLOCK : NEAR] + right_bias,
                    scores[NEAR : NEAR + HALF] + left_bias,
                    scores[NEAR + HALF : NEAR + 2 * HALF] + right_bias,
                    scores[NEAR + 2 * HALF :] + left_bias,
                ]
            scores = jnp.concatenate(pieces, axis=0)
            s_own[head, block] = scores
            own_peak[head][block] = scores.max(axis=0, keepdims=True)

    if heads > 1:
        arrived(gfull.at[0 : heads - 1], x_recv.at[0])
    grad_full = jnp.concatenate([gfull[r] for r in range(heads)], axis=1)
    grad = dot_nt(grad_full, w_ref[...]).astype(BF16)
    grad_t = dot_nt(w_ref[...], grad_full).astype(BF16)

    arrived(up.at[: HALF + PART], row_recv.at[6])
    att_t = []
    for head in range(HEADS_HERE):
        raw = dot_nt(up[:, head_cols(head)], q_ref[:, head_cols(head)])
        pieces, first = [], 0
        for count, piece_bias in up_bias:
            pieces.append(raw[first : first + count] + piece_bias)
            first += count
        raw = jnp.concatenate(pieces, axis=0)
        peak = jnp.maximum(jnp.concatenate(own_peak[head], axis=1), raw.max(axis=0, keepdims=True))
        lifted_up = jnp.exp2((raw - peak) * EXP2_SCALE)
        total = lifted_up.sum(axis=0, keepdims=True)
        own_total = []
        for block in range(2):
            block_peak = peak[:, block * BLOCK : (block + 1) * BLOCK]
            lifted = jnp.exp2((s_own[head, block] - block_peak) * EXP2_SCALE)
            s_own[head, block] = lifted
            own_total.append(lifted.sum(axis=0, keepdims=True))
        inv = 1.0 / (total + jnp.concatenate(own_total, axis=1))
        prob_up = lifted_up * inv
        s_up[head] = prob_up
        up_att = dot_tn(up[:, value_cols(head)], prob_up.astype(BF16))
        own_att = []
        for block in range(2):
            prob = s_own[head, block] * inv[:, block * BLOCK : (block + 1) * BLOCK]
            s_own[head, block] = prob
            own_att.append(dot_tn(block_keys(block, value_cols(head)), prob.astype(BF16)))
        att_t.append(up_att + jnp.concatenate(own_att, axis=1))
    att16_t = jnp.concatenate(att_t, axis=0).astype(BF16)

    for c in range(2):
        half = dot(att16_t[c * BLOCK : (c + 1) * BLOCK], grad_full)
        pg32[c] = half
        pg16[c] = half.astype(BF16)
    send(pg16.at[1 - core], got_half, red_send, red_recv.at[0], sibling)

    delta = []
    dq_t = []
    for head in range(HEADS_HERE):
        g_t = grad_t[head_cols(head)]
        delta.append((g_t.astype(F32) * att_t[head]).sum(axis=0, keepdims=True))
        prob = s_up[head]
        dprob = dot(up[:, value_cols(head)], g_t)
        dscore = (prob * (dprob - delta[head]) * SCALE).astype(BF16)
        dq_t.append(dot_tn(up[:, head_cols(head)], dscore))
        gu[:, head_cols(head)] = dot(dscore, q_ref[:, head_cols(head)]).astype(BF16)
        gu[:, value_cols(head)] = dot(prob.astype(BF16), grad[:, head_cols(head)]).astype(BF16)
    send(rows_of(gu, 3 * HALF + (1 - core) * PART, PART), from_sib.at[HALF:], grad_send, grad_recv.at[5], sibling)
    send(gu.at[2 * HALF : 3 * HALF], from_sib.at[:HALF], grad_send, grad_recv.at[5], sibling)

    arrived(got_half, red_recv.at[0])
    chunk, width = BLOCK // zs, mine.shape[3]
    for p in range(PIECES):
        cols = slice(p * width, (p + 1) * width)
        for i in range(zs):
            window = slice(i * chunk, (i + 1) * chunk)
            mine[p, i] = (pg32[core, window, cols] + got_half[window, cols].astype(F32)).astype(BF16)
        for r in far_first:
            src = mine.at[p, lax.rem(major + r, zs)]
            send(src, got_major.at[p, r - 1], red_send, red_recv.at[1 + p], firsts[r - 1])

    arrived(from_sib, grad_recv.at[5])
    gsum[2 * HALF :] = (gu[pl.ds(pl.multiple_of(mine_part, 16), PART)].astype(F32) + from_sib[HALF:].astype(F32)).astype(BF16)
    send(rows_of(gsum, 2 * HALF + 96 + side * 48, 48), from_mate, grad_send, grad_recv.at[6], mate)
    for slot in range(3):
        src = gsum.at[2 * HALF + slot * 32 : 2 * HALF + (slot + 1) * 32]
        send(src, got3.at[slot], grad_send, grad_recv.at[3], three[(1, 0, 2)[slot]])
    gsum[: 2 * HALF] = gu[: 2 * HALF]
    shared = pl.ds(pl.multiple_of(core * HALF, 16), HALF)
    gsum[shared] = (gu[shared].astype(F32) + from_sib[:HALF].astype(F32)).astype(BF16)
    for slot in range(2):
        src = gsum.at[slot * HALF : (slot + 1) * HALF]
        send(src, got2.at[slot], grad_send, grad_recv.at[2], two[1 - slot])

    for head in range(HEADS_HERE):
        own_dq = []
        for block in range(2):
            cols = slice(block * BLOCK, (block + 1) * BLOCK)
            prob = s_own[head, block]
            dprob = dot(block_keys(block, value_cols(head)), grad_t[head_cols(head), cols])
            dscore = (prob * (dprob - delta[head][:, cols]) * SCALE).astype(BF16)
            own_dq.append(dot_tn(block_keys(block, head_cols(head)), dscore))
            dkey = dot(dscore, block_queries(block, head))
            dval = dot(prob.astype(BF16), grad[cols, head_cols(head)])
            for grads, column in ((dkey, head_cols(head)), (dval, value_cols(head))):
                if block == 0:
                    edge[0, :, column] = grads[:BLOCK]
                    e_near[:, column] = grads[BLOCK:NEAR]
                    g1[: 3 * HALF, column] = grads[NEAR:]
                else:
                    e_near[:, column] = e_near[:, column] + grads[: 2 * BLOCK]
                    edge[1, :, column] = grads[2 * BLOCK : NEAR]
                    g1[HALF : 3 * HALF, column] = g1[HALF : 3 * HALF, column] + grads[NEAR : NEAR + 2 * HALF]
                    g1[3 * HALF :, column] = grads[NEAR + 2 * HALF :]
        dq_t[head] = dq_t[head] + jnp.concatenate(own_dq, axis=1)
    levels = spread_matrix()
    pairs = levels[0][:BLOCK, :HALF]
    near_out[0, :BLOCK] = (edge[0] + dot(pairs, g1[3 * HALF :].astype(BF16))).astype(BF16)
    near_out[0, BLOCK:] = g1[HALF : 2 * HALF].astype(BF16)
    near_out[1, :BLOCK] = (edge[1] + dot(pairs, g1[:HALF].astype(BF16))).astype(BF16)
    near_out[1, BLOCK:] = g1[2 * HALF : 3 * HALF].astype(BF16)
    dq_ref[...] = jnp.concatenate(dq_t, axis=0).T.astype(BF16)
    write(dq_ref, dq_out)

    partial = dot(att16_t.T, w_ref[...])
    for r in range(heads):
        part[r] = partial[:, r * FEAT : (r + 1) * FEAT].astype(BF16)
    for r, target in enumerate(across):
        send(part.at[target[1]], got_part.at[r], x_send, x_recv.at[1], target)

    for p in range(PIECES):
        arrived(got_major.at[p], red_recv.at[1 + p])
        total = mine[p, major].astype(F32)
        for r in range(zs - 1):
            total = total + got_major[p, r].astype(F32)
        lines[p, minor] = total.astype(BF16)
        for r in far_first:
            send(lines.at[p, minor], lines.at[p, minor], red_send, red_recv.at[1 + PIECES + p], seconds[r - 1])
    send(near_out.at[0], got_near.at[1], grad_send, grad_recv.at[0], left)
    send(near_out.at[1], got_near.at[0], grad_send, grad_recv.at[0], right)
    arrived(from_mate, grad_recv.at[6])
    kept = pl.ds(pl.multiple_of(2 * HALF + 96 + (1 - side) * 48, 16), 48)
    gsum[kept] = (gsum[kept].astype(F32) + from_mate[...].astype(F32)).astype(BF16)
    for slot in range(3):
        src = rows_of(gsum, 2 * HALF + 96 + (1 - side) * 48 + slot * 16, 16)
        send(src, got4.at[slot], grad_send, grad_recv.at[4], four[(1, 0, 2)[slot]])

    def store_piece(half, p, i):
        rows = pl.ds(pl.multiple_of(half * BLOCK + i * chunk, chunk), chunk)
        cols = slice(p * width, (p + 1) * width)
        pg_ref[rows, cols] = final[half, p, i].astype(F32)
        write(pg_ref.at[rows, cols], pg_out.at[rows, cols])

    line = final.at[core, 0, major]
    for p in range(PIECES):
        arrived(lines.at[p, : ys - 1], red_recv.at[1 + PIECES + p])
        total = lines[p, 0].astype(F32)
        for i in range(1, ys):
            total = total + lines[p, i].astype(F32)
        piece = final.at[core, p, major]
        final[core, p, major] = total.astype(BF16)
        for r in far_first:
            send(piece, piece, red_send, last_recv.at[p, r - 1], firsts[r - 1])
        send(piece, piece, red_send, sib_recv.at[p, 0], sibling)
        store_piece(core, p, major)

    if heads > 1:
        arrived(got_part, x_recv.at[1])
    projected = part[h].astype(F32)
    for r in range(heads - 1):
        projected = projected + got_part[r].astype(F32)
    proj_ref[...] = projected.astype(BF16)
    write(proj_ref, proj_out)

    order = sorted(range(1, zs), key=lambda r: min(r, zs - r))

    def hand_on(distances):
        for r in distances:
            for p in range(PIECES):
                arrived(line, last_recv.at[p, r - 1])
                i = lax.rem(major + zs - r, zs)
                piece = final.at[core, p, i]
                send(piece, piece, red_send, sib_recv.at[p, r], sibling)
                store_piece(core, p, i)

    hand_on(order[:4])

    arrived(got4, grad_recv.at[4])
    arrived(got3, grad_recv.at[3])
    arrived(got2, grad_recv.at[2])
    arrived(got_near, grad_recv.at[0])
    rows_grad = e_near[...] + jnp.concatenate([got_near[0, :BLOCK], got_near[1, :BLOCK]], axis=0).astype(F32)
    rows_grad = rows_grad + dot(levels[0], jnp.concatenate([got_near[1, BLOCK:], got_near[0, BLOCK:]], axis=0))
    for level, got in ((1, got2), (2, got3), (3, got4)):
        total = got[0].astype(F32)
        for i in range(1, got.shape[0]):
            total = total + got[i].astype(F32)
        rows_grad = rows_grad + dot(levels[level], total.astype(BF16))
    dk_ref[...] = rows_grad[:, :FEAT].astype(BF16)
    dv_ref[...] = rows_grad[:, FEAT:].astype(BF16)
    write(dk_ref, dk_out)
    write(dv_ref, dv_out)

    hand_on(order[4:])
    for r in [0, *order]:
        for p in range(PIECES):
            arrived(line, sib_recv.at[p, r])
            store_piece(1 - core, p, lax.rem(minor + zs - r, zs))

    arrived(up.at[: 48 + 96 + 2 * HALF], row_send)
    arrived(up.at[: 2 * BLOCK + 2 * HALF], row_send)
    arrived(up.at[: 48 + HALF + PART], row_send)
    arrived(from_sib, grad_send)
    arrived(up.at[: 48 + 96 + 2 * HALF + 48], grad_send)
    arrived(near_out, grad_send)
    if heads > 1:
        arrived(gfull.at[0 : heads - 1], x_send)
        arrived(got_part, x_send)
    arrived(got_half, red_send)
    arrived(got_major, red_send)
    arrived(lines.at[:, : ys - 1], red_send)
    arrived(final.at[0, :, : zs - 1], red_send)
    arrived(final.at[0], red_send)
    for result in (proj_ref, dq_ref, dk_ref, dv_ref, pg_ref):
        arrived(result, out_sem)


def finish(*refs):
    results, outs, held, load_sems, store_sem = refs[:5], refs[5:10], refs[10:15], refs[15], refs[16]
    whole = pl.ds(0, ROWS)
    parts = [(4, pl.ds(i * ROWS // 4, ROWS // 4)) for i in range(4)] + [(i, whole) for i in range(4)]
    loads = [
        pltpu.make_async_copy(results[i].at[rows], held[i].at[rows], load_sems.at[n])
        for n, (i, rows) in enumerate(parts)
    ]
    for load in loads:
        load.start()
    for load, (i, rows) in zip(loads, parts):
        load.wait()
        pltpu.make_async_copy(held[i].at[rows], outs[i].at[rows], store_sem).start()
    for ref in held:
        pltpu.make_async_copy(ref, ref, store_sem).wait()


def body(zs, ys, queries, keys, values, grad_out, proj_weight):
    devices = lax.axis_size("seq")
    heads = lax.axis_size("head")
    model = proj_weight.shape[1]
    chunk = BLOCK // zs
    hbm = pl.BlockSpec(memory_space=pltpu.HBM)
    wide = 2 * FEAT
    scratch = [
        ((ROWS, FEAT), BF16),
        ((ROWS, FEAT), BF16),
        ((ROWS, FEAT), BF16),
        ((ROWS, FEAT), BF16),
        ((FEAT, model), F32),
        ((ROWS, FEAT), BF16),
        ((FEAT, model), BF16),
        ((4 * BLOCK, wide), BF16),
        ((4 * HALF, wide), BF16),
        ((240, wide), BF16),
        ((UPPER, wide), BF16),
        ((heads, ROWS, FEAT), BF16),
        ((2, BLOCK, wide), F32),
        ((ROWS, wide), F32),
        ((4 * HALF, wide), F32),
        ((2, BLOCK + HALF, wide), BF16),
        ((UPPER, wide), BF16),
        ((HALF + PART, wide), BF16),
        ((2 * HALF + PART, wide), BF16),
        ((48, wide), BF16),
        ((2, BLOCK + HALF, wide), BF16),
        ((2, HALF, wide), BF16),
        ((3, HALF // 2, wide), BF16),
        ((3, HALF // 4, wide), BF16),
        ((heads, ROWS, FEAT), BF16),
        ((max(heads - 1, 1), ROWS, FEAT), BF16),
        ((HEADS_HERE, 2, OWN_KEYS, BLOCK), F32),
        ((HEADS_HERE, UPPER, ROWS), F32),
        ((2, BLOCK, model), F32),
        ((2, BLOCK, model), BF16),
        ((BLOCK, model), BF16),
        ((PIECES, zs, chunk, model // PIECES), BF16),
        ((PIECES, zs - 1, chunk, model // PIECES), BF16),
        ((PIECES, ys, chunk, model // PIECES), BF16),
        ((2, PIECES, zs, chunk, model // PIECES), BF16),
    ]
    like = jax.ShapeDtypeStruct
    dma = pltpu.SemaphoreType.DMA
    small = like((ROWS, FEAT), BF16)
    results = pl.pallas_call(
        functools.partial(kernel, devices, heads, zs, ys),
        out_shape=(small, small, small, small, like((FEAT, model), F32)),
        in_specs=[hbm] * 5,
        out_specs=[hbm] * 5,
        scratch_shapes=[pltpu.VMEM(shape, kind) for shape, kind in scratch]
        + [dma((5,)), dma, dma, dma((7,)), dma, dma((7,)), dma, dma((2,)), dma, dma((1 + 2 * PIECES,)), dma((PIECES, zs - 1)), dma((PIECES, zs))],
        compiler_params=pltpu.CompilerParams(
            collective_id=0, has_side_effects=True, vmem_limit_bytes=63 * 1024 * 1024
        ),
        name="attention",
    )(queries, keys, values, grad_out, proj_weight)
    return pl.pallas_call(
        finish,
        out_shape=(small, small, small, small, like((FEAT, model), F32)),
        in_specs=[hbm] * 5,
        out_specs=[hbm] * 5,
        scratch_shapes=[pltpu.VMEM((ROWS, FEAT), BF16)] * 4 + [pltpu.VMEM((FEAT, model), F32), dma((8,)), dma],
        name="finish",
    )(*results)


def solution(mesh):
    devices = mesh.shape["seq"]
    zs = math.isqrt(devices // 2)
    ys = devices // (2 * zs)
    spec = P("seq", "head")
    return jax.shard_map(
        functools.partial(body, zs, ys),
        mesh=mesh,
        in_specs=(spec, spec, spec, spec, P("head", None)),
        out_specs=(spec, spec, spec, spec, P("head", None)),
        check_vma=False,
    )
```
